256 devices in a mesh: gx: 16 (over z, core), gy: 16 (over x, y).
Axes of the slice: x: 4, y: 4, z: 8, core: 2. Of those that a mesh axis runs over, the one named last changes fastest.
Arguments:
- residual_in: float32 [2, 256, 256, 128], P(None, 'gx', 'gy'), may hold values from -6 to 6
- wave_sq: float32 [256, 256, 128], P('gx', 'gy'), may hold values from 0.005 to 0.08
Outputs:
- correction: float32 [2, 256, 256, 128], P(None, 'gx', 'gy')
The draws below stay inside these ranges and needn't reach their ends.
All inputs are finite; a program needn't handle non-finite values.
Results may differ from the reference program's by a relative error of at most 0.00002.
Values sent between devices are 32-bit elements; how exact they have to be, the bound alone decides.
No kernel may reach another device: no remote copies, remote signals or barrier semaphores. Data moves between devices by JAX's collectives and lax.ppermute only.
A program may use at most 128 MiB of HBM per device.

```python
import math
import jax
import jax.numpy as jnp
from jax import lax

LEVELS = 5
COARSE_SWEEPS = 6
NX = 256
NY = 256
NZ = 128


def draw_residual_in(key, part):
    key = jax.random.fold_in(key, 11)
    rough = jax.random.normal(key, (2, NX, NY, NZ), jnp.float32)
    values = jnp.clip(rough, -6.0, 6.0)
    return values.astype(jnp.float32)


def levels(rng, extent, shards, least, high):
    def one(dim, shards_of):
        heights = jax.random.uniform(jax.random.fold_in(jax.random.fold_in(rng, 6), dim), (shards_of,), jnp.float32, least / len(shards), high / len(shards))
        return jnp.repeat(jnp.exp(heights), extent[dim] // shards_of).reshape((-1,) + (1,) * (len(extent) - dim - 1))

    gain = one(*shards[0])
    for cut in shards[1:]:
        gain = gain * one(*cut)
    return gain


def setup_inputs(seed: int = 0) -> dict:
    seeds = jax.random.split(jax.random.key(seed), 3)
    residual_in = draw_residual_in(jax.random.fold_in(seeds[2], 71), 0)
    wave_sq = jnp.clip(jnp.exp(math.log(0.08) - 2.7725887 * jax.random.uniform(seeds[1], (NX, NY, NZ), jnp.float32) ** levels(seeds[1], (NX, NY, NZ), ((0, 16), (1, 16)), -0.2, 0.2)), 0.005, 0.08)
    return dict(residual_in=residual_in, wave_sq=wave_sq)


OMEGA = 0.6
SHIFT = 0.5


def pad_depth(field):
    return jnp.pad(field, ((0, 0), (0, 0), (0, 0), (1, 1)))


def pad_plane(field):
    return jnp.pad(field, ((0, 0), (1, 1), (1, 1), (0, 0)))


def operator_apply(padded, wave_sq, lap_scale):
    full = pad_depth(padded)
    centre = full[:, 1:-1, 1:-1, 1:-1]
    summed = full[:, 2:, 1:-1, 1:-1] + full[:, :-2, 1:-1, 1:-1]
    summed = summed + full[:, 1:-1, 2:, 1:-1] + full[:, 1:-1, :-2, 1:-1]
    summed = summed + full[:, 1:-1, 1:-1, 2:] + full[:, 1:-1, 1:-1, :-2]
    laplace = lap_scale * (6.0 * centre - summed)
    real_part = laplace[0] - wave_sq * (centre[0] + SHIFT * centre[1])
    imag_part = laplace[1] - wave_sq * (centre[1] - SHIFT * centre[0])
    return jnp.stack([real_part, imag_part])


def inverse_diagonal(wave_sq, lap_scale):
    diag_real = 6.0 * lap_scale - wave_sq
    diag_imag = SHIFT * wave_sq
    modulus = diag_real * diag_real + diag_imag * diag_imag
    return diag_real / modulus, -diag_imag / modulus


def complex_mul(inv_real, inv_imag, values):
    return jnp.stack([inv_real * values[0] - inv_imag * values[1], inv_real * values[1] + inv_imag * values[0]])


def relax(field, padded, source, wave_sq, lap_scale, inv_real, inv_imag):
    misfit = source - operator_apply(padded, wave_sq, lap_scale)
    return field + OMEGA * complex_mul(inv_real, inv_imag, misfit)


def restrict_cells(values):
    dims_all = values.shape
    leading = dims_all[:-3]
    offset = len(leading)
    blocks = values.reshape(leading + (dims_all[-3] // 2, 2, dims_all[-2] // 2, 2, dims_all[-1] // 2, 2))
    return jnp.mean(blocks, axis=(offset + 1, offset + 3, offset + 5))


def prolong_axis(padded, axis_dim):
    count_c = padded.shape[axis_dim] - 2
    lower_part = lax.slice_in_dim(padded, 0, count_c, axis=axis_dim)
    middle = lax.slice_in_dim(padded, 1, count_c + 1, axis=axis_dim)
    upper_part = lax.slice_in_dim(padded, 2, count_c + 2, axis=axis_dim)
    even_cells = 0.25 * lower_part + 0.75 * middle
    odd_cells = 0.75 * middle + 0.25 * upper_part
    paired = jnp.stack([even_cells, odd_cells], axis=axis_dim + 1)
    new_shape = padded.shape[:axis_dim] + (2 * count_c,) + padded.shape[axis_dim + 1:]
    return paired.reshape(new_shape)


def prolong(padded_all):
    result = prolong_axis(padded_all, 1)
    result = prolong_axis(result, 2)
    return prolong_axis(result, 3)


def smooth_level(source, wave_sq, lap_scale, rim_of, coarse_of):
    inv_real, inv_imag = inverse_diagonal(wave_sq, lap_scale)
    field = OMEGA * complex_mul(inv_real, inv_imag, source)
    field = relax(field, rim_of(field), source, wave_sq, lap_scale, inv_real, inv_imag)
    misfit = source - operator_apply(rim_of(field), wave_sq, lap_scale)
    coarse_corr = coarse_of(restrict_cells(misfit), restrict_cells(wave_sq))
    field = field + prolong(pad_depth(coarse_corr))
    for sweep_no in range(2):
        field = relax(field, rim_of(field), source, wave_sq, lap_scale, inv_real, inv_imag)
    return field


def coarsest(source, wave_sq, lap_scale):
    inv_real, inv_imag = inverse_diagonal(wave_sq, lap_scale)
    field = OMEGA * complex_mul(inv_real, inv_imag, source)
    for sweep_no in range(COARSE_SWEEPS - 1):
        field = relax(field, pad_plane(field), source, wave_sq, lap_scale, inv_real, inv_imag)
    misfit = source - operator_apply(pad_plane(field), wave_sq, lap_scale)
    total_real = jnp.sum(misfit[0])
    total_imag = jnp.sum(misfit[1])
    factor = 1.0 / ((1.0 + SHIFT * SHIFT) * jnp.sum(wave_sq))
    shift_real = -(total_real - SHIFT * total_imag) * factor
    shift_imag = -(total_imag + SHIFT * total_real) * factor
    return field + jnp.stack([shift_real, shift_imag])[:, None, None, None]


def whole_cycle(source, wave_sq, grid_level):
    lap_scale = 0.25 ** grid_level
    if grid_level == LEVELS - 1:
        return coarsest(source, wave_sq, lap_scale)

    def coarse_of(coarse_src, coarse_wave):
        return pad_plane(whole_cycle(coarse_src, coarse_wave, grid_level + 1))

    return smooth_level(source, wave_sq, lap_scale, pad_plane, coarse_of)


def reference(residual_in, wave_sq):
    return whole_cycle(residual_in, wave_sq, 0)
```

```python
import functools

import jax
import jax.numpy as jnp
from jax import lax
from jax.experimental import pallas as pl
from jax.experimental.pallas import tpu as pltpu
from jax.sharding import PartitionSpec as P

OMEGA = 0.6
SHIFT = 0.5
F32 = jnp.float32


def lroll(v, shift):
    return pltpu.roll(v, shift % v.shape[1], 1)


def sroll(v, shift):
    return pltpu.roll(v, shift % v.shape[0], 0)


def lanes(rows):
    return lax.broadcasted_iota(jnp.int32, (rows, 128), 1)


def sublanes(rows):
    return lax.broadcasted_iota(jnp.int32, (rows, 128), 0)


def row_mask(rows, first, count):
    place = sublanes(rows) + first
    return jnp.where((place >= 0) & (place < count), F32(1), F32(0))


def scalar_mask(place, count):
    return jnp.where((place >= 0) & (place < count), F32(1), F32(0))


def z_pair(v, lane, step):
    low = jnp.where(lane >= step, lroll(v, step), 0.0)
    high = jnp.where(lane < 128 - step, lroll(v, -step), 0.0)
    return low, high


def z_sum(v, lane, step):
    low, high = z_pair(v, lane, step)
    return low + high


def y_sum(v):
    return sroll(v, 1) + sroll(v, -1)


def inverse(w, scale, keep):
    real = 6.0 * scale - w
    imag = SHIFT * w
    factor = (OMEGA * keep) / (real * real + imag * imag)
    return real * factor, -imag * factor


def misfit(f, w, v, nb, scale):
    (fr, fi), (vr, vi), (nr, ni) = f, v, nb
    mr = fr - scale * (6.0 * vr - nr) + w * (vr + SHIFT * vi)
    mi = fi - scale * (6.0 * vi - ni) + w * (vi - SHIFT * vr)
    return mr, mi


def cmul(g, m):
    return g[0] * m[0] - g[1] * m[1], g[0] * m[1] + g[1] * m[0]


def repeat(low, high, step, unroll=1):
    def run(i, carry):
        step(i)
        return carry

    lax.fori_loop(low, high, run, 0, unroll=unroll)


class Window:
    def __init__(self, src, gain, scale, pad, neighbours):
        self.src, self.gain, self.scale, self.pad = src, gain, scale, pad
        self.neighbours = neighbours

    def start(self, row, keep, out):
        w = self.src[2, row]
        g = inverse(w, self.scale, keep)
        self.gain[0, row], self.gain[1, row] = g
        u = cmul(g, (self.src[0, row], self.src[1, row]))
        out[0, row + self.pad], out[1, row + self.pad] = u

    def misfit(self, row, field):
        at = row + self.pad
        v = (field[0, at], field[1, at])
        nb = tuple(self.neighbours(field, c, at, v[c]) for c in range(2))
        f = (self.src[0, row], self.src[1, row])
        return v, misfit(f, self.src[2, row], v, nb, self.scale)

    def relaxed(self, row, field):
        v, m = self.misfit(row, field)
        d = cmul((self.gain[0, row], self.gain[1, row]), m)
        return v[0] + d[0], v[1] + d[1]

    def relax(self, row, field, out):
        at = row + self.pad
        out[0, at], out[1, at] = self.relaxed(row, field)


def near0(lane, ref, c, at, v):
    return ref[c, at - 1] + ref[c, at + 1] + y_sum(v) + z_sum(v, lane, 1)


def near1(lane, ref, c, at, v):
    low = lroll(ref[c, at - 1] + v, -1)
    high = lroll(v + ref[c, at + 1], 1)
    return jnp.where(lane % 2 == 0, low, high) + y_sum(v) + z_sum(v, lane, 2)


def near2_sparse(lane, ref, c, at, v):
    return ref[c, at - 1] + ref[c, at + 1] + y_sum(v) + z_sum(v, lane, 4)


def near2(lane, ref, c, at, v):
    slot = lane % 4
    low = jnp.where(slot == 0, lroll(ref[c, at - 1], -3), lroll(v, 1))
    high = jnp.where(slot == 3, lroll(ref[c, at + 1], 3), lroll(v, -1))
    return low + high + y_sum(v) + z_sum(v, lane, 4)


def level0(src, gain, first, ix, iy):
    lane = lanes(24)
    win = Window(src, gain, 1.0, 0, functools.partial(near0, lane))
    inside = row_mask(24, iy * 16 - 3, 256)
    repeat(0, 22, lambda x: win.start(x, inside * scalar_mask(ix * 16 - 3 + x, 256), first), 2)
    return win, inside


def level1(src, gain, first, ix, iy):
    lane = lanes(24)
    win = Window(src, gain, 0.25, 1, functools.partial(near1, lane))
    inside = row_mask(24, iy * 8 - 8, 128)
    repeat(0, 10, lambda q: win.start(q, inside * scalar_mask(ix * 4 - 3 + q, 64), first), 2)
    return win, inside


def down0_kernel(idx, src, out, gain, ua, ub, tmp):
    ix, iy = idx[0], idx[1]
    win, _ = level0(src, gain, ua, ix, iy)
    repeat(2, 20, lambda x: win.relax(x, ua, ub), 2)
    lane = lanes(8)
    even = lane % 2 == 0

    def halve(q):
        rows = []
        for half in range(2):
            x = 4 * q + 3 + 2 * half
            _, m0 = win.misfit(x, ub)
            _, m1 = win.misfit(x + 1, ub)
            parts = (m0[0] + m1[0], m0[1] + m1[1], src[2, x] + src[2, x + 1])
            got = []
            for c in range(3):
                tmp[c, 2 * q + half] = parts[c]
                t = tmp[c, 2 * q + half, pl.ds(3, 8, 2)] + tmp[c, 2 * q + half, pl.ds(4, 8, 2)]
                got.append(0.125 * (t + lroll(t, -1)))
            rows.append(got)
        for c in range(3):
            out[c, q] = jnp.where(even, rows[0][c], lroll(rows[1][c], 1))

    repeat(0, 4, halve)


def down1_kernel(idx, src, out, gain, ua, ub, tmp, src2, gain2, va, vb):
    ix, iy = idx[0], idx[1]
    for buf in (ua, ub):
        for c in range(2):
            buf[c, 0] = jnp.zeros((24, 128), F32)
            buf[c, 11] = jnp.zeros((24, 128), F32)
    win, _ = level1(src, gain, ua, ix, iy)
    repeat(0, 10, lambda q: win.relax(q, ua, ub), 2)
    lane = lanes(8)

    def halve(q):
        _, m = win.misfit(q, ub)
        parts = (m[0], m[1], src[2, q])
        for c in range(3):
            t = parts[c] + lroll(parts[c], -1)
            tmp[c, q] = t + lroll(t, -2)
            src2[c, q - 1] = 0.125 * (tmp[c, q, pl.ds(4, 8, 2)] + tmp[c, q, pl.ds(5, 8, 2)])

    repeat(1, 9, halve)
    for buf in (va, vb):
        for c in range(2):
            buf[c, 0] = jnp.zeros((8, 128), F32)
            buf[c, 9] = jnp.zeros((8, 128), F32)
    win2 = Window(src2, gain2, 0.0625, 1, functools.partial(near2_sparse, lane))
    inside = row_mask(8, iy * 4 - 2, 64)
    for q in range(8):
        win2.start(q, inside * scalar_mask(ix * 4 - 2 + q, 64), va)
    for q in range(1, 7):
        win2.relax(q, va, vb)
    res = [win2.misfit(q, vb)[1] for q in range(2, 6)]
    for c in range(3):
        packed = jnp.where(lane % 4 == 0, src2[c, 2], 0.0)
        for j in range(1, 4):
            packed = packed + lroll(jnp.where(lane % 4 == 0, src2[c, 2 + j], 0.0), j)
        out[pl.ds(4 * c, 4), :] = packed[2:6]

    def third(low, high):
        t = low + high
        t = t + sroll(t, -1)
        t = 0.125 * (t + lroll(t, -4))
        return jnp.where(lane % 8 == 0, t, 0.0)

    def merged(values):
        return values[2:3] + lroll(values[4:5], 1)

    field = jnp.zeros((8, 128), F32)
    wave = jnp.zeros((8, 128), F32)
    for xl in range(2):
        for part in range(2):
            field = field + lroll(third(res[2 * xl][part], res[2 * xl + 1][part]), 4 * part + 2 * xl)
        t = third(src2[2, 2 + 2 * xl], src2[2, 3 + 2 * xl])
        wave = wave + lroll(t, 2 * xl) + lroll(t, 4 + 2 * xl)
    out[pl.ds(12, 1), :] = merged(field)
    out[pl.ds(13, 1), :] = merged(wave)
    out[pl.ds(14, 2), :] = jnp.zeros((2, 128), F32)


def swap(v, real):
    return jnp.where(real, lroll(v, -4), lroll(v, 4))


def up_kernel(
    idx, src0, src1, got, out,
    f3, w3, ga3, gb3, ua3, ub3, f4, w4, ga4, gb4, ua4, ub4, e3,
    src2, gain2, ua2, ub2, wide2, gain1, ua1, ub1, wide1, wide0, gain0, ua0, ub0,
):
    ix, iy = idx[0], idx[1]
    flat = got.reshape(16 * 96, 128)
    lane = lanes(16)
    real = lane // 4 % 2 == 0
    sign = jnp.where(real, F32(SHIFT), F32(-SHIFT))
    xlow = lane // 2 % 2 == 0
    ylow = lane % 2 == 0
    row = sublanes(16)
    zero16 = jnp.zeros((16, 128), F32)

    def y_pair(v):
        return jnp.where(row >= 1, sroll(v, 1), 0.0), jnp.where(row < 15, sroll(v, -1), 0.0)

    def packed_gain(w, scale):
        gr, gi = inverse(w, scale, 1.0)
        return gr, jnp.where(real, -gi, gi)

    def near3(ref, at, v):
        down, up = y_pair(v)
        xs = jnp.where(xlow, lroll(ref[at - 1] + v, -2), lroll(v + ref[at + 1], 2))
        ys = jnp.where(ylow, lroll(v + down, -1), lroll(v + up, 1))
        return xs + ys + z_sum(v, lane, 8)

    def near4(ref, at, v):
        down, up = y_pair(v)
        return ref[at - 1] + ref[at + 1] + down + up + z_sum(v, lane, 16)

    def make(f, w, ga, gb, scale, near):
        def start(x, out_ref):
            ga[x], gb[x] = packed_gain(w[x], scale)
            out_ref[x + 1] = ga[x] * f[x] + gb[x] * swap(f[x], real)

        def miss(x, ref):
            v = ref[x + 1]
            m = f[x] - scale * (6.0 * v - near(ref, x + 1, v)) + w[x] * (v + sign * swap(v, real))
            return v, m

        def relax(x, ref, out_ref):
            v, m = miss(x, ref)
            out_ref[x + 1] = v + ga[x] * m + gb[x] * swap(m, real)

        return start, miss, relax

    for buf in (ua3, ub3, ua4, ub4):
        buf[0] = zero16
        buf[17] = zero16

    for x in range(16):
        f3[x] = flat[pl.ds(2 * x, 16, 96), :]
        w3[x] = flat[pl.ds(2 * x + 1, 16, 96), :]
    start3, miss3, relax3 = make(f3, w3, ga3, gb3, 1.0 / 64, near3)
    start4, miss4, relax4 = make(f4, w4, ga4, gb4, 1.0 / 256, near4)
    repeat(0, 16, lambda x: start3(x, ua3), 4)
    repeat(0, 16, lambda x: relax3(x, ua3, ub3), 4)

    def eighth(v):
        v = v + lroll(v, -1)
        v = v + lroll(v, -2)
        return 0.125 * (v + lroll(v, -8))

    def halve3(x):
        f4[x] = eighth(miss3(x, ub3)[1])
        w4[x] = eighth(w3[x])
        start4(x, ua4)

    repeat(0, 16, halve3, 4)
    now, other = ua4, ub4
    for _ in range(5):
        repeat(0, 16, lambda x: relax4(x, now, other), 4)
        now, other = other, now
    total_m = zero16
    total_w = zero16
    for x in range(16):
        total_m = total_m + miss4(x, now)[1]
        total_w = total_w + w4[x]
    sum_r = jnp.sum(jnp.where(lane % 16 == 0, total_m, 0.0))
    sum_i = jnp.sum(jnp.where(lane % 16 == 4, total_m, 0.0))
    sum_w = jnp.sum(jnp.where(lane % 16 == 0, total_w, 0.0))
    numer = jnp.where(real, sum_r - SHIFT * sum_i, sum_i + SHIFT * sum_r)
    const = -numer / (jnp.full((16, 128), (1.0 + SHIFT * SHIFT), F32) * sum_w)

    keep4 = (lane % 16 == 0) | (lane % 16 == 4)
    zlow = lane // 8 % 2 == 0

    def spread4(x):
        t = jnp.where(keep4, now[x + 1] + const, 0.0)
        t = t + lroll(t, 1)
        t = t + lroll(t, 2)
        t = t + lroll(t, 8)
        low, high = z_pair(t, lane, 16)
        t = 0.75 * t + 0.25 * jnp.where(zlow, low, high)
        down, up = y_pair(t)
        other[x + 1] = 0.75 * t + 0.25 * jnp.where(ylow, down, up)

    repeat(0, 16, spread4, 4)

    def correct3(x):
        side = jnp.where(xlow, other[x], other[x + 2])
        ub3[x + 1] = ub3[x + 1] + 0.75 * other[x + 1] + 0.25 * side

    repeat(0, 16, correct3, 4)
    repeat(0, 16, lambda x: relax3(x, ub3, ua3), 4)
    for at in (0, 1, 2, 19, 20, 21):
        e3[at] = jnp.zeros((32, 128), F32)
    for at in range(3, 19):
        e3[at, pl.ds(0, 8), :] = jnp.zeros((8, 128), F32)
        e3[at, pl.ds(24, 8), :] = jnp.zeros((8, 128), F32)

    def finish3(x):
        relax3(x, ua3, ub3)
        e3[x + 3, pl.ds(8, 16), :] = ub3[x + 1]

    repeat(0, 16, finish3, 4)

    lane8 = lanes(8)
    lane24 = lanes(24)
    zero24 = jnp.zeros((24, 128), F32)
    for b in range(5):
        for c in range(3):
            src2[c, b] = zero24
    for g in range(5):
        other_y = lax.rem(iy + 14 + g, 16)
        for b in range(5):
            for c in range(3):
                src2[c, b, pl.ds(4 * g, 4), :] = got[other_y, pl.ds(32 + 12 * b + 4 * c, 4), :]
    for buf in (ua2, ub2):
        for c in range(2):
            buf[c, 0] = zero24
            buf[c, 6] = zero24
    win2 = Window(src2, gain2, 0.0625, 1, functools.partial(near2, lane24))
    inside2 = row_mask(24, iy * 4 - 8, 64)
    keep2 = [inside2 * scalar_mask(ix - 2 + b, 16) for b in range(5)]
    for b in range(5):
        win2.start(b, keep2[b], ua2)
    for b in range(5):
        win2.relax(b, ua2, ub2)
    near = [e3[ix + bb, pl.ds(iy + 5, 8), :] for bb in range(7)]
    xl3 = lane8 // 2 % 2
    a_low = lane8 % 2 == 0
    b_low = lane8 // 4 % 2 == 0
    for c in range(2):
        sides = []
        for yl in range(2):
            pick = (lane8 // 4 % 2 == c) & (lane8 % 2 == yl)
            cells = []
            for v in near:
                t = jnp.where(pick, v, 0.0)
                t = t + lroll(t, 1 - 2 * yl)
                t = t + lroll(t, 4 - 8 * c)
                low, high = z_pair(t, lane8, 8)
                cells.append(0.75 * t + 0.25 * jnp.where(b_low, low, high))
            blocks = []
            for b in range(1, 6):
                low = lroll(jnp.where(a_low, cells[b - 1], cells[b]), -2)
                high = lroll(jnp.where(a_low, cells[b], cells[b + 1]), 2)
                blocks.append(0.75 * cells[b] + 0.25 * jnp.where(xl3 == 0, low, high))
            sides.append(blocks)
        for b in range(5):
            t0, t1 = sides[0][b], sides[1][b]
            wide2[c, b, pl.ds(0, 8, 4), :] = 0.75 * t0 + 0.25 * sroll(t1, 1)
            wide2[c, b, pl.ds(1, 8, 4), :] = 0.75 * t0 + 0.25 * t1
            wide2[c, b, pl.ds(2, 8, 4), :] = 0.75 * t1 + 0.25 * t0
            wide2[c, b, pl.ds(3, 8, 4), :] = 0.75 * t1 + 0.25 * sroll(t0, -1)
            fix = wide2[c, b, pl.ds(4, 24), :]
            ub2[c, b + 1] = ub2[c, b + 1] + jnp.where(keep2[b] > 0, fix, 0.0)
    for b in range(5):
        win2.relax(b, ub2, ua2)
    for b in range(1, 4):
        win2.relax(b, ua2, ub2)

    for buf in (ua1, ub1):
        for c in range(2):
            buf[c, 0] = zero24
            buf[c, 11] = zero24
    win1, inside1 = level1(src1, gain1, ua1, ix, iy)
    repeat(0, 10, lambda q: win1.relax(q, ua1, ub1), 2)
    slot4 = lane24 % 4
    for c in range(2):
        cells = []
        for at in range(12):
            b, xl = 1 + at // 4, at % 4
            t = jnp.where(slot4 == xl, ub2[c, b + 1], 0.0)
            t = lroll(t, -xl) if xl else t
            t = t + lroll(t, 1)
            t = t + lroll(t, 2)
            low, high = z_pair(t, lane24, 4)
            cells.append(0.75 * t + 0.25 * jnp.where(slot4 < 2, low, high))
        for q in range(10):
            side = jnp.where(lane24 % 2 == 0, cells[q], cells[q + 2])
            t = 0.75 * cells[q + 1] + 0.25 * side
            wide1[c, q, pl.ds(0, 24, 2), :] = 0.75 * t + 0.25 * sroll(t, 1)
            wide1[c, q, pl.ds(1, 24, 2), :] = 0.75 * t + 0.25 * sroll(t, -1)
            keep = inside1 * scalar_mask(ix * 4 - 3 + q, 64)
            fix = wide1[c, q, pl.ds(8, 24), :]
            ub1[c, q + 1] = ub1[c, q + 1] + jnp.where(keep > 0, fix, 0.0)
    repeat(0, 10, lambda q: win1.relax(q, ub1, ua1), 2)
    repeat(1, 9, lambda q: win1.relax(q, ua1, ub1), 2)

    win0, inside0 = level0(src0, gain0, ua0, ix, iy)
    repeat(1, 21, lambda x: win0.relax(x, ua0, ub0), 2)
    for c in range(2):
        for x in (0, 21):
            ub0[c, x] = zero24

    def widen(q):
        for c in range(2):
            t = ub1[c, q + 1]
            even = jnp.where(lane24 % 2 == 0, t, lroll(t, 1))
            odd = jnp.where(lane24 % 2 == 0, lroll(t, -1), t)
            for p, v in ((0, even), (1, odd)):
                low, high = z_pair(v, lane24, 2)
                v = 0.75 * v + 0.25 * jnp.where(lane24 % 2 == 0, low, high)
                wide0[c, 2 * q + p, pl.ds(0, 24, 2), :] = 0.75 * v + 0.25 * sroll(v, 1)
                wide0[c, 2 * q + p, pl.ds(1, 24, 2), :] = 0.75 * v + 0.25 * sroll(v, -1)

    repeat(2, 8, widen)

    def correct0(at):
        for c in range(2):
            low = wide0[c, at - 1, pl.ds(13, 24), :]
            mid = wide0[c, at, pl.ds(13, 24), :]
            high = wide0[c, at + 1, pl.ds(13, 24), :]
            for child, side in ((0, low), (1, high)):
                x = 2 * at - 9 + child
                keep = inside0 * scalar_mask(ix * 16 - 3 + x, 256)
                fix = 0.75 * mid + 0.25 * side
                ub0[c, x] = ub0[c, x] + jnp.where(keep > 0, fix, 0.0)

    repeat(5, 15, correct0)
    repeat(2, 20, lambda x: win0.relax(x, ub0, ua0), 2)

    def finish0(x):
        ur, ui = win0.relaxed(x + 3, ua0)
        ub0[0, x + 3], ub0[1, x + 3] = ur, ui
        out[0, x] = ub0[0, x + 3, pl.ds(3, 16), :]
        out[1, x] = ub0[1, x + 3, pl.ds(3, 16), :]

    repeat(0, 16, finish0, 2)


def call(kernel, name, out_shape, scratch, *args):
    vmem = pl.BlockSpec(memory_space=pltpu.VMEM)
    return pl.pallas_call(
        kernel,
        name=name,
        out_shape=jax.ShapeDtypeStruct(out_shape, F32),
        in_specs=[pl.BlockSpec(memory_space=pltpu.SMEM)] + [vmem] * (len(args) - 1),
        out_specs=vmem,
        scratch_shapes=[pltpu.VMEM(shape, F32) for shape in scratch],
        compiler_params=pltpu.CompilerParams(vmem_limit_bytes=40 * 1024 * 1024),
    )(*args)


def send(value, axis, step):
    count = lax.axis_size(axis)
    return lax.ppermute(value, axis, [(i, (i + step) % count) for i in range(count)])


def share(value, axis):
    count = lax.axis_size(axis)
    return lax.all_to_all(jnp.broadcast_to(value[None], (count,) + value.shape), axis, 0, 0)


def body(residual_in, wave_sq):
    ix = lax.axis_index("gx")
    iy = lax.axis_index("gy")
    idx = jnp.stack([ix, iy]).astype(jnp.int32)

    own = jnp.concatenate([residual_in, wave_sq[None]], axis=0)
    low = send(own[:, 13:], "gx", 1)
    high = send(own[:, :3], "gx", -1)
    strip = jnp.concatenate([low, own, high], axis=1)
    low = send(strip[:, :, 13:].transpose(0, 2, 1, 3).reshape(9, 22, 128), "gy", 1)
    high = send(strip[:, :, :3].transpose(0, 2, 1, 3).reshape(9, 22, 128), "gy", -1)
    low = low.reshape(3, 3, 22, 128).transpose(0, 2, 1, 3)
    high = high.reshape(3, 3, 22, 128).transpose(0, 2, 1, 3)
    src0 = jnp.concatenate([low, strip, high, jnp.zeros((3, 22, 2, 128), F32)], axis=2)

    n0 = (2, 22, 24, 128)
    n1 = (2, 12, 24, 128)
    own1 = call(
        down0_kernel, "down0", (3, 4, 8, 128), [n0, n0, n0, (3, 8, 24, 128)], idx, src0
    )
    low = send(own1[:, 1:], "gx", 1)
    high = send(own1[:, :3], "gx", -1)
    strip = jnp.concatenate([low, own1, high], axis=1)
    low = send(strip, "gy", 1)
    high = send(strip, "gy", -1)
    src1 = jnp.concatenate([low, strip, high], axis=2)

    part = call(
        down1_kernel,
        "down1",
        (16, 128),
        [(2, 10, 24, 128), n1, n1, (3, 10, 24, 128)]
        + [(3, 8, 8, 128), (2, 8, 8, 128), (2, 10, 8, 128), (2, 10, 8, 128)],
        idx,
        src1,
    )
    line = share(part, "gx")
    ring = jnp.concatenate([line[14:], line, line[:2]], axis=0)
    blocks = lax.dynamic_slice(ring, (ix, 0, 0), (5, 12, 128))
    mine = jnp.concatenate(
        [line[:, 12:14].reshape(32, 128), blocks.reshape(60, 128), jnp.zeros((4, 128), F32)], axis=0
    )
    got = share(mine, "gy")

    one = (16, 16, 128)
    two = (18, 16, 128)
    return call(
        up_kernel,
        "up",
        (2, 16, 16, 128),
        [one, one, one, one, two, two, one, one, one, one, two, two, (22, 32, 128)]
        + [(3, 5, 24, 128), (2, 5, 24, 128), (2, 7, 24, 128), (2, 7, 24, 128), (2, 5, 32, 128)]
        + [(2, 10, 24, 128), n1, n1, (2, 10, 48, 128), (2, 16, 48, 128), n0, n0, n0],
        idx,
        src0,
        src1,
        got,
    )


def solution(mesh):
    placed = (P(None, "gx", "gy", None), P("gx", "gy", None))
    return jax.shard_map(
        body, mesh=mesh, in_specs=placed, out_specs=P(None, "gx", "gy", None), check_vma=False
    )
```

```python
import functools

import jax
import jax.numpy as jnp
from jax import lax
from jax.experimental import pallas as pl
from jax.experimental.pallas import tpu as pltpu
from jax.sharding import PartitionSpec as P

OMEGA = 0.6
SHIFT = 0.5
F32 = jnp.float32


def lroll(v, shift):
    return pltpu.roll(v, shift % v.shape[1], 1)


def sroll(v, shift):
    return pltpu.roll(v, shift % v.shape[0], 0)


def lanes(rows):
    return lax.broadcasted_iota(jnp.int32, (rows, 128), 1)


def sublanes(rows):
    return lax.broadcasted_iota(jnp.int32, (rows, 128), 0)


def row_mask(rows, first, count):
    place = sublanes(rows) + first
    return jnp.where((place >= 0) & (place < count), F32(1), F32(0))


def scalar_mask(place, count):
    return jnp.where((place >= 0) & (place < count), F32(1), F32(0))


def z_pair(v, lane, step):
    low = jnp.where(lane >= step, lroll(v, step), 0.0)
    high = jnp.where(lane < 128 - step, lroll(v, -step), 0.0)
    return low, high


def z_sum(v, lane, step):
    low, high = z_pair(v, lane, step)
    return low + high


def y_sum(v):
    return sroll(v, 1) + sroll(v, -1)


def inverse(w, scale, keep):
    real = 6.0 * scale - w
    imag = SHIFT * w
    factor = (OMEGA * keep) / (real * real + imag * imag)
    return real * factor, -imag * factor


def misfit(f, w, v, nb, scale):
    (fr, fi), (vr, vi), (nr, ni) = f, v, nb
    mr = fr - scale * (6.0 * vr - nr) + w * (vr + SHIFT * vi)
    mi = fi - scale * (6.0 * vi - ni) + w * (vi - SHIFT * vr)
    return mr, mi


def cmul(g, m):
    return g[0] * m[0] - g[1] * m[1], g[0] * m[1] + g[1] * m[0]


def repeat(low, high, step, unroll=1):
    def run(i, carry):
        step(i)
        return carry

    lax.fori_loop(low, high, run, 0, unroll=unroll)


class Window:
    def __init__(self, src, gain, scale, pad, neighbours):
        self.src, self.gain, self.scale, self.pad = src, gain, scale, pad
        self.neighbours = neighbours

    def start(self, row, keep, out):
        w = self.src[2, row]
        g = inverse(w, self.scale, keep)
        self.gain[0, row], self.gain[1, row] = g
        u = cmul(g, (self.src[0, row], self.src[1, row]))
        out[0, row + self.pad], out[1, row + self.pad] = u

    def misfit(self, row, field):
        at = row + self.pad
        v = (field[0, at], field[1, at])
        nb = tuple(self.neighbours(field, c, at, v[c]) for c in range(2))
        f = (self.src[0, row], self.src[1, row])
        return v, misfit(f, self.src[2, row], v, nb, self.scale)

    def relaxed(self, row, field):
        v, m = self.misfit(row, field)
        d = cmul((self.gain[0, row], self.gain[1, row]), m)
        return v[0] + d[0], v[1] + d[1]

    def relax(self, row, field, out):
        at = row + self.pad
        out[0, at], out[1, at] = self.relaxed(row, field)


def near0(lane, ref, c, at, v):
    return ref[c, at - 1] + ref[c, at + 1] + y_sum(v) + z_sum(v, lane, 1)


def near1(lane, ref, c, at, v):
    low = lroll(ref[c, at - 1] + v, -1)
    high = lroll(v + ref[c, at + 1], 1)
    return jnp.where(lane % 2 == 0, low, high) + y_sum(v) + z_sum(v, lane, 2)


def near2_sparse(lane, ref, c, at, v):
    return ref[c, at - 1] + ref[c, at + 1] + y_sum(v) + z_sum(v, lane, 4)


def near2(lane, ref, c, at, v):
    slot = lane % 4
    low = jnp.where(slot == 0, lroll(ref[c, at - 1], -3), lroll(v, 1))
    high = jnp.where(slot == 3, lroll(ref[c, at + 1], 3), lroll(v, -1))
    return low + high + y_sum(v) + z_sum(v, lane, 4)


def level0(src, gain, first, ix, iy):
    lane = lanes(24)
    win = Window(src, gain, 1.0, 0, functools.partial(near0, lane))
    inside = row_mask(24, iy * 16 - 3, 256)
    repeat(0, 22, lambda x: win.start(x, inside * scalar_mask(ix * 16 - 3 + x, 256), first), 2)
    return win, inside


def level1(src, gain, first, ix, iy):
    lane = lanes(24)
    win = Window(src, gain, 0.25, 1, functools.partial(near1, lane))
    inside = row_mask(24, iy * 8 - 8, 128)
    repeat(0, 10, lambda q: win.start(q, inside * scalar_mask(ix * 4 - 3 + q, 64), first), 2)
    return win, inside


def down0_kernel(idx, src, out, gain, ub, ua, tmp):
    ix, iy = idx[0], idx[1]
    win, _ = level0(src, gain, ua, ix, iy)
    repeat(1, 21, lambda x: win.relax(x, ua, ub), 4)
    for c in range(2):
        for x in (0, 21):
            ub[c, x] = jnp.zeros((24, 128), F32)
    lane = lanes(8)
    even = lane % 2 == 0

    def halve(q):
        rows = []
        for half in range(2):
            x = 4 * q + 3 + 2 * half
            _, m0 = win.misfit(x, ub)
            _, m1 = win.misfit(x + 1, ub)
            parts = (m0[0] + m1[0], m0[1] + m1[1], src[2, x] + src[2, x + 1])
            got = []
            for c in range(3):
                tmp[c, 2 * q + half] = parts[c]
                t = tmp[c, 2 * q + half, pl.ds(3, 8, 2)] + tmp[c, 2 * q + half, pl.ds(4, 8, 2)]
                got.append(0.125 * (t + lroll(t, -1)))
            rows.append(got)
        for c in range(3):
            out[c, q] = jnp.where(even, rows[0][c], lroll(rows[1][c], 1))

    repeat(0, 4, halve)


def down1_kernel(idx, src, out, gain, ub, ua, tmp, src2, gain2, va, vb):
    ix, iy = idx[0], idx[1]
    for buf in (ua, ub):
        for c in range(2):
            buf[c, 0] = jnp.zeros((24, 128), F32)
            buf[c, 11] = jnp.zeros((24, 128), F32)
    win, _ = level1(src, gain, ua, ix, iy)
    repeat(0, 10, lambda q: win.relax(q, ua, ub), 5)
    lane = lanes(8)

    def halve(q):
        _, m = win.misfit(q, ub)
        parts = (m[0], m[1], src[2, q])
        for c in range(3):
            t = parts[c] + lroll(parts[c], -1)
            tmp[c, q] = t + lroll(t, -2)
            src2[c, q - 1] = 0.125 * (tmp[c, q, pl.ds(4, 8, 2)] + tmp[c, q, pl.ds(5, 8, 2)])

    repeat(1, 9, halve)
    for buf in (va, vb):
        for c in range(2):
            buf[c, 0] = jnp.zeros((8, 128), F32)
            buf[c, 9] = jnp.zeros((8, 128), F32)
    win2 = Window(src2, gain2, 0.0625, 1, functools.partial(near2_sparse, lane))
    inside = row_mask(8, iy * 4 - 2, 64)
    for q in range(8):
        win2.start(q, inside * scalar_mask(ix * 4 - 2 + q, 64), va)
    for q in range(1, 7):
        win2.relax(q, va, vb)
    res = [win2.misfit(q, vb)[1] for q in range(2, 6)]
    for c in range(3):
        packed = jnp.where(lane % 4 == 0, src2[c, 2], 0.0)
        for j in range(1, 4):
            packed = packed + lroll(jnp.where(lane % 4 == 0, src2[c, 2 + j], 0.0), j)
        out[pl.ds(4 * c, 4), :] = packed[2:6]

    def third(low, high):
        t = low + high
        t = t + sroll(t, -1)
        t = 0.125 * (t + lroll(t, -4))
        return jnp.where(lane % 8 == 0, t, 0.0)

    def merged(values):
        return values[2:3] + lroll(values[4:5], 1)

    field = jnp.zeros((8, 128), F32)
    wave = jnp.zeros((8, 128), F32)
    for xl in range(2):
        for part in range(2):
            field = field + lroll(third(res[2 * xl][part], res[2 * xl + 1][part]), 4 * part + 2 * xl)
        t = third(src2[2, 2 + 2 * xl], src2[2, 3 + 2 * xl])
        wave = wave + lroll(t, 2 * xl) + lroll(t, 4 + 2 * xl)
    out[pl.ds(12, 1), :] = merged(field)
    out[pl.ds(13, 1), :] = merged(wave)
    out[pl.ds(14, 2), :] = jnp.zeros((2, 128), F32)


def swap(v, real):
    return jnp.where(real, lroll(v, -4), lroll(v, 4))


def up_kernel(
    idx, src0, gain0, ub0, src1, gain1, ub1, got, out,
    f3, w3, ga3, gb3, u3, f4, w4, s4, e3, src2, gain2, u2, wide2, cell1, u1, wide1, wide0, ua0, ub0s,
):
    ix, iy = idx[0], idx[1]
    flat = got.reshape(16 * 96, 128)
    lane = lanes(16)
    real = lane // 4 % 2 == 0
    sign = jnp.where(real, F32(SHIFT), F32(-SHIFT))
    xlow = lane // 2 % 2 == 0
    ylow = lane % 2 == 0
    zlow = lane // 8 % 2 == 0
    slot = lane % 4
    row = sublanes(16)
    zero16 = jnp.zeros((16, 128), F32)

    def y_pair(v):
        return jnp.where(row >= 1, sroll(v, 1), 0.0), jnp.where(row < 15, sroll(v, -1), 0.0)

    def packed_gain(w, scale):
        gr, gi = inverse(w, scale, 1.0)
        return gr, jnp.where(real, -gi, gi)

    def packed_misfit(f, w, v, nb, scale):
        return f - scale * (6.0 * v - nb) + w * (v + sign * swap(v, real))

    for at in (0, 1, 2, 19, 20, 21):
        for ref in (f3, w3, ga3, gb3):
            ref[at] = zero16
        for p in range(2):
            u3[p, at] = zero16
        e3[at] = jnp.zeros((32, 128), F32)
    for at in range(3, 19):
        e3[at, pl.ds(0, 8), :] = jnp.zeros((8, 128), F32)
        e3[at, pl.ds(24, 8), :] = jnp.zeros((8, 128), F32)

    def start3(x):
        at = x + 3
        f3[at] = flat[pl.ds(2 * x, 16, 96), :]
        w = flat[pl.ds(2 * x + 1, 16, 96), :]
        w3[at] = w
        ga, gb = packed_gain(w, 1.0 / 64)
        ga3[at], gb3[at] = ga, gb
        u3[0, at] = ga * f3[at] + gb * swap(f3[at], real)

    def miss3(p, at):
        v = u3[p, at]
        down, up = y_pair(v)
        xs = jnp.where(xlow, lroll(u3[p, at - 1] + v, -2), lroll(v + u3[p, at + 1], 2))
        ys = jnp.where(ylow, lroll(v + down, -1), lroll(v + up, 1))
        return v, packed_misfit(f3[at], w3[at], v, xs + ys + z_sum(v, lane, 8), 1.0 / 64)

    def relax3(p, at):
        v, m = miss3(p, at)
        u3[1 - p, at] = v + ga3[at] * m + gb3[at] * swap(m, real)

    repeat(0, 16, start3, 8)
    repeat(3, 19, lambda at: relax3(0, at), 8)

    first = (slot == 0) & zlow

    def eighth(v):
        v = v + lroll(v, -1)
        v = v + lroll(v, -2)
        return jnp.where(first, 0.125 * (v + lroll(v, -8)), 0.0)

    def halve3(r):
        f, w = zero16, zero16
        for k in range(4):
            at = 4 * k + r + 3
            fk, wk = eighth(miss3(1, at)[1]), eighth(w3[at])
            f = f + (lroll(fk, k) if k else fk)
            w = w + (lroll(wk, k) if k else wk)
        f4[r], w4[r] = f, w

    repeat(0, 4, halve3, 2)
    fs = [f4[r] for r in range(4)]
    ws = [w4[r] for r in range(4)]
    gs = [packed_gain(w, 1.0 / 256) for w in ws]

    def miss4(us):
        low = jnp.where(slot >= 1, lroll(us[3], 1), 0.0)
        high = jnp.where(slot < 3, lroll(us[0], -1), 0.0)
        wide = [low, *us, high]
        ms = []
        for r in range(4):
            down, up = y_pair(us[r])
            nb = wide[r] + wide[r + 2] + down + up + z_sum(us[r], lane, 16)
            ms.append(packed_misfit(fs[r], ws[r], us[r], nb, 1.0 / 256))
        return ms

    def relax4(_, us):
        ms = miss4(us)
        return tuple(u + g[0] * m + g[1] * swap(m, real) for u, g, m in zip(us, gs, ms))

    us = tuple(g[0] * f + g[1] * swap(f, real) for g, f in zip(gs, fs))
    us = lax.fori_loop(0, 5, relax4, us)
    ms = miss4(us)
    total_m = ms[0] + ms[1] + ms[2] + ms[3]
    total_w = ws[0] + ws[1] + ws[2] + ws[3]
    sum_r = jnp.sum(jnp.where(zlow & real, total_m, 0.0))
    sum_i = jnp.sum(jnp.where(zlow & ~real, total_m, 0.0))
    sum_w = jnp.sum(jnp.where(zlow & real, total_w, 0.0))
    numer = jnp.where(real, sum_r - SHIFT * sum_i, sum_i + SHIFT * sum_r)
    const = -numer / (jnp.full((16, 128), (1.0 + SHIFT * SHIFT), F32) * sum_w)
    for r in range(4):
        s4[r] = jnp.where(zlow, us[r] + const, 0.0)

    def spread4(j):
        x = ix - 4 + j
        inside = (x >= 0) & (x < 16)
        x = jnp.clip(x, 0, 15)
        k = x // 4
        t = jnp.where((slot == k) & inside, s4[x - 4 * k], 0.0)
        t = pltpu.roll(t, lax.rem(128 - k, 128), 1)
        t = t + lroll(t, 1)
        t = t + lroll(t, 2)
        t = t + lroll(t, 8)
        low, high = z_pair(t, lane, 16)
        t = 0.75 * t + 0.25 * jnp.where(zlow, low, high)
        down, up = y_pair(t)
        return 0.75 * t + 0.25 * jnp.where(ylow, down, up)

    wide = [spread4(j) for j in range(9)]
    for j in range(7):
        at = ix + j
        fix = 0.75 * wide[j + 1] + 0.25 * jnp.where(xlow, wide[j], wide[j + 2])
        fix = jnp.where((at >= 3) & (at < 19), fix, 0.0)
        u3[1, at] = u3[1, at] + fix

    def sweep3(i):
        for j in range(1, 6):
            relax3(1 - i, ix + j)

    repeat(0, 2, sweep3)
    for j in range(1, 6):
        e3[ix + j, pl.ds(8, 16), :] = u3[1, ix + j]
    for j in (0, 6):
        e3[ix + j] = jnp.zeros((32, 128), F32)

    lane8 = lanes(8)
    lane24 = lanes(24)
    zero24 = jnp.zeros((24, 128), F32)
    for b in range(5):
        for c in range(3):
            src2[c, b] = zero24

    def fetch(g):
        other_y = lax.rem(iy + 14 + g, 16)
        for b in range(5):
            for c in range(3):
                src2[c, b, pl.ds(4 * g, 4), :] = got[other_y, pl.ds(32 + 12 * b + 4 * c, 4), :]

    for g in range(5):
        fetch(g)
    for p in range(2):
        for c in range(2):
            u2[p, c, 0] = zero24
            u2[p, c, 6] = zero24
    win2 = Window(src2, gain2, 0.0625, 1, functools.partial(near2, lane24))
    inside2 = row_mask(24, iy * 4 - 8, 64)
    keep2 = [inside2 * scalar_mask(ix - 2 + b, 16) for b in range(5)]
    for b in range(5):
        win2.start(b, keep2[b], u2.at[0])
    a_low = lane8 % 2 == 0
    b_low = lane8 // 4 % 2 == 0
    x_low = lane8 // 2 % 2 == 0

    def widen3(c):
        sides = []
        shift = jnp.where(c == 0, 4, 124)
        for yl in range(2):
            pick = (lane8 // 4 % 2 == c) & (lane8 % 2 == yl)
            cells = []
            for bb in range(7):
                t = jnp.where(pick, e3[ix + bb, pl.ds(iy + 5, 8), :], 0.0)
                t = t + lroll(t, 1 - 2 * yl)
                t = t + pltpu.roll(t, shift, 1)
                low, high = z_pair(t, lane8, 8)
                cells.append(0.75 * t + 0.25 * jnp.where(b_low, low, high))
            blocks = []
            for b in range(1, 6):
                low = lroll(jnp.where(a_low, cells[b - 1], cells[b]), -2)
                high = lroll(jnp.where(a_low, cells[b], cells[b + 1]), 2)
                blocks.append(0.75 * cells[b] + 0.25 * jnp.where(x_low, low, high))
            sides.append(blocks)
        for b in range(5):
            t0, t1 = sides[0][b], sides[1][b]
            wide2[c, b, pl.ds(0, 8, 4), :] = 0.75 * t0 + 0.25 * sroll(t1, 1)
            wide2[c, b, pl.ds(1, 8, 4), :] = 0.75 * t0 + 0.25 * t1
            wide2[c, b, pl.ds(2, 8, 4), :] = 0.75 * t1 + 0.25 * t0
            wide2[c, b, pl.ds(3, 8, 4), :] = 0.75 * t1 + 0.25 * sroll(t0, -1)

    repeat(0, 2, widen3)

    def sweep2(i):
        now, later = lax.rem(i, 2), 1 - lax.rem(i, 2)
        add = jnp.where(i == 0, F32(1), F32(0))
        for b in range(5):
            new = win2.relaxed(b, u2.at[now])
            for c in range(2):
                fix = wide2[c, b, pl.ds(4, 24), :] * (keep2[b] * add)
                u2[later, c, b + 1] = new[c] + fix

    repeat(0, 3, sweep2)

    lane16 = lanes(16)
    slot4 = lane16 % 4

    def widen2(b):
        for xl in range(4):
            for c in range(2):
                t = jnp.where(slot4 == xl, u2[1, c, b + 1, pl.ds(4, 16), :], 0.0)
                t = lroll(t, -xl) if xl else t
                t = t + lroll(t, 1)
                t = t + lroll(t, 2)
                low, high = z_pair(t, lane16, 4)
                cell1[c, 4 * b - 4 + xl] = 0.75 * t + 0.25 * jnp.where(slot4 < 2, low, high)

    repeat(1, 4, widen2)
    lane_even = lane16 % 2 == 0

    def mix2(q):
        for c in range(2):
            side = jnp.where(lane_even, cell1[c, q], cell1[c, q + 2])
            t = 0.75 * cell1[c, q + 1] + 0.25 * side
            wide1[c, q, pl.ds(0, 16, 2), :] = 0.75 * t + 0.25 * sroll(t, 1)
            wide1[c, q, pl.ds(1, 16, 2), :] = 0.75 * t + 0.25 * sroll(t, -1)

    repeat(0, 10, mix2, 5)
    for p in range(2):
        for c in range(2):
            u1[p, c, 0] = zero24
            u1[p, c, 11] = zero24
    inside1 = row_mask(24, iy * 8 - 8, 128)

    def correct1(q):
        keep = inside1 * scalar_mask(ix * 4 - 3 + q, 64)
        for c in range(2):
            u1[0, c, q + 1] = ub1[c, q + 1] + wide1[c, q, pl.ds(0, 24), :] * keep

    repeat(0, 10, correct1, 5)
    win1 = Window(src1, gain1, 0.25, 1, functools.partial(near1, lane24))

    def sweep1(i):
        repeat(0, 10, lambda q: win1.relax(q, u1.at[i], u1.at[1 - i]), 5)

    repeat(0, 2, sweep1)

    def widen1(q):
        for c in range(2):
            t = u1[0, c, q + 1, pl.ds(5, 16), :]
            up, down = lroll(t, 1), lroll(t, -1)
            for p in range(2):
                v = jnp.where(lane_even, t, up) if p == 0 else jnp.where(lane_even, down, t)
                low, high = z_pair(v, lane16, 2)
                v = 0.75 * v + 0.25 * jnp.where(lane_even, low, high)
                wide0[c, 2 * q + p, pl.ds(0, 16, 2), :] = 0.75 * v + 0.25 * sroll(v, 1)
                wide0[c, 2 * q + p, pl.ds(1, 16, 2), :] = 0.75 * v + 0.25 * sroll(v, -1)

    repeat(2, 8, widen1, 2)
    inside0 = row_mask(24, iy * 16 - 3, 256)

    def correct0(at):
        for c in range(2):
            low = wide0[c, at - 1, pl.ds(3, 24), :]
            mid = wide0[c, at, pl.ds(3, 24), :]
            high = wide0[c, at + 1, pl.ds(3, 24), :]
            for child, side in ((0, low), (1, high)):
                x = 2 * at - 9 + child
                keep = inside0 * scalar_mask(ix * 16 - 3 + x, 256)
                ua0[c, x] = ub0[c, x] + (0.75 * mid + 0.25 * side) * keep

    repeat(5, 15, correct0, 2)
    win0 = Window(src0, gain0, 1.0, 0, functools.partial(near0, lane24))
    repeat(2, 20, lambda x: win0.relax(x, ua0, ub0s), 3)

    def finish0(x):
        new = win0.relaxed(x + 3, ub0s)
        for c in range(2):
            ua0[c, x + 3] = new[c]
            out[c, x] = ua0[c, x + 3, pl.ds(3, 16), :]

    repeat(0, 16, finish0, 4)


def call(kernel, name, out_shape, scratch, *args):
    vmem = pl.BlockSpec(memory_space=pltpu.VMEM)
    return pl.pallas_call(
        kernel,
        name=name,
        out_shape=[jax.ShapeDtypeStruct(shape, F32) for shape in out_shape],
        in_specs=[pl.BlockSpec(memory_space=pltpu.SMEM)] + [vmem] * (len(args) - 1),
        out_specs=[vmem] * len(out_shape),
        scratch_shapes=[pltpu.VMEM(shape, F32) for shape in scratch],
        compiler_params=pltpu.CompilerParams(vmem_limit_bytes=40 * 1024 * 1024),
    )(*args)


def send(value, axis, step):
    count = lax.axis_size(axis)
    return lax.ppermute(value, axis, [(i, (i + step) % count) for i in range(count)])


def share(value, axis):
    count = lax.axis_size(axis)
    return lax.all_to_all(jnp.broadcast_to(value[None], (count,) + value.shape), axis, 0, 0)


def body(residual_in, wave_sq):
    ix = lax.axis_index("gx")
    iy = lax.axis_index("gy")
    idx = jnp.stack([ix, iy]).astype(jnp.int32)

    own = jnp.concatenate([residual_in, wave_sq[None]], axis=0)
    low = send(own[:, 13:], "gx", 1)
    high = send(own[:, :3], "gx", -1)
    strip = jnp.concatenate([low, own, high], axis=1)
    low = send(strip[:, :, 13:].transpose(0, 2, 1, 3).reshape(9, 22, 128), "gy", 1)
    high = send(strip[:, :, :3].transpose(0, 2, 1, 3).reshape(9, 22, 128), "gy", -1)
    low = low.reshape(3, 3, 22, 128).transpose(0, 2, 1, 3)
    high = high.reshape(3, 3, 22, 128).transpose(0, 2, 1, 3)
    src0 = jnp.concatenate([low, strip, high, jnp.zeros((3, 22, 2, 128), F32)], axis=2)

    n0 = (2, 22, 24, 128)
    n1 = (2, 12, 24, 128)
    own1, gain0, first0 = call(
        down0_kernel, "down0", [(3, 4, 8, 128), n0, n0], [n0, (3, 8, 24, 128)], idx, src0
    )
    low = send(own1[:, 1:], "gx", 1)
    high = send(own1[:, :3], "gx", -1)
    strip = jnp.concatenate([low, own1, high], axis=1)
    low = send(strip, "gy", 1)
    high = send(strip, "gy", -1)
    src1 = jnp.concatenate([low, strip, high], axis=2)

    part, gain1, first1 = call(
        down1_kernel,
        "down1",
        [(16, 128), (2, 10, 24, 128), n1],
        [n1, (3, 10, 24, 128), (3, 8, 8, 128), (2, 8, 8, 128), (2, 10, 8, 128), (2, 10, 8, 128)],
        idx,
        src1,
    )
    line = share(part, "gx")
    ring = jnp.concatenate([line[14:], line, line[:2]], axis=0)
    blocks = lax.dynamic_slice(ring, (ix, 0, 0), (5, 12, 128))
    mine = jnp.concatenate(
        [line[:, 12:14].reshape(32, 128), blocks.reshape(60, 128), jnp.zeros((4, 128), F32)], axis=0
    )
    got = share(mine, "gy")

    wide = (22, 16, 128)
    return call(
        up_kernel,
        "up",
        [(2, 16, 16, 128)],
        [wide, wide, wide, wide, (2, 22, 16, 128)]
        + [(4, 16, 128), (4, 16, 128), (4, 16, 128), (22, 32, 128)]
        + [(3, 5, 24, 128), (2, 5, 24, 128), (2, 2, 7, 24, 128), (2, 5, 32, 128)]
        + [(2, 12, 16, 128), (2, 2, 12, 24, 128), (2, 10, 32, 128), (2, 16, 32, 128), n0, n0],
        idx,
        src0,
        gain0,
        first0,
        src1,
        gain1,
        first1,
        got,
    )[0]


def solution(mesh):
    placed = (P(None, "gx", "gy", None), P("gx", "gy", None))
    return jax.shard_map(
        body, mesh=mesh, in_specs=placed, out_specs=P(None, "gx", "gy", None), check_vma=False
    )
```

```python
import functools

import jax
import jax.numpy as jnp
from jax import lax
from jax.experimental import pallas as pl
from jax.experimental.pallas import tpu as pltpu
from jax.sharding import PartitionSpec as P

OMEGA = 0.6
SHIFT = 0.5
F32 = jnp.float32


def lroll(v, shift):
    return pltpu.roll(v, shift % v.shape[1], 1)


def sroll(v, shift):
    return pltpu.roll(v, shift % v.shape[0], 0)


def lanes(rows):
    return lax.broadcasted_iota(jnp.int32, (rows, 128), 1)


def sublanes(rows):
    return lax.broadcasted_iota(jnp.int32, (rows, 128), 0)


def row_mask(rows, first, count):
    place = sublanes(rows) + first
    return jnp.where((place >= 0) & (place < count), F32(1), F32(0))


def scalar_mask(place, count):
    return jnp.where((place >= 0) & (place < count), F32(1), F32(0))


def z_pair(v, lane, step):
    low = jnp.where(lane >= step, lroll(v, step), 0.0)
    high = jnp.where(lane < 128 - step, lroll(v, -step), 0.0)
    return low, high


def z_sum(v, lane, step):
    low, high = z_pair(v, lane, step)
    return low + high


def y_sum(v):
    return sroll(v, 1) + sroll(v, -1)


def inverse(w, scale, keep):
    real = 6.0 * scale - w
    imag = SHIFT * w
    factor = (OMEGA * keep) / (real * real + imag * imag)
    return real * factor, -imag * factor


def misfit(f, w, v, nb, scale):
    (fr, fi), (vr, vi), (nr, ni) = f, v, nb
    mr = fr - scale * (6.0 * vr - nr) + w * (vr + SHIFT * vi)
    mi = fi - scale * (6.0 * vi - ni) + w * (vi - SHIFT * vr)
    return mr, mi


def cmul(g, m):
    return g[0] * m[0] - g[1] * m[1], g[0] * m[1] + g[1] * m[0]


def repeat(low, high, step, unroll=1):
    def run(i, carry):
        step(i)
        return carry

    lax.fori_loop(low, high, run, 0, unroll=unroll)


class Window:
    def __init__(self, src, gain, scale, pad, neighbours):
        self.src, self.gain, self.scale, self.pad = src, gain, scale, pad
        self.neighbours = neighbours

    def start(self, row, keep, out):
        w = self.src[2, row]
        g = inverse(w, self.scale, keep)
        self.gain[0, row], self.gain[1, row] = g
        u = cmul(g, (self.src[0, row], self.src[1, row]))
        out[0, row + self.pad], out[1, row + self.pad] = u

    def misfit(self, row, field):
        at = row + self.pad
        v = (field[0, at], field[1, at])
        nb = tuple(self.neighbours(field, c, at, v[c]) for c in range(2))
        f = (self.src[0, row], self.src[1, row])
        return v, misfit(f, self.src[2, row], v, nb, self.scale)

    def relaxed(self, row, field):
        v, m = self.misfit(row, field)
        d = cmul((self.gain[0, row], self.gain[1, row]), m)
        return v[0] + d[0], v[1] + d[1]

    def relax(self, row, field, out):
        at = row + self.pad
        out[0, at], out[1, at] = self.relaxed(row, field)


def near0(lane, ref, c, at, v):
    return ref[c, at - 1] + ref[c, at + 1] + y_sum(v) + z_sum(v, lane, 1)


def near1(lane, ref, c, at, v):
    low = lroll(ref[c, at - 1] + v, -1)
    high = lroll(v + ref[c, at + 1], 1)
    return jnp.where(lane % 2 == 0, low, high) + y_sum(v) + z_sum(v, lane, 2)


def near2(lane, ref, c, at, v):
    slot = lane % 4
    low = jnp.where(slot == 0, lroll(ref[c, at - 1], -3), lroll(v, 1))
    high = jnp.where(slot == 3, lroll(ref[c, at + 1], 3), lroll(v, -1))
    return low + high + y_sum(v) + z_sum(v, lane, 4)


def level0(src, gain, first, ix, iy):
    lane = lanes(24)
    win = Window(src, gain, 1.0, 0, functools.partial(near0, lane))
    inside = row_mask(24, iy * 16 - 3, 256)
    repeat(0, 22, lambda x: win.start(x, inside * scalar_mask(ix * 16 - 3 + x, 256), first), 2)
    return win, inside


def down0_kernel(idx, src, out, gain, ub, ua, tmp):
    ix, iy = idx[0], idx[1]
    win, _ = level0(src, gain, ua, ix, iy)
    repeat(1, 21, lambda x: win.relax(x, ua, ub), 4)
    for c in range(2):
        for x in (0, 21):
            ub[c, x] = jnp.zeros((24, 128), F32)
    lane = lanes(8)
    even = lane % 2 == 0

    def halve(q):
        rows = []
        for half in range(2):
            x = 4 * q + 3 + 2 * half
            _, m0 = win.misfit(x, ub)
            _, m1 = win.misfit(x + 1, ub)
            parts = (m0[0] + m1[0], m0[1] + m1[1], src[2, x] + src[2, x + 1])
            got = []
            for c in range(3):
                tmp[c, 2 * q + half] = parts[c]
                t = tmp[c, 2 * q + half, pl.ds(3, 8, 2)] + tmp[c, 2 * q + half, pl.ds(4, 8, 2)]
                got.append(0.125 * (t + lroll(t, -1)))
            rows.append(got)
        for c in range(3):
            out[c, q] = jnp.where(even, rows[0][c], lroll(rows[1][c], 1))

    repeat(0, 4, halve)


def down1_kernel(idx, src, out, src2, gain, ub, ua, tmp, gain2, va, vb):
    ix, iy = idx[0], idx[1]
    lane24 = lanes(24)
    zero24 = jnp.zeros((24, 128), F32)
    for buf in (ua, ub):
        for c in range(2):
            buf[c, 0] = zero24
            buf[c, 13] = zero24
    win = Window(src, gain, 0.25, 1, functools.partial(near1, lane24))
    inside = row_mask(24, iy * 8 - 8, 128)
    repeat(0, 12, lambda q: win.start(q, inside * scalar_mask(ix * 4 - 4 + q, 64), ua), 4)
    repeat(0, 12, lambda q: win.relax(q, ua, ub), 4)
    lane = lanes(16)
    corner = lane % 4 == 0

    def halve(b):
        for j in range(4):
            q = 4 * b + j
            _, m = win.misfit(q, ub)
            parts = (m[0], m[1], src[2, q])
            for c in range(3):
                t = parts[c] + lroll(parts[c], -1)
                tmp[c, q, pl.ds(0, 24), :] = t + lroll(t, -2)
                tmp[c, q, pl.ds(24, 8), :] = jnp.zeros((8, 128), F32)
        for c in range(3):
            packed = jnp.zeros((16, 128), F32)
            for j in range(4):
                q = 4 * b + j
                t = tmp[c, q, pl.ds(0, 16, 2), :] + tmp[c, q, pl.ds(1, 16, 2), :]
                t = jnp.where(corner, 0.125 * t, 0.0)
                packed = packed + (lroll(t, j) if j else t)
            src2[c, b] = packed

    repeat(0, 3, halve)
    for buf in (va, vb):
        for c in range(2):
            buf[c, 0] = jnp.zeros((16, 128), F32)
            buf[c, 4] = jnp.zeros((16, 128), F32)
    win2 = Window(src2, gain2, 0.0625, 1, functools.partial(near2, lane))
    inside2 = row_mask(16, iy * 4 - 4, 64)
    for b in range(3):
        win2.start(b, inside2 * scalar_mask(ix - 1 + b, 16), va)
    for b in range(3):
        win2.relax(b, va, vb)
    _, m = win2.misfit(1, vb)

    def third(v):
        t = v + lroll(v, -1)
        t = t + lroll(t, -4)
        t = 0.125 * jnp.where((lane % 2 == 0) & (lane % 8 < 4), t + sroll(t, -1), 0.0)
        return t[4:5] + lroll(t[6:7], 1)

    field = third(m[0]) + lroll(third(m[1]), 4)
    wave = third(src2[2, 1])
    wave = wave + lroll(wave, 4)
    pair = jnp.concatenate([field, wave] * 4, axis=0)

    def spread(i):
        out[i] = pair

    repeat(0, 64, spread, 8)


def swap(v, real):
    return jnp.where(real, lroll(v, -4), lroll(v, 4))


def up_kernel(
    idx, src0, gain0, ub0, src1, gain1, ub1, src2, flat, out,
    f3, w3, ga3, gb3, ua3, ub3, f4, w4, s4, e3, gain2, u2, wide2, cell1, ua1, ut1, wide1, wide0, ua0, ut0,
):
    ix, iy = idx[0], idx[1]
    lane = lanes(16)
    real = lane // 4 % 2 == 0
    sign = jnp.where(real, F32(SHIFT), F32(-SHIFT))
    xlow = lane // 2 % 2 == 0
    ylow = lane % 2 == 0
    zlow = lane // 8 % 2 == 0
    slot = lane % 4
    row = sublanes(16)
    zero16 = jnp.zeros((16, 128), F32)

    def y_pair(v):
        return jnp.where(row >= 1, sroll(v, 1), 0.0), jnp.where(row < 15, sroll(v, -1), 0.0)

    def packed_gain(w, scale):
        gr, gi = inverse(w, scale, 1.0)
        return gr, jnp.where(real, -gi, gi)

    def packed_misfit(f, w, v, nb, scale):
        return f - scale * (6.0 * v - nb) + w * (v + sign * swap(v, real))

    for at in (0, 1, 2, 19, 20, 21):
        for ref in (f3, w3, ga3, gb3):
            ref[at] = zero16
        for ref in (ua3, ub3):
            ref[at] = zero16
    for j in range(7):
        e3[j] = jnp.zeros((32, 128), F32)

    def start3(x):
        at = x + 3
        f3[at] = flat[pl.ds(32 * x, 16, 2), :]
        w = flat[pl.ds(32 * x + 1, 16, 2), :]
        w3[at] = w
        ga, gb = packed_gain(w, 1.0 / 64)
        ga3[at], gb3[at] = ga, gb
        ua3[at] = ga * f3[at] + gb * swap(f3[at], real)

    def miss3(ref, at):
        v = ref[at]
        down, up = y_pair(v)
        xs = jnp.where(xlow, lroll(ref[at - 1] + v, -2), lroll(v + ref[at + 1], 2))
        ys = jnp.where(ylow, lroll(v + down, -1), lroll(v + up, 1))
        return v, packed_misfit(f3[at], w3[at], v, xs + ys + z_sum(v, lane, 8), 1.0 / 64)

    def relaxed3(ref, at):
        v, m = miss3(ref, at)
        return v + ga3[at] * m + gb3[at] * swap(m, real)

    def relax3(at):
        ub3[at] = relaxed3(ua3, at)

    repeat(0, 16, start3, 8)
    repeat(3, 19, relax3, 8)

    first = (slot == 0) & zlow

    def eighth(v):
        v = v + lroll(v, -1)
        v = v + lroll(v, -2)
        return jnp.where(first, 0.125 * (v + lroll(v, -8)), 0.0)

    def halve3(r):
        f, w = zero16, zero16
        for k in range(4):
            at = 4 * k + r + 3
            fk, wk = eighth(miss3(ub3, at)[1]), eighth(w3[at])
            f = f + (lroll(fk, k) if k else fk)
            w = w + (lroll(wk, k) if k else wk)
        f4[r], w4[r] = f, w

    repeat(0, 4, halve3, 2)
    fs = [f4[r] for r in range(4)]
    ws = [w4[r] for r in range(4)]
    gs = [packed_gain(w, 1.0 / 256) for w in ws]

    def miss4(us):
        low = jnp.where(slot >= 1, lroll(us[3], 1), 0.0)
        high = jnp.where(slot < 3, lroll(us[0], -1), 0.0)
        wide = [low, *us, high]
        ms = []
        for r in range(4):
            down, up = y_pair(us[r])
            nb = wide[r] + wide[r + 2] + down + up + z_sum(us[r], lane, 16)
            ms.append(packed_misfit(fs[r], ws[r], us[r], nb, 1.0 / 256))
        return ms

    def relax4(_, us):
        ms = miss4(us)
        return tuple(u + g[0] * m + g[1] * swap(m, real) for u, g, m in zip(us, gs, ms))

    us = tuple(g[0] * f + g[1] * swap(f, real) for g, f in zip(gs, fs))
    us = lax.fori_loop(0, 5, relax4, us)
    ms = miss4(us)
    total_m = ms[0] + ms[1] + ms[2] + ms[3]
    total_w = ws[0] + ws[1] + ws[2] + ws[3]
    sum_r = jnp.sum(jnp.where(zlow & real, total_m, 0.0))
    sum_i = jnp.sum(jnp.where(zlow & ~real, total_m, 0.0))
    sum_w = jnp.sum(jnp.where(zlow & real, total_w, 0.0))
    numer = jnp.where(real, sum_r - SHIFT * sum_i, sum_i + SHIFT * sum_r)
    const = -numer / (jnp.full((16, 128), (1.0 + SHIFT * SHIFT), F32) * sum_w)
    for r in range(4):
        s4[r] = jnp.where(zlow, us[r] + const, 0.0)

    def spread4(j):
        x = ix - 4 + j
        inside = (x >= 0) & (x < 16)
        x = jnp.clip(x, 0, 15)
        k = x // 4
        t = jnp.where((slot == k) & inside, s4[x - 4 * k], 0.0)
        t = pltpu.roll(t, lax.rem(128 - k, 128), 1)
        t = t + lroll(t, 1)
        t = t + lroll(t, 2)
        t = t + lroll(t, 8)
        low, high = z_pair(t, lane, 16)
        t = 0.75 * t + 0.25 * jnp.where(zlow, low, high)
        down, up = y_pair(t)
        return 0.75 * t + 0.25 * jnp.where(ylow, down, up)

    wide = [spread4(j) for j in range(9)]
    for j in range(7):
        at = ix + j
        fix = 0.75 * wide[j + 1] + 0.25 * jnp.where(xlow, wide[j], wide[j + 2])
        fix = jnp.where((at >= 3) & (at < 19), fix, 0.0)
        ub3[at] = ub3[at] + fix

    def sweep3(_):
        new = [relaxed3(ub3, ix + j) for j in range(1, 6)]
        for j in range(1, 6):
            ub3[ix + j] = new[j - 1]

    repeat(0, 2, sweep3)
    for j in range(1, 6):
        e3[j, pl.ds(8, 16), :] = ub3[ix + j]

    lane8 = lanes(8)
    lane24 = lanes(24)
    zero24 = jnp.zeros((24, 128), F32)
    for c in range(2):
        u2[c, 0] = zero24
        u2[c, 6] = zero24
    win2 = Window(src2, gain2, 0.0625, 1, functools.partial(near2, lane24))
    inside2 = row_mask(24, iy * 4 - 8, 64)
    keep2 = [inside2 * scalar_mask(ix - 2 + b, 16) for b in range(5)]
    for b in range(5):
        win2.start(b, keep2[b], u2)
    a_low = lane8 % 2 == 0
    b_low = lane8 // 4 % 2 == 0
    x_low = lane8 // 2 % 2 == 0

    def widen3(c):
        sides = []
        shift = jnp.where(c == 0, 4, 124)
        for yl in range(2):
            pick = (lane8 // 4 % 2 == c) & (lane8 % 2 == yl)
            cells = []
            for bb in range(7):
                t = jnp.where(pick, e3[bb, pl.ds(iy + 5, 8), :], 0.0)
                t = t + lroll(t, 1 - 2 * yl)
                t = t + pltpu.roll(t, shift, 1)
                low, high = z_pair(t, lane8, 8)
                cells.append(0.75 * t + 0.25 * jnp.where(b_low, low, high))
            blocks = []
            for b in range(1, 6):
                low = lroll(jnp.where(a_low, cells[b - 1], cells[b]), -2)
                high = lroll(jnp.where(a_low, cells[b], cells[b + 1]), 2)
                blocks.append(0.75 * cells[b] + 0.25 * jnp.where(x_low, low, high))
            sides.append(blocks)
        for b in range(5):
            t0, t1 = sides[0][b], sides[1][b]
            wide2[c, b, pl.ds(0, 8, 4), :] = 0.75 * t0 + 0.25 * sroll(t1, 1)
            wide2[c, b, pl.ds(1, 8, 4), :] = 0.75 * t0 + 0.25 * t1
            wide2[c, b, pl.ds(2, 8, 4), :] = 0.75 * t1 + 0.25 * t0
            wide2[c, b, pl.ds(3, 8, 4), :] = 0.75 * t1 + 0.25 * sroll(t0, -1)

    repeat(0, 2, widen3)

    def sweep2(i):
        add = jnp.where(i == 0, F32(1), F32(0))
        new = [win2.relaxed(b, u2) for b in range(5)]
        for b in range(5):
            for c in range(2):
                fix = wide2[c, b, pl.ds(4, 24), :] * (keep2[b] * add)
                u2[c, b + 1] = new[b][c] + fix

    repeat(0, 3, sweep2)

    lane16 = lanes(16)
    slot4 = lane16 % 4

    def widen2(b):
        for xl in range(4):
            for c in range(2):
                t = jnp.where(slot4 == xl, u2[c, b + 1, pl.ds(4, 16), :], 0.0)
                t = lroll(t, -xl) if xl else t
                t = t + lroll(t, 1)
                t = t + lroll(t, 2)
                low, high = z_pair(t, lane16, 4)
                cell1[c, 4 * b - 4 + xl] = 0.75 * t + 0.25 * jnp.where(slot4 < 2, low, high)

    repeat(1, 4, widen2)
    lane_even = lane16 % 2 == 0

    def mix2(q):
        for c in range(2):
            side = jnp.where(lane_even, cell1[c, q - 1], cell1[c, q + 1])
            t = 0.75 * cell1[c, q] + 0.25 * side
            wide1[c, q, pl.ds(0, 16, 2), :] = 0.75 * t + 0.25 * sroll(t, 1)
            wide1[c, q, pl.ds(1, 16, 2), :] = 0.75 * t + 0.25 * sroll(t, -1)

    repeat(2, 10, mix2, 4)
    for c in range(2):
        ua1[c, 2] = zero24
        ua1[c, 11] = zero24
    inside1 = row_mask(24, iy * 8 - 8, 128)

    def correct1(q):
        keep = inside1 * scalar_mask(ix * 4 - 4 + q, 64)
        for c in range(2):
            ua1[c, q + 1] = ub1[c, q + 1] + wide1[c, q, pl.ds(0, 24), :] * keep

    repeat(2, 10, correct1, 4)
    win1 = Window(src1, gain1, 0.25, 1, functools.partial(near1, lane24))

    repeat(2, 10, lambda q: win1.relax(q, ua1, ut1), 4)
    repeat(3, 9, lambda q: win1.relax(q, ut1, ua1), 3)

    def widen1(q):
        for c in range(2):
            t = ua1[c, q + 1, pl.ds(5, 16), :]
            up, down = lroll(t, 1), lroll(t, -1)
            for p in range(2):
                v = jnp.where(lane_even, t, up) if p == 0 else jnp.where(lane_even, down, t)
                low, high = z_pair(v, lane16, 2)
                v = 0.75 * v + 0.25 * jnp.where(lane_even, low, high)
                wide0[c, 2 * q - 2 + p, pl.ds(0, 16, 2), :] = 0.75 * v + 0.25 * sroll(v, 1)
                wide0[c, 2 * q - 2 + p, pl.ds(1, 16, 2), :] = 0.75 * v + 0.25 * sroll(v, -1)

    repeat(3, 9, widen1, 2)
    inside0 = row_mask(24, iy * 16 - 3, 256)

    def correct0(at):
        for c in range(2):
            low = wide0[c, at - 1, pl.ds(3, 24), :]
            mid = wide0[c, at, pl.ds(3, 24), :]
            high = wide0[c, at + 1, pl.ds(3, 24), :]
            for child, side in ((0, low), (1, high)):
                x = 2 * at - 9 + child
                keep = inside0 * scalar_mask(ix * 16 - 3 + x, 256)
                ua0[c, x] = ub0[c, x] + (0.75 * mid + 0.25 * side) * keep

    repeat(5, 15, correct0, 2)
    win0 = Window(src0, gain0, 1.0, 0, functools.partial(near0, lane24))
    repeat(2, 20, lambda x: win0.relax(x, ua0, ut0), 3)

    def finish0(x):
        new = win0.relaxed(x + 3, ut0)
        for c in range(2):
            ua0[c, x + 3] = new[c]
            out[c, x] = ua0[c, x + 3, pl.ds(3, 16), :]

    repeat(0, 16, finish0, 4)


def call(kernel, name, out_shape, scratch, *args):
    vmem = pl.BlockSpec(memory_space=pltpu.VMEM)
    return pl.pallas_call(
        kernel,
        name=name,
        out_shape=[jax.ShapeDtypeStruct(shape, F32) for shape in out_shape],
        in_specs=[pl.BlockSpec(memory_space=pltpu.SMEM)] + [vmem] * (len(args) - 1),
        out_specs=[vmem] * len(out_shape),
        scratch_shapes=[pltpu.VMEM(shape, F32) for shape in scratch],
        compiler_params=pltpu.CompilerParams(vmem_limit_bytes=40 * 1024 * 1024),
    )(*args)


def send(value, axis, step):
    count = lax.axis_size(axis)
    return lax.ppermute(value, axis, [(i, (i + step) % count) for i in range(count)])


def share(value, axis):
    count = lax.axis_size(axis)
    return lax.all_to_all(jnp.broadcast_to(value[None], (count,) + value.shape), axis, 0, 0)


def body(residual_in, wave_sq):
    ix = lax.axis_index("gx")
    iy = lax.axis_index("gy")
    idx = jnp.stack([ix, iy]).astype(jnp.int32)

    own = jnp.concatenate([residual_in, wave_sq[None]], axis=0)
    low = send(own[:, 13:], "gx", 1)
    high = send(own[:, :3], "gx", -1)
    strip = jnp.concatenate([low, own, high], axis=1)
    low = send(strip[:, :, 13:].transpose(0, 2, 1, 3).reshape(9, 22, 128), "gy", 1)
    high = send(strip[:, :, :3].transpose(0, 2, 1, 3).reshape(9, 22, 128), "gy", -1)
    low = low.reshape(3, 3, 22, 128).transpose(0, 2, 1, 3)
    high = high.reshape(3, 3, 22, 128).transpose(0, 2, 1, 3)
    src0 = jnp.concatenate([low, strip, high, jnp.zeros((3, 22, 2, 128), F32)], axis=2)

    n0 = (2, 22, 24, 128)
    n1 = (2, 14, 24, 128)
    own1, gain0, first0 = call(
        down0_kernel, "down0", [(3, 4, 8, 128), n0, n0], [n0, (3, 8, 24, 128)], idx, src0
    )
    low = send(own1, "gx", 1)
    high = send(own1, "gx", -1)
    strip = jnp.concatenate([low, own1, high], axis=1)
    low = send(strip, "gy", 1)
    high = send(strip, "gy", -1)
    src1 = jnp.concatenate([low, strip, high], axis=2)

    part, own2, gain1, first1 = call(
        down1_kernel,
        "down1",
        [(64, 8, 128), (3, 3, 16, 128), (2, 12, 24, 128), n1],
        [n1, (3, 12, 32, 128), (2, 3, 16, 128), (2, 5, 16, 128), (2, 5, 16, 128)],
        idx,
        src1,
    )
    part = part.reshape(256, 2, 128)
    flat = lax.all_to_all(part, ("gx", "gy"), 0, 0).reshape(512, 128)
    low = send(own2[:, :2], "gx", 1)
    high = send(own2[:, 1:], "gx", -1)
    strip = jnp.concatenate([low, own2[:, 1:2], high], axis=1)
    low = send(strip[:, :, :8], "gy", 1)
    high = send(strip[:, :, 4:12], "gy", -1)
    src2 = jnp.concatenate(
        [low, strip[:, :, 4:8], high, jnp.zeros((3, 5, 4, 128), F32)], axis=2
    )

    wide = (22, 16, 128)
    return call(
        up_kernel,
        "up",
        [(2, 16, 16, 128)],
        [wide, wide, wide, wide, wide, wide]
        + [(4, 16, 128), (4, 16, 128), (4, 16, 128), (7, 32, 128)]
        + [(2, 5, 24, 128), (2, 7, 24, 128), (2, 5, 32, 128)]
        + [(2, 12, 16, 128), n1, n1, (2, 12, 32, 128), (2, 16, 32, 128), n0, n0],
        idx,
        src0,
        gain0,
        first0,
        src1,
        gain1,
        first1,
        src2,
        flat,
    )[0]


def solution(mesh):
    placed = (P(None, "gx", "gy", None), P("gx", "gy", None))
    return jax.shard_map(
        body, mesh=mesh, in_specs=placed, out_specs=P(None, "gx", "gy", None), check_vma=False
    )
```

```python
import functools

import jax
import jax.numpy as jnp
from jax import lax
from jax.experimental import pallas as pl
from jax.experimental.pallas import tpu as pltpu
from jax.sharding import Mesh, PartitionSpec as P

OMEGA = 0.6
SHIFT = 0.5
F32 = jnp.float32
GX = ("z", "c")


def lroll(v, shift):
    return pltpu.roll(v, shift % v.shape[1], 1)


def sroll(v, shift):
    return pltpu.roll(v, shift % v.shape[0], 0)


def lanes(rows):
    return lax.broadcasted_iota(jnp.int32, (rows, 128), 1)


def sublanes(rows):
    return lax.broadcasted_iota(jnp.int32, (rows, 128), 0)


def row_mask(rows, first, count):
    place = sublanes(rows) + first
    return jnp.where((place >= 0) & (place < count), F32(1), F32(0))


def scalar_mask(place, count):
    return jnp.where((place >= 0) & (place < count), F32(1), F32(0))


def z_pair(v, lane, step):
    low = jnp.where(lane >= step, lroll(v, step), 0.0)
    high = jnp.where(lane < 128 - step, lroll(v, -step), 0.0)
    return low, high


def z_sum(v, lane, step):
    low, high = z_pair(v, lane, step)
    return low + high


def y_sum(v):
    return sroll(v, 1) + sroll(v, -1)


def inverse(w, scale, keep):
    real = 6.0 * scale - w
    imag = SHIFT * w
    factor = (OMEGA * keep) / (real * real + imag * imag)
    return real * factor, -imag * factor


def misfit(f, w, v, nb, scale):
    (fr, fi), (vr, vi), (nr, ni) = f, v, nb
    mr = fr - scale * (6.0 * vr - nr) + w * (vr + SHIFT * vi)
    mi = fi - scale * (6.0 * vi - ni) + w * (vi - SHIFT * vr)
    return mr, mi


def cmul(g, m):
    return g[0] * m[0] - g[1] * m[1], g[0] * m[1] + g[1] * m[0]


def repeat(low, high, step, unroll=1):
    def run(i, carry):
        step(i)
        return carry

    lax.fori_loop(low, high, run, 0, unroll=unroll)


class Window:
    def __init__(self, src, gain, scale, pad, neighbours):
        self.src, self.gain, self.scale, self.pad = src, gain, scale, pad
        self.neighbours = neighbours

    def start(self, row, keep, out):
        w = self.src[2, row]
        g = inverse(w, self.scale, keep)
        self.gain[0, row], self.gain[1, row] = g
        u = cmul(g, (self.src[0, row], self.src[1, row]))
        out[0, row + self.pad], out[1, row + self.pad] = u

    def misfit(self, row, field):
        at = row + self.pad
        v = (field[0, at], field[1, at])
        nb = tuple(self.neighbours(field, c, at, v[c]) for c in range(2))
        f = (self.src[0, row], self.src[1, row])
        return v, misfit(f, self.src[2, row], v, nb, self.scale)

    def relaxed(self, row, field):
        v, m = self.misfit(row, field)
        d = cmul((self.gain[0, row], self.gain[1, row]), m)
        return v[0] + d[0], v[1] + d[1]

    def relax(self, row, field, out):
        at = row + self.pad
        out[0, at], out[1, at] = self.relaxed(row, field)


def near0(lane, ref, c, at, v):
    return ref[c, at - 1] + ref[c, at + 1] + y_sum(v) + z_sum(v, lane, 1)


def near1(lane, ref, c, at, v):
    low = lroll(ref[c, at - 1] + v, -1)
    high = lroll(v + ref[c, at + 1], 1)
    return jnp.where(lane % 2 == 0, low, high) + y_sum(v) + z_sum(v, lane, 2)


def near2(lane, ref, c, at, v):
    slot = lane % 4
    low = jnp.where(slot == 0, lroll(ref[c, at - 1], -3), lroll(v, 1))
    high = jnp.where(slot == 3, lroll(ref[c, at + 1], 3), lroll(v, -1))
    return low + high + y_sum(v) + z_sum(v, lane, 4)


def level0(src, gain, first, ix, iy):
    lane = lanes(24)
    win = Window(src, gain, 1.0, 0, functools.partial(near0, lane))
    inside = row_mask(24, iy * 16 - 3, 256)
    repeat(0, 22, lambda x: win.start(x, inside * scalar_mask(ix * 16 - 3 + x, 256), first), 2)
    return win, inside


def down0_kernel(idx, src, out, gain, ub, ua, tmp):
    ix, iy = idx[0], idx[1]
    win, _ = level0(src, gain, ua, ix, iy)
    repeat(1, 21, lambda x: win.relax(x, ua, ub), 4)
    for c in range(2):
        for x in (0, 21):
            ub[c, x] = jnp.zeros((24, 128), F32)
    lane = lanes(8)
    even = lane % 2 == 0

    def halve(q):
        rows = []
        for half in range(2):
            x = 4 * q + 3 + 2 * half
            _, m0 = win.misfit(x, ub)
            _, m1 = win.misfit(x + 1, ub)
            parts = (m0[0] + m1[0], m0[1] + m1[1], src[2, x] + src[2, x + 1])
            got = []
            for c in range(3):
                tmp[c, 2 * q + half] = parts[c]
                t = tmp[c, 2 * q + half, pl.ds(3, 8, 2)] + tmp[c, 2 * q + half, pl.ds(4, 8, 2)]
                got.append(0.125 * (t + lroll(t, -1)))
            rows.append(got)
        for c in range(3):
            out[c, q] = jnp.where(even, rows[0][c], lroll(rows[1][c], 1))

    repeat(0, 4, halve)


def down1_kernel(idx, src, out, src2, gain, ub, ua, tmp, gain2, va, vb):
    ix, iy = idx[0], idx[1]
    lane24 = lanes(24)
    zero24 = jnp.zeros((24, 128), F32)
    for buf in (ua, ub):
        for c in range(2):
            buf[c, 0] = zero24
            buf[c, 13] = zero24
    win = Window(src, gain, 0.25, 1, functools.partial(near1, lane24))
    inside = row_mask(24, iy * 8 - 8, 128)
    repeat(0, 12, lambda q: win.start(q, inside * scalar_mask(ix * 4 - 4 + q, 64), ua), 4)
    repeat(0, 12, lambda q: win.relax(q, ua, ub), 4)
    lane = lanes(16)
    corner = lane % 4 == 0

    def halve(b):
        for j in range(4):
            q = 4 * b + j
            _, m = win.misfit(q, ub)
            parts = (m[0], m[1], src[2, q])
            for c in range(3):
                t = parts[c] + lroll(parts[c], -1)
                tmp[c, q, pl.ds(0, 24), :] = t + lroll(t, -2)
                tmp[c, q, pl.ds(24, 8), :] = jnp.zeros((8, 128), F32)
        for c in range(3):
            packed = jnp.zeros((16, 128), F32)
            for j in range(4):
                q = 4 * b + j
                t = tmp[c, q, pl.ds(0, 16, 2), :] + tmp[c, q, pl.ds(1, 16, 2), :]
                t = jnp.where(corner, 0.125 * t, 0.0)
                packed = packed + (lroll(t, j) if j else t)
            src2[c, b] = packed

    repeat(0, 3, halve)
    for buf in (va, vb):
        for c in range(2):
            buf[c, 0] = jnp.zeros((16, 128), F32)
            buf[c, 4] = jnp.zeros((16, 128), F32)
    win2 = Window(src2, gain2, 0.0625, 1, functools.partial(near2, lane))
    inside2 = row_mask(16, iy * 4 - 4, 64)
    for b in range(3):
        win2.start(b, inside2 * scalar_mask(ix - 1 + b, 16), va)
    for b in range(3):
        win2.relax(b, va, vb)
    _, m = win2.misfit(1, vb)

    def third(v):
        t = v + lroll(v, -1)
        t = t + lroll(t, -4)
        t = 0.125 * jnp.where((lane % 2 == 0) & (lane % 8 < 4), t + sroll(t, -1), 0.0)
        return t[4:5] + lroll(t[6:7], 1)

    field = third(m[0]) + lroll(third(m[1]), 4)
    wave = third(src2[2, 1])
    wave = wave + lroll(wave, 4)
    pair = jnp.concatenate([field, wave] * 4, axis=0)

    def spread(i):
        out[i] = pair

    repeat(0, 32, spread, 8)


def swap(v, real):
    return jnp.where(real, lroll(v, -4), lroll(v, 4))


def coarse_kernel(idx, own, other, out, f3, w3, ga3, gb3, ua3, ub3, f4, w4, s4, e3):
    ix, iy = idx[0], idx[1]
    lane = lanes(16)
    real = lane // 4 % 2 == 0
    sign = jnp.where(real, F32(SHIFT), F32(-SHIFT))
    xlow = lane // 2 % 2 == 0
    ylow = lane % 2 == 0
    zlow = lane // 8 % 2 == 0
    slot = lane % 4
    row = sublanes(16)
    zero16 = jnp.zeros((16, 128), F32)

    def y_pair(v):
        return jnp.where(row >= 1, sroll(v, 1), 0.0), jnp.where(row < 15, sroll(v, -1), 0.0)

    def packed_gain(w, scale):
        gr, gi = inverse(w, scale, 1.0)
        return gr, jnp.where(real, -gi, gi)

    def packed_misfit(f, w, v, nb, scale):
        return f - scale * (6.0 * v - nb) + w * (v + sign * swap(v, real))

    for at in (0, 1, 2, 19, 20, 21):
        for ref in (f3, w3, ga3, gb3):
            ref[at] = zero16
        for ref in (ua3, ub3):
            ref[at] = zero16
    for j in range(7):
        e3[j] = jnp.zeros((32, 128), F32)

    core = lax.rem(ix, 2)

    def start3(z):
        for part, at in ((own, 2 * z + core + 3), (other, 2 * z + 4 - core)):
            f = part[pl.ds(32 * z, 16, 2), :]
            w = part[pl.ds(32 * z + 1, 16, 2), :]
            ga, gb = packed_gain(w, 1.0 / 64)
            f3[at], w3[at], ga3[at], gb3[at] = f, w, ga, gb
            ua3[at] = ga * f + gb * swap(f, real)

    def miss3(ref, at):
        v = ref[at]
        down, up = y_pair(v)
        xs = jnp.where(xlow, lroll(ref[at - 1] + v, -2), lroll(v + ref[at + 1], 2))
        ys = jnp.where(ylow, lroll(v + down, -1), lroll(v + up, 1))
        return v, packed_misfit(f3[at], w3[at], v, xs + ys + z_sum(v, lane, 8), 1.0 / 64)

    def relaxed3(ref, at):
        v, m = miss3(ref, at)
        return v + ga3[at] * m + gb3[at] * swap(m, real)

    def relax3(at):
        ub3[at] = relaxed3(ua3, at)

    repeat(0, 8, start3, 4)
    repeat(3, 19, relax3, 8)

    first = (slot == 0) & zlow

    def eighth(v):
        v = v + lroll(v, -1)
        v = v + lroll(v, -2)
        return jnp.where(first, 0.125 * (v + lroll(v, -8)), 0.0)

    def halve3(r):
        f, w = zero16, zero16
        for k in range(4):
            at = 4 * k + r + 3
            fk, wk = eighth(miss3(ub3, at)[1]), eighth(w3[at])
            f = f + (lroll(fk, k) if k else fk)
            w = w + (lroll(wk, k) if k else wk)
        f4[r], w4[r] = f, w

    repeat(0, 4, halve3, 2)
    fs = [f4[r] for r in range(4)]
    ws = [w4[r] for r in range(4)]
    gs = [packed_gain(w, 1.0 / 256) for w in ws]

    def miss4(us):
        low = jnp.where(slot >= 1, lroll(us[3], 1), 0.0)
        high = jnp.where(slot < 3, lroll(us[0], -1), 0.0)
        wide = [low, *us, high]
        ms = []
        for r in range(4):
            down, up = y_pair(us[r])
            nb = wide[r] + wide[r + 2] + down + up + z_sum(us[r], lane, 16)
            ms.append(packed_misfit(fs[r], ws[r], us[r], nb, 1.0 / 256))
        return ms

    def relax4(_, us):
        ms = miss4(us)
        return tuple(u + g[0] * m + g[1] * swap(m, real) for u, g, m in zip(us, gs, ms))

    us = tuple(g[0] * f + g[1] * swap(f, real) for g, f in zip(gs, fs))
    us = lax.fori_loop(0, 5, relax4, us)
    ms = miss4(us)
    total_m = ms[0] + ms[1] + ms[2] + ms[3]
    total_w = ws[0] + ws[1] + ws[2] + ws[3]
    sum_r = jnp.sum(jnp.where(zlow & real, total_m, 0.0))
    sum_i = jnp.sum(jnp.where(zlow & ~real, total_m, 0.0))
    sum_w = jnp.sum(jnp.where(zlow & real, total_w, 0.0))
    numer = jnp.where(real, sum_r - SHIFT * sum_i, sum_i + SHIFT * sum_r)
    const = -numer / (jnp.full((16, 128), (1.0 + SHIFT * SHIFT), F32) * sum_w)
    for r in range(4):
        s4[r] = jnp.where(zlow, us[r] + const, 0.0)

    def spread4(j):
        x = ix - 4 + j
        inside = (x >= 0) & (x < 16)
        x = jnp.clip(x, 0, 15)
        k = x // 4
        t = jnp.where((slot == k) & inside, s4[x - 4 * k], 0.0)
        t = pltpu.roll(t, lax.rem(128 - k, 128), 1)
        t = t + lroll(t, 1)
        t = t + lroll(t, 2)
        t = t + lroll(t, 8)
        low, high = z_pair(t, lane, 16)
        t = 0.75 * t + 0.25 * jnp.where(zlow, low, high)
        down, up = y_pair(t)
        return 0.75 * t + 0.25 * jnp.where(ylow, down, up)

    wide = [spread4(j) for j in range(9)]
    for j in range(7):
        at = ix + j
        fix = 0.75 * wide[j + 1] + 0.25 * jnp.where(xlow, wide[j], wide[j + 2])
        fix = jnp.where((at >= 3) & (at < 19), fix, 0.0)
        ub3[at] = ub3[at] + fix

    def sweep3(_):
        new = [relaxed3(ub3, ix + j) for j in range(1, 6)]
        for j in range(1, 6):
            ub3[ix + j] = new[j - 1]

    repeat(0, 2, sweep3)
    for j in range(1, 6):
        e3[j, pl.ds(8, 16), :] = ub3[ix + j]

    for j in range(7):
        out[j] = e3[j, pl.ds(iy + 5, 8), :]


def up_kernel(
    idx, src0, gain0, ub0, src1, gain1, ub1, src2, near, out,
    gain2, u2, wide2, cell1, ua1, ut1, wide1, wide0, ua0, ut0,
):
    ix, iy = idx[0], idx[1]
    lane8 = lanes(8)
    lane24 = lanes(24)
    zero24 = jnp.zeros((24, 128), F32)
    for c in range(2):
        u2[c, 0] = zero24
        u2[c, 6] = zero24
    win2 = Window(src2, gain2, 0.0625, 1, functools.partial(near2, lane24))
    inside2 = row_mask(24, iy * 4 - 8, 64)
    keep2 = [inside2 * scalar_mask(ix - 2 + b, 16) for b in range(5)]
    for b in range(5):
        win2.start(b, keep2[b], u2)
    a_low = lane8 % 2 == 0
    b_low = lane8 // 4 % 2 == 0
    x_low = lane8 // 2 % 2 == 0

    def widen3(c):
        sides = []
        shift = jnp.where(c == 0, 4, 124)
        for yl in range(2):
            pick = (lane8 // 4 % 2 == c) & (lane8 % 2 == yl)
            cells = []
            for bb in range(7):
                t = jnp.where(pick, near[bb], 0.0)
                t = t + lroll(t, 1 - 2 * yl)
                t = t + pltpu.roll(t, shift, 1)
                low, high = z_pair(t, lane8, 8)
                cells.append(0.75 * t + 0.25 * jnp.where(b_low, low, high))
            blocks = []
            for b in range(1, 6):
                low = lroll(jnp.where(a_low, cells[b - 1], cells[b]), -2)
                high = lroll(jnp.where(a_low, cells[b], cells[b + 1]), 2)
                blocks.append(0.75 * cells[b] + 0.25 * jnp.where(x_low, low, high))
            sides.append(blocks)
        for b in range(5):
            t0, t1 = sides[0][b], sides[1][b]
            wide2[c, b, pl.ds(0, 8, 4), :] = 0.75 * t0 + 0.25 * sroll(t1, 1)
            wide2[c, b, pl.ds(1, 8, 4), :] = 0.75 * t0 + 0.25 * t1
            wide2[c, b, pl.ds(2, 8, 4), :] = 0.75 * t1 + 0.25 * t0
            wide2[c, b, pl.ds(3, 8, 4), :] = 0.75 * t1 + 0.25 * sroll(t0, -1)

    repeat(0, 2, widen3)

    def sweep2(i):
        add = jnp.where(i == 0, F32(1), F32(0))
        new = [win2.relaxed(b, u2) for b in range(5)]
        for b in range(5):
            for c in range(2):
                fix = wide2[c, b, pl.ds(4, 24), :] * (keep2[b] * add)
                u2[c, b + 1] = new[b][c] + fix

    repeat(0, 3, sweep2)

    lane16 = lanes(16)
    slot4 = lane16 % 4

    def widen2(b):
        for xl in range(4):
            for c in range(2):
                t = jnp.where(slot4 == xl, u2[c, b + 1, pl.ds(4, 16), :], 0.0)
                t = lroll(t, -xl) if xl else t
                t = t + lroll(t, 1)
                t = t + lroll(t, 2)
                low, high = z_pair(t, lane16, 4)
                cell1[c, 4 * b - 4 + xl] = 0.75 * t + 0.25 * jnp.where(slot4 < 2, low, high)

    repeat(1, 4, widen2)
    lane_even = lane16 % 2 == 0

    def mix2(q):
        for c in range(2):
            side = jnp.where(lane_even, cell1[c, q - 1], cell1[c, q + 1])
            t = 0.75 * cell1[c, q] + 0.25 * side
            wide1[c, q, pl.ds(0, 16, 2), :] = 0.75 * t + 0.25 * sroll(t, 1)
            wide1[c, q, pl.ds(1, 16, 2), :] = 0.75 * t + 0.25 * sroll(t, -1)

    repeat(2, 10, mix2, 4)
    for c in range(2):
        ua1[c, 2] = zero24
        ua1[c, 11] = zero24
    inside1 = row_mask(24, iy * 8 - 8, 128)

    def correct1(q):
        keep = inside1 * scalar_mask(ix * 4 - 4 + q, 64)
        for c in range(2):
            ua1[c, q + 1] = ub1[c, q + 1] + wide1[c, q, pl.ds(0, 24), :] * keep

    repeat(2, 10, correct1, 4)
    win1 = Window(src1, gain1, 0.25, 1, functools.partial(near1, lane24))

    repeat(2, 10, lambda q: win1.relax(q, ua1, ut1), 4)
    repeat(3, 9, lambda q: win1.relax(q, ut1, ua1), 3)

    def widen1(q):
        for c in range(2):
            t = ua1[c, q + 1, pl.ds(5, 16), :]
            up, down = lroll(t, 1), lroll(t, -1)
            for p in range(2):
                v = jnp.where(lane_even, t, up) if p == 0 else jnp.where(lane_even, down, t)
                low, high = z_pair(v, lane16, 2)
                v = 0.75 * v + 0.25 * jnp.where(lane_even, low, high)
                wide0[c, 2 * q - 2 + p, pl.ds(0, 16, 2), :] = 0.75 * v + 0.25 * sroll(v, 1)
                wide0[c, 2 * q - 2 + p, pl.ds(1, 16, 2), :] = 0.75 * v + 0.25 * sroll(v, -1)

    repeat(3, 9, widen1, 2)
    inside0 = row_mask(24, iy * 16 - 3, 256)

    def correct0(at):
        for c in range(2):
            low = wide0[c, at - 1, pl.ds(3, 24), :]
            mid = wide0[c, at, pl.ds(3, 24), :]
            high = wide0[c, at + 1, pl.ds(3, 24), :]
            for child, side in ((0, low), (1, high)):
                x = 2 * at - 9 + child
                keep = inside0 * scalar_mask(ix * 16 - 3 + x, 256)
                ua0[c, x] = ub0[c, x] + (0.75 * mid + 0.25 * side) * keep

    repeat(5, 15, correct0, 2)
    win0 = Window(src0, gain0, 1.0, 0, functools.partial(near0, lane24))
    repeat(2, 20, lambda x: win0.relax(x, ua0, ut0), 3)

    def finish0(x):
        new = win0.relaxed(x + 3, ut0)
        for c in range(2):
            ua0[c, x + 3] = new[c]
            out[c, x] = ua0[c, x + 3, pl.ds(3, 16), :]

    repeat(0, 16, finish0, 4)


def call(kernel, name, out_shape, scratch, *args, micros=2):
    vmem = pl.BlockSpec(memory_space=pltpu.VMEM)
    return pl.pallas_call(
        kernel,
        name=name,
        out_shape=[jax.ShapeDtypeStruct(shape, F32) for shape in out_shape],
        in_specs=[pl.BlockSpec(memory_space=pltpu.SMEM)] + [vmem] * (len(args) - 1),
        out_specs=[vmem] * len(out_shape),
        scratch_shapes=[pltpu.VMEM(shape, F32) for shape in scratch],
        cost_estimate=pl.CostEstimate(
            flops=0, bytes_accessed=micros * 3_500_000, transcendentals=0
        ),
        compiler_params=pltpu.CompilerParams(vmem_limit_bytes=40 * 1024 * 1024),
    )(*args)


def send(value, axis, step):
    count = lax.axis_size(axis)
    return lax.ppermute(value, axis, [(i, (i + step) % count) for i in range(count)])


def body(residual_in, wave_sq):
    ix = lax.axis_index(GX)
    iy = lax.axis_index("gy")
    idx = jnp.stack([ix, iy]).astype(jnp.int32)

    own = jnp.concatenate([residual_in, wave_sq[None]], axis=0)
    low = send(own[:, 13:], GX, 1)
    high = send(own[:, :3], GX, -1)
    strip = jnp.concatenate([low, own, high], axis=1)
    low = send(strip[:, :, 13:].transpose(0, 2, 1, 3).reshape(9, 22, 128), "gy", 1)
    high = send(strip[:, :, :3].transpose(0, 2, 1, 3).reshape(9, 22, 128), "gy", -1)
    low = low.reshape(3, 3, 22, 128).transpose(0, 2, 1, 3)
    high = high.reshape(3, 3, 22, 128).transpose(0, 2, 1, 3)
    src0 = jnp.concatenate([low, strip, high, jnp.zeros((3, 22, 2, 128), F32)], axis=2)

    n0 = (2, 22, 24, 128)
    n1 = (2, 14, 24, 128)
    own1, gain0, first0 = call(
        down0_kernel, "down0", [(3, 4, 8, 128), n0, n0], [n0, (3, 8, 24, 128)], idx, src0
    )
    low = send(own1, GX, 1)
    high = send(own1, GX, -1)
    strip = jnp.concatenate([low, own1, high], axis=1)
    low = send(strip, "gy", 1)
    high = send(strip, "gy", -1)
    src1 = jnp.concatenate([low, strip, high], axis=2)

    part, own2, gain1, first1 = call(
        down1_kernel,
        "down1",
        [(32, 8, 128), (3, 3, 16, 128), (2, 12, 24, 128), n1],
        [n1, (3, 12, 32, 128), (2, 3, 16, 128), (2, 5, 16, 128), (2, 5, 16, 128)],
        idx,
        src1,
    )
    part = part.reshape(128, 2, 128)
    line = lax.all_to_all(part, ("z", "gy"), 0, 0).reshape(256, 128)
    low = send(own2[:, :2], GX, 1)
    high = send(own2[:, 1:], GX, -1)
    strip = jnp.concatenate([low, own2[:, 1:2], high], axis=1)
    low = send(strip[:, :, :8], "gy", 1)
    high = send(strip[:, :, 4:12], "gy", -1)
    src2 = jnp.concatenate(
        [low, strip[:, :, 4:8], high, jnp.zeros((3, 5, 4, 128), F32)], axis=2
    )

    cross = lax.ppermute(line, "c", [(0, 1), (1, 0)])

    wide = (22, 16, 128)
    near = call(
        coarse_kernel,
        "coarse",
        [(7, 8, 128)],
        [wide, wide, wide, wide, wide, wide]
        + [(4, 16, 128), (4, 16, 128), (4, 16, 128), (7, 32, 128)],
        idx,
        line,
        cross,
        micros=5,
    )[0]
    return call(
        up_kernel,
        "up",
        [(2, 16, 16, 128)],
        [(2, 5, 24, 128), (2, 7, 24, 128), (2, 5, 32, 128)]
        + [(2, 12, 16, 128), n1, n1, (2, 12, 32, 128), (2, 16, 32, 128), n0, n0],
        idx,
        src0,
        gain0,
        first0,
        src1,
        gain1,
        first1,
        src2,
        near,
        micros=6,
    )[0]


def solution(mesh):
    rows, columns = mesh.devices.shape
    fine = Mesh(mesh.devices.reshape(rows // 2, 2, columns), ("z", "c", "gy"))
    placed = (P(None, GX, "gy", None), P(GX, "gy", None))
    return jax.shard_map(
        body, mesh=fine, in_specs=placed, out_specs=P(None, GX, "gy", None), check_vma=False
    )
```

```python
import functools

import jax
import jax.numpy as jnp
from jax import lax
from jax.experimental import pallas as pl
from jax.experimental.pallas import tpu as pltpu
from jax.sharding import PartitionSpec as P

OMEGA = 0.6
SHIFT = 0.5
F32 = jnp.float32


def lroll(v, shift):
    return pltpu.roll(v, shift % v.shape[1], 1)


def sroll(v, shift):
    return pltpu.roll(v, shift % v.shape[0], 0)


def lanes(rows):
    return lax.broadcasted_iota(jnp.int32, (rows, 128), 1)


def sublanes(rows):
    return lax.broadcasted_iota(jnp.int32, (rows, 128), 0)


def row_mask(rows, first, count):
    place = sublanes(rows) + first
    return jnp.where((place >= 0) & (place < count), F32(1), F32(0))


def scalar_mask(place, count):
    return jnp.where((place >= 0) & (place < count), F32(1), F32(0))


def z_pair(v, lane, step):
    low = jnp.where(lane >= step, lroll(v, step), 0.0)
    high = jnp.where(lane < 128 - step, lroll(v, -step), 0.0)
    return low, high


def z_sum(v, lane, step):
    low, high = z_pair(v, lane, step)
    return low + high


def y_sum(v):
    return sroll(v, 1) + sroll(v, -1)


def inverse(w, scale, keep):
    real = 6.0 * scale - w
    imag = SHIFT * w
    factor = (OMEGA * keep) / (real * real + imag * imag)
    return real * factor, -imag * factor


def misfit(f, w, v, nb, scale):
    (fr, fi), (vr, vi), (nr, ni) = f, v, nb
    mr = fr - scale * (6.0 * vr - nr) + w * (vr + SHIFT * vi)
    mi = fi - scale * (6.0 * vi - ni) + w * (vi - SHIFT * vr)
    return mr, mi


def cmul(g, m):
    return g[0] * m[0] - g[1] * m[1], g[0] * m[1] + g[1] * m[0]


def repeat(low, high, step, unroll=1):
    def run(i, carry):
        step(i)
        return carry

    lax.fori_loop(low, high, run, 0, unroll=unroll)


class Window:
    def __init__(self, src, gain, scale, pad, neighbours):
        self.src, self.gain, self.scale, self.pad = src, gain, scale, pad
        self.neighbours = neighbours

    def start(self, row, keep, out):
        w = self.src[2, row]
        g = inverse(w, self.scale, keep)
        self.gain[0, row], self.gain[1, row] = g
        u = cmul(g, (self.src[0, row], self.src[1, row]))
        out[0, row + self.pad], out[1, row + self.pad] = u

    def misfit(self, row, field):
        at = row + self.pad
        v = (field[0, at], field[1, at])
        nb = tuple(self.neighbours(field, c, at, v[c]) for c in range(2))
        f = (self.src[0, row], self.src[1, row])
        return v, misfit(f, self.src[2, row], v, nb, self.scale)

    def relaxed(self, row, field):
        v, m = self.misfit(row, field)
        d = cmul((self.gain[0, row], self.gain[1, row]), m)
        return v[0] + d[0], v[1] + d[1]

    def relax(self, row, field, out):
        at = row + self.pad
        out[0, at], out[1, at] = self.relaxed(row, field)


def near0(lane, ref, c, at, v):
    return ref[c, at - 1] + ref[c, at + 1] + y_sum(v) + z_sum(v, lane, 1)


def near1(lane, ref, c, at, v):
    low = lroll(ref[c, at - 1] + v, -1)
    high = lroll(v + ref[c, at + 1], 1)
    return jnp.where(lane % 2 == 0, low, high) + y_sum(v) + z_sum(v, lane, 2)


def near2(lane, ref, c, at, v):
    slot = lane % 4
    low = jnp.where(slot == 0, lroll(ref[c, at - 1], -3), lroll(v, 1))
    high = jnp.where(slot == 3, lroll(ref[c, at + 1], 3), lroll(v, -1))
    return low + high + y_sum(v) + z_sum(v, lane, 4)


def level0(src, gain, first, ix, iy):
    lane = lanes(24)
    win = Window(src, gain, 1.0, 0, functools.partial(near0, lane))
    inside = row_mask(24, iy * 16 - 3, 256)
    repeat(0, 22, lambda x: win.start(x, inside * scalar_mask(ix * 16 - 3 + x, 256), first), 2)
    return win, inside


def down0_kernel(idx, src, out, gain, ub, ua, tmp):
    ix, iy = idx[0], idx[1]
    win, _ = level0(src, gain, ua, ix, iy)
    repeat(1, 21, lambda x: win.relax(x, ua, ub), 4)
    for c in range(2):
        for x in (0, 21):
            ub[c, x] = jnp.zeros((24, 128), F32)
    lane = lanes(8)
    even = lane % 2 == 0

    def halve(q):
        rows = []
        for half in range(2):
            x = 4 * q + 3 + 2 * half
            _, m0 = win.misfit(x, ub)
            _, m1 = win.misfit(x + 1, ub)
            parts = (m0[0] + m1[0], m0[1] + m1[1], src[2, x] + src[2, x + 1])
            got = []
            for c in range(3):
                tmp[c, 2 * q + half] = parts[c]
                t = tmp[c, 2 * q + half, pl.ds(3, 8, 2)] + tmp[c, 2 * q + half, pl.ds(4, 8, 2)]
                got.append(0.125 * (t + lroll(t, -1)))
            rows.append(got)
        for c in range(3):
            out[c, q] = jnp.where(even, rows[0][c], lroll(rows[1][c], 1))

    repeat(0, 4, halve)


def down1_kernel(idx, src, out, src2, gain, ub, ua, tmp, gain2, va, vb):
    ix, iy = idx[0], idx[1]
    lane24 = lanes(24)
    zero24 = jnp.zeros((24, 128), F32)
    for buf in (ua, ub):
        for c in range(2):
            buf[c, 0] = zero24
            buf[c, 13] = zero24
    win = Window(src, gain, 0.25, 1, functools.partial(near1, lane24))
    inside = row_mask(24, iy * 8 - 8, 128)
    repeat(0, 12, lambda q: win.start(q, inside * scalar_mask(ix * 4 - 4 + q, 64), ua), 4)
    repeat(0, 12, lambda q: win.relax(q, ua, ub), 4)
    lane = lanes(16)
    corner = lane % 4 == 0

    def halve(b):
        for j in range(4):
            q = 4 * b + j
            _, m = win.misfit(q, ub)
            parts = (m[0], m[1], src[2, q])
            for c in range(3):
                t = parts[c] + lroll(parts[c], -1)
                tmp[c, q, pl.ds(0, 24), :] = t + lroll(t, -2)
                tmp[c, q, pl.ds(24, 8), :] = jnp.zeros((8, 128), F32)
        for c in range(3):
            packed = jnp.zeros((16, 128), F32)
            for j in range(4):
                q = 4 * b + j
                t = tmp[c, q, pl.ds(0, 16, 2), :] + tmp[c, q, pl.ds(1, 16, 2), :]
                t = jnp.where(corner, 0.125 * t, 0.0)
                packed = packed + (lroll(t, j) if j else t)
            src2[c, b] = packed

    repeat(0, 3, halve)
    for buf in (va, vb):
        for c in range(2):
            buf[c, 0] = jnp.zeros((16, 128), F32)
            buf[c, 4] = jnp.zeros((16, 128), F32)
    win2 = Window(src2, gain2, 0.0625, 1, functools.partial(near2, lane))
    inside2 = row_mask(16, iy * 4 - 4, 64)
    for b in range(3):
        win2.start(b, inside2 * scalar_mask(ix - 1 + b, 16), va)
    for b in range(3):
        win2.relax(b, va, vb)
    _, m = win2.misfit(1, vb)

    def third(v):
        t = v + lroll(v, -1)
        t = t + lroll(t, -4)
        t = 0.125 * jnp.where((lane % 2 == 0) & (lane % 8 < 4), t + sroll(t, -1), 0.0)
        return t[4:5] + lroll(t[6:7], 1)

    field = third(m[0]) + lroll(third(m[1]), 4)
    wave = third(src2[2, 1])
    wave = wave + lroll(wave, 4)
    pair = jnp.concatenate([field, wave] * 4, axis=0)

    def spread(i):
        out[i] = pair

    repeat(0, 64, spread, 8)


def swap(v, real):
    return jnp.where(real, lroll(v, -4), lroll(v, 4))


def up_kernel(
    idx, src0, gain0, ub0, src1, gain1, ub1, src2, flat, out,
    f3, w3, ga3, gb3, ua3, ub3, f4, w4, s4, e3, gain2, u2, wide2, cell1, ua1, ut1, wide1, wide0, ua0, ut0,
):
    ix, iy = idx[0], idx[1]
    lane = lanes(16)
    real = lane // 4 % 2 == 0
    sign = jnp.where(real, F32(SHIFT), F32(-SHIFT))
    xlow = lane // 2 % 2 == 0
    ylow = lane % 2 == 0
    zlow = lane // 8 % 2 == 0
    slot = lane % 4
    row = sublanes(16)
    zero16 = jnp.zeros((16, 128), F32)

    def y_pair(v):
        return jnp.where(row >= 1, sroll(v, 1), 0.0), jnp.where(row < 15, sroll(v, -1), 0.0)

    def packed_gain(w, scale):
        gr, gi = inverse(w, scale, 1.0)
        return gr, jnp.where(real, -gi, gi)

    def packed_misfit(f, w, v, nb, scale):
        return f - scale * (6.0 * v - nb) + w * (v + sign * swap(v, real))

    for at in (0, 1, 2, 19, 20, 21):
        for ref in (f3, w3, ga3, gb3):
            ref[at] = zero16
        for ref in (ua3, ub3):
            ref[at] = zero16
    for j in range(7):
        e3[j] = jnp.zeros((32, 128), F32)

    def start3(x):
        at = x + 3
        f3[at] = flat[pl.ds(32 * x, 16, 2), :]
        w = flat[pl.ds(32 * x + 1, 16, 2), :]
        w3[at] = w
        ga, gb = packed_gain(w, 1.0 / 64)
        ga3[at], gb3[at] = ga, gb
        ua3[at] = ga * f3[at] + gb * swap(f3[at], real)

    def miss3(ref, at):
        v = ref[at]
        down, up = y_pair(v)
        xs = jnp.where(xlow, lroll(ref[at - 1] + v, -2), lroll(v + ref[at + 1], 2))
        ys = jnp.where(ylow, lroll(v + down, -1), lroll(v + up, 1))
        return v, packed_misfit(f3[at], w3[at], v, xs + ys + z_sum(v, lane, 8), 1.0 / 64)

    def relaxed3(ref, at):
        v, m = miss3(ref, at)
        return v + ga3[at] * m + gb3[at] * swap(m, real)

    def relax3(at):
        ub3[at] = relaxed3(ua3, at)

    repeat(0, 16, start3, 8)
    repeat(3, 19, relax3, 8)

    first = (slot == 0) & zlow

    def eighth(v):
        v = v + lroll(v, -1)
        v = v + lroll(v, -2)
        return jnp.where(first, 0.125 * (v + lroll(v, -8)), 0.0)

    def halve3(r):
        f, w = zero16, zero16
        for k in range(4):
            at = 4 * k + r + 3
            fk, wk = eighth(miss3(ub3, at)[1]), eighth(w3[at])
            f = f + (lroll(fk, k) if k else fk)
            w = w + (lroll(wk, k) if k else wk)
        f4[r], w4[r] = f, w

    repeat(0, 4, halve3, 2)
    fs = [f4[r] for r in range(4)]
    ws = [w4[r] for r in range(4)]
    gs = [packed_gain(w, 1.0 / 256) for w in ws]

    def miss4(us):
        low = jnp.where(slot >= 1, lroll(us[3], 1), 0.0)
        high = jnp.where(slot < 3, lroll(us[0], -1), 0.0)
        wide = [low, *us, high]
        ms = []
        for r in range(4):
            down, up = y_pair(us[r])
            nb = wide[r] + wide[r + 2] + down + up + z_sum(us[r], lane, 16)
            ms.append(packed_misfit(fs[r], ws[r], us[r], nb, 1.0 / 256))
        return ms

    def relax4(_, us):
        ms = miss4(us)
        return tuple(u + g[0] * m + g[1] * swap(m, real) for u, g, m in zip(us, gs, ms))

    us = tuple(g[0] * f + g[1] * swap(f, real) for g, f in zip(gs, fs))
    us = lax.fori_loop(0, 5, relax4, us)
    ms = miss4(us)
    total_m = ms[0] + ms[1] + ms[2] + ms[3]
    total_w = ws[0] + ws[1] + ws[2] + ws[3]
    sum_r = jnp.sum(jnp.where(zlow & real, total_m, 0.0))
    sum_i = jnp.sum(jnp.where(zlow & ~real, total_m, 0.0))
    sum_w = jnp.sum(jnp.where(zlow & real, total_w, 0.0))
    numer = jnp.where(real, sum_r - SHIFT * sum_i, sum_i + SHIFT * sum_r)
    const = -numer / (jnp.full((16, 128), (1.0 + SHIFT * SHIFT), F32) * sum_w)
    for r in range(4):
        s4[r] = jnp.where(zlow, us[r] + const, 0.0)

    def spread4(j):
        x = ix - 4 + j
        inside = (x >= 0) & (x < 16)
        x = jnp.clip(x, 0, 15)
        k = x // 4
        t = jnp.where((slot == k) & inside, s4[x - 4 * k], 0.0)
        t = pltpu.roll(t, lax.rem(128 - k, 128), 1)
        t = t + lroll(t, 1)
        t = t + lroll(t, 2)
        t = t + lroll(t, 8)
        low, high = z_pair(t, lane, 16)
        t = 0.75 * t + 0.25 * jnp.where(zlow, low, high)
        down, up = y_pair(t)
        return 0.75 * t + 0.25 * jnp.where(ylow, down, up)

    wide = [spread4(j) for j in range(9)]
    for j in range(7):
        at = ix + j
        fix = 0.75 * wide[j + 1] + 0.25 * jnp.where(xlow, wide[j], wide[j + 2])
        fix = jnp.where((at >= 3) & (at < 19), fix, 0.0)
        ub3[at] = ub3[at] + fix

    def sweep3(_):
        new = [relaxed3(ub3, ix + j) for j in range(1, 6)]
        for j in range(1, 6):
            ub3[ix + j] = new[j - 1]

    repeat(0, 2, sweep3)
    for j in range(1, 6):
        e3[j, pl.ds(8, 16), :] = ub3[ix + j]

    lane8 = lanes(8)
    lane24 = lanes(24)
    zero24 = jnp.zeros((24, 128), F32)
    for c in range(2):
        u2[c, 0] = zero24
        u2[c, 6] = zero24
    win2 = Window(src2, gain2, 0.0625, 1, functools.partial(near2, lane24))
    inside2 = row_mask(24, iy * 4 - 8, 64)
    keep2 = [inside2 * scalar_mask(ix - 2 + b, 16) for b in range(5)]
    for b in range(5):
        win2.start(b, keep2[b], u2)
    a_low = lane8 % 2 == 0
    b_low = lane8 // 4 % 2 == 0
    x_low = lane8 // 2 % 2 == 0

    def widen3(c):
        sides = []
        shift = jnp.where(c == 0, 4, 124)
        for yl in range(2):
            pick = (lane8 // 4 % 2 == c) & (lane8 % 2 == yl)
            cells = []
            for bb in range(7):
                t = jnp.where(pick, e3[bb, pl.ds(iy + 5, 8), :], 0.0)
                t = t + lroll(t, 1 - 2 * yl)
                t = t + pltpu.roll(t, shift, 1)
                low, high = z_pair(t, lane8, 8)
                cells.append(0.75 * t + 0.25 * jnp.where(b_low, low, high))
            blocks = []
            for b in range(1, 6):
                low = lroll(jnp.where(a_low, cells[b - 1], cells[b]), -2)
                high = lroll(jnp.where(a_low, cells[b], cells[b + 1]), 2)
                blocks.append(0.75 * cells[b] + 0.25 * jnp.where(x_low, low, high))
            sides.append(blocks)
        for b in range(5):
            t0, t1 = sides[0][b], sides[1][b]
            wide2[c, b, pl.ds(0, 8, 4), :] = 0.75 * t0 + 0.25 * sroll(t1, 1)
            wide2[c, b, pl.ds(1, 8, 4), :] = 0.75 * t0 + 0.25 * t1
            wide2[c, b, pl.ds(2, 8, 4), :] = 0.75 * t1 + 0.25 * t0
            wide2[c, b, pl.ds(3, 8, 4), :] = 0.75 * t1 + 0.25 * sroll(t0, -1)

    repeat(0, 2, widen3)

    def sweep2(i):
        add = jnp.where(i == 0, F32(1), F32(0))
        new = [win2.relaxed(b, u2) for b in range(5)]
        for b in range(5):
            for c in range(2):
                fix = wide2[c, b, pl.ds(4, 24), :] * (keep2[b] * add)
                u2[c, b + 1] = new[b][c] + fix

    repeat(0, 3, sweep2)

    lane16 = lanes(16)
    slot4 = lane16 % 4

    def widen2(b):
        for xl in range(4):
            for c in range(2):
                t = jnp.where(slot4 == xl, u2[c, b + 1, pl.ds(4, 16), :], 0.0)
                t = lroll(t, -xl) if xl else t
                t = t + lroll(t, 1)
                t = t + lroll(t, 2)
                low, high = z_pair(t, lane16, 4)
                cell1[c, 4 * b - 4 + xl] = 0.75 * t + 0.25 * jnp.where(slot4 < 2, low, high)

    repeat(1, 4, widen2)
    lane_even = lane16 % 2 == 0

    def mix2(q):
        for c in range(2):
            side = jnp.where(lane_even, cell1[c, q - 1], cell1[c, q + 1])
            t = 0.75 * cell1[c, q] + 0.25 * side
            wide1[c, q, pl.ds(0, 16, 2), :] = 0.75 * t + 0.25 * sroll(t, 1)
            wide1[c, q, pl.ds(1, 16, 2), :] = 0.75 * t + 0.25 * sroll(t, -1)

    repeat(2, 10, mix2, 4)
    for c in range(2):
        ua1[c, 2] = zero24
        ua1[c, 11] = zero24
    inside1 = row_mask(24, iy * 8 - 8, 128)

    def correct1(q):
        keep = inside1 * scalar_mask(ix * 4 - 4 + q, 64)
        for c in range(2):
            ua1[c, q + 1] = ub1[c, q + 1] + wide1[c, q, pl.ds(0, 24), :] * keep

    repeat(2, 10, correct1, 4)
    win1 = Window(src1, gain1, 0.25, 1, functools.partial(near1, lane24))

    repeat(2, 10, lambda q: win1.relax(q, ua1, ut1), 4)
    repeat(3, 9, lambda q: win1.relax(q, ut1, ua1), 3)

    def widen1(q):
        for c in range(2):
            t = ua1[c, q + 1, pl.ds(5, 16), :]
            up, down = lroll(t, 1), lroll(t, -1)
            for p in range(2):
                v = jnp.where(lane_even, t, up) if p == 0 else jnp.where(lane_even, down, t)
                low, high = z_pair(v, lane16, 2)
                v = 0.75 * v + 0.25 * jnp.where(lane_even, low, high)
                wide0[c, 2 * q - 2 + p, pl.ds(0, 16, 2), :] = 0.75 * v + 0.25 * sroll(v, 1)
                wide0[c, 2 * q - 2 + p, pl.ds(1, 16, 2), :] = 0.75 * v + 0.25 * sroll(v, -1)

    repeat(3, 9, widen1, 2)
    inside0 = row_mask(24, iy * 16 - 3, 256)

    def correct0(at):
        for c in range(2):
            low = wide0[c, at - 1, pl.ds(3, 24), :]
            mid = wide0[c, at, pl.ds(3, 24), :]
            high = wide0[c, at + 1, pl.ds(3, 24), :]
            for child, side in ((0, low), (1, high)):
                x = 2 * at - 9 + child
                keep = inside0 * scalar_mask(ix * 16 - 3 + x, 256)
                ua0[c, x] = ub0[c, x] + (0.75 * mid + 0.25 * side) * keep

    repeat(5, 15, correct0, 2)
    win0 = Window(src0, gain0, 1.0, 0, functools.partial(near0, lane24))
    repeat(2, 20, lambda x: win0.relax(x, ua0, ut0), 3)

    def finish0(x):
        new = win0.relaxed(x + 3, ut0)
        for c in range(2):
            ua0[c, x + 3] = new[c]
            out[c, x] = ua0[c, x + 3, pl.ds(3, 16), :]

    repeat(0, 16, finish0, 4)


def call(kernel, name, out_shape, scratch, *args):
    vmem = pl.BlockSpec(memory_space=pltpu.VMEM)
    return pl.pallas_call(
        kernel,
        name=name,
        out_shape=[jax.ShapeDtypeStruct(shape, F32) for shape in out_shape],
        in_specs=[pl.BlockSpec(memory_space=pltpu.SMEM)] + [vmem] * (len(args) - 1),
        out_specs=[vmem] * len(out_shape),
        scratch_shapes=[pltpu.VMEM(shape, F32) for shape in scratch],
        compiler_params=pltpu.CompilerParams(vmem_limit_bytes=40 * 1024 * 1024),
    )(*args)


BOTH = ("gx", "gy")


def partners(axis, first):
    counts = [lax.axis_size(name) for name in BOTH]
    along = BOTH.index(axis)
    pairs = []
    for i in range(counts[0]):
        for j in range(counts[1]):
            place = [i, j]
            other = ((place[along] + first) ^ 1) - first
            if 0 <= other < counts[along]:
                place[along] = other
            else:
                place[1 - along] ^= 1
            pairs.append((i * counts[1] + j, place[0] * counts[1] + place[1]))
    return pairs


def trade(to_low, to_high, axis):
    even = lax.axis_index(axis) % 2 == 0
    if to_low is to_high:
        one = two = to_low
    else:
        one = jnp.where(even, to_high, to_low)
        two = jnp.where(even, to_low, to_high)
    one = lax.ppermute(one, BOTH, partners(axis, 0))
    two = lax.ppermute(two, BOTH, partners(axis, 1))
    return jnp.where(even, two, one), jnp.where(even, one, two)


def body(residual_in, wave_sq):
    ix = lax.axis_index("gx")
    iy = lax.axis_index("gy")
    idx = jnp.stack([ix, iy]).astype(jnp.int32)

    own = jnp.concatenate([residual_in, wave_sq[None]], axis=0)
    low, high = trade(own[:, :3], own[:, 13:], "gx")
    strip = jnp.concatenate([low, own, high], axis=1)
    low, high = trade(
        strip[:, :, :3].transpose(0, 2, 1, 3).reshape(9, 22, 128),
        strip[:, :, 13:].transpose(0, 2, 1, 3).reshape(9, 22, 128),
        "gy",
    )
    low = low.reshape(3, 3, 22, 128).transpose(0, 2, 1, 3)
    high = high.reshape(3, 3, 22, 128).transpose(0, 2, 1, 3)
    src0 = jnp.concatenate([low, strip, high, jnp.zeros((3, 22, 2, 128), F32)], axis=2)

    n0 = (2, 22, 24, 128)
    n1 = (2, 14, 24, 128)
    own1, gain0, first0 = call(
        down0_kernel, "down0", [(3, 4, 8, 128), n0, n0], [n0, (3, 8, 24, 128)], idx, src0
    )
    low, high = trade(own1, own1, "gx")
    strip = jnp.concatenate([low, own1, high], axis=1)
    low, high = trade(strip, strip, "gy")
    src1 = jnp.concatenate([low, strip, high], axis=2)

    part, own2, gain1, first1 = call(
        down1_kernel,
        "down1",
        [(64, 8, 128), (3, 3, 16, 128), (2, 12, 24, 128), n1],
        [n1, (3, 12, 32, 128), (2, 3, 16, 128), (2, 5, 16, 128), (2, 5, 16, 128)],
        idx,
        src1,
    )
    part = part.reshape(256, 2, 128)
    flat = lax.all_to_all(part, ("gx", "gy"), 0, 0).reshape(512, 128)
    low, high = trade(own2[:, 1:], own2[:, :2], "gx")
    strip = jnp.concatenate([low, own2[:, 1:2], high], axis=1)
    low, high = trade(strip[:, :, 4:12], strip[:, :, :8], "gy")
    src2 = jnp.concatenate(
        [low, strip[:, :, 4:8], high, jnp.zeros((3, 5, 4, 128), F32)], axis=2
    )

    wide = (22, 16, 128)
    return call(
        up_kernel,
        "up",
        [(2, 16, 16, 128)],
        [wide, wide, wide, wide, wide, wide]
        + [(4, 16, 128), (4, 16, 128), (4, 16, 128), (7, 32, 128)]
        + [(2, 5, 24, 128), (2, 7, 24, 128), (2, 5, 32, 128)]
        + [(2, 12, 16, 128), n1, n1, (2, 12, 32, 128), (2, 16, 32, 128), n0, n0],
        idx,
        src0,
        gain0,
        first0,
        src1,
        gain1,
        first1,
        src2,
        flat,
    )[0]


def solution(mesh):
    placed = (P(None, "gx", "gy", None), P("gx", "gy", None))
    return jax.shard_map(
        body, mesh=mesh, in_specs=placed, out_specs=P(None, "gx", "gy", None), check_vma=False
    )
```

```python
import functools

import jax
import jax.numpy as jnp
from jax import lax
from jax.experimental import pallas as pl
from jax.experimental.pallas import tpu as pltpu
from jax.sharding import PartitionSpec as P

OMEGA = 0.6
SHIFT = 0.5
F32 = jnp.float32


def lroll(v, shift):
    return pltpu.roll(v, shift % v.shape[1], 1)


def sroll(v, shift):
    return pltpu.roll(v, shift % v.shape[0], 0)


def lanes(rows):
    return lax.broadcasted_iota(jnp.int32, (rows, 128), 1)


def sublanes(rows):
    return lax.broadcasted_iota(jnp.int32, (rows, 128), 0)


def row_mask(rows, first, count):
    place = sublanes(rows) + first
    return jnp.where((place >= 0) & (place < count), F32(1), F32(0))


def scalar_mask(place, count):
    return jnp.where((place >= 0) & (place < count), F32(1), F32(0))


def z_pair(v, lane, step):
    low = jnp.where(lane >= step, lroll(v, step), 0.0)
    high = jnp.where(lane < 128 - step, lroll(v, -step), 0.0)
    return low, high


def z_sum(v, lane, step):
    low, high = z_pair(v, lane, step)
    return low + high


def y_sum(v):
    return sroll(v, 1) + sroll(v, -1)


def inverse(w, scale, keep):
    real = 6.0 * scale - w
    imag = SHIFT * w
    factor = (OMEGA * keep) / (real * real + imag * imag)
    return real * factor, -imag * factor


def misfit(f, w, v, nb, scale):
    (fr, fi), (vr, vi), (nr, ni) = f, v, nb
    mr = fr - scale * (6.0 * vr - nr) + w * (vr + SHIFT * vi)
    mi = fi - scale * (6.0 * vi - ni) + w * (vi - SHIFT * vr)
    return mr, mi


def cmul(g, m):
    return g[0] * m[0] - g[1] * m[1], g[0] * m[1] + g[1] * m[0]


def repeat(low, high, step, unroll=1):
    def run(i, carry):
        step(i)
        return carry

    lax.fori_loop(low, high, run, 0, unroll=unroll)


class Window:
    def __init__(self, src, gain, scale, pad, neighbours):
        self.src, self.gain, self.scale, self.pad = src, gain, scale, pad
        self.neighbours = neighbours

    def start(self, row, keep, out):
        w = self.src[2, row]
        g = inverse(w, self.scale, keep)
        self.gain[0, row], self.gain[1, row] = g
        u = cmul(g, (self.src[0, row], self.src[1, row]))
        out[0, row + self.pad], out[1, row + self.pad] = u

    def misfit(self, row, field):
        at = row + self.pad
        v = (field[0, at], field[1, at])
        nb = tuple(self.neighbours(field, c, at, v[c]) for c in range(2))
        f = (self.src[0, row], self.src[1, row])
        return v, misfit(f, self.src[2, row], v, nb, self.scale)

    def relaxed(self, row, field):
        v, m = self.misfit(row, field)
        d = cmul((self.gain[0, row], self.gain[1, row]), m)
        return v[0] + d[0], v[1] + d[1]

    def relax(self, row, field, out):
        at = row + self.pad
        out[0, at], out[1, at] = self.relaxed(row, field)


def near0(lane, ref, c, at, v):
    return ref[c, at - 1] + ref[c, at + 1] + y_sum(v) + z_sum(v, lane, 1)


def near1(lane, ref, c, at, v):
    low = lroll(ref[c, at - 1] + v, -1)
    high = lroll(v + ref[c, at + 1], 1)
    return jnp.where(lane % 2 == 0, low, high) + y_sum(v) + z_sum(v, lane, 2)


def near2(lane, ref, c, at, v):
    slot = lane % 4
    low = jnp.where(slot == 0, lroll(ref[c, at - 1], -3), lroll(v, 1))
    high = jnp.where(slot == 3, lroll(ref[c, at + 1], 3), lroll(v, -1))
    return low + high + y_sum(v) + z_sum(v, lane, 4)


def level0(src, gain, first, ix, iy):
    lane = lanes(24)
    win = Window(src, gain, 1.0, 0, functools.partial(near0, lane))
    inside = row_mask(24, iy * 16 - 3, 256)
    repeat(0, 22, lambda x: win.start(x, inside * scalar_mask(ix * 16 - 3 + x, 256), first), 2)
    return win, inside


def down0_kernel(idx, src, out, gain, ub, ua, tmp):
    ix, iy = idx[0], idx[1]
    win, _ = level0(src, gain, ua, ix, iy)
    repeat(1, 21, lambda x: win.relax(x, ua, ub), 4)
    for c in range(2):
        for x in (0, 21):
            ub[c, x] = jnp.zeros((24, 128), F32)
    lane = lanes(8)
    even = lane % 2 == 0

    def halve(q):
        rows = []
        for half in range(2):
            x = 4 * q + 3 + 2 * half
            _, m0 = win.misfit(x, ub)
            _, m1 = win.misfit(x + 1, ub)
            parts = (m0[0] + m1[0], m0[1] + m1[1], src[2, x] + src[2, x + 1])
            got = []
            for c in range(3):
                tmp[c, 2 * q + half] = parts[c]
                t = tmp[c, 2 * q + half, pl.ds(3, 8, 2)] + tmp[c, 2 * q + half, pl.ds(4, 8, 2)]
                got.append(0.125 * (t + lroll(t, -1)))
            rows.append(got)
        for c in range(3):
            out[c, q] = jnp.where(even, rows[0][c], lroll(rows[1][c], 1))

    repeat(0, 4, halve)


def down1_kernel(idx, src, out, src2, gain, ub, ua, tmp, gain2, va, vb):
    ix, iy = idx[0], idx[1]
    lane24 = lanes(24)
    zero24 = jnp.zeros((24, 128), F32)
    for buf in (ua, ub):
        for c in range(2):
            buf[c, 0] = zero24
            buf[c, 11] = zero24
    win = Window(src, gain, 0.25, 1, functools.partial(near1, lane24))
    inside = row_mask(24, iy * 8 - 8, 128)
    repeat(0, 10, lambda q: win.start(q, inside * scalar_mask(ix * 4 - 3 + q, 64), ua), 5)
    repeat(0, 10, lambda q: win.relax(q, ua, ub), 5)
    lane = lanes(16)
    corner = lane % 4 == 0

    def halve(q):
        _, m = win.misfit(q, ub)
        parts = (m[0], m[1], src[2, q])
        for c in range(3):
            t = parts[c] + lroll(parts[c], -1)
            tmp[c, q, pl.ds(0, 24), :] = t + lroll(t, -2)
            tmp[c, q, pl.ds(24, 8), :] = jnp.zeros((8, 128), F32)

    repeat(1, 9, halve, 4)

    def cell(c, q):
        t = tmp[c, q, pl.ds(0, 16, 2), :] + tmp[c, q, pl.ds(1, 16, 2), :]
        return jnp.where(corner, 0.125 * t, 0.0)

    for c in range(3):
        src2[c, 0] = lroll(cell(c, 1), 2) + lroll(cell(c, 2), 3)
        src2[c, 1] = sum((lroll(cell(c, 3 + j), j) for j in range(1, 4)), cell(c, 3))
        src2[c, 2] = cell(c, 7) + lroll(cell(c, 8), 1)
    for buf in (va, vb):
        for c in range(2):
            buf[c, 0] = jnp.zeros((16, 128), F32)
            buf[c, 4] = jnp.zeros((16, 128), F32)
    win2 = Window(src2, gain2, 0.0625, 1, functools.partial(near2, lane))
    inside2 = row_mask(16, iy * 4 - 4, 64)
    for b in range(3):
        win2.start(b, inside2 * scalar_mask(ix - 1 + b, 16), va)
    for b in range(3):
        win2.relax(b, va, vb)
    _, m = win2.misfit(1, vb)

    def third(v):
        t = v + lroll(v, -1)
        t = t + lroll(t, -4)
        t = 0.125 * jnp.where((lane % 2 == 0) & (lane % 8 < 4), t + sroll(t, -1), 0.0)
        return t[4:5] + lroll(t[6:7], 1)

    field = third(m[0]) + lroll(third(m[1]), 4)
    wave = third(src2[2, 1])
    wave = wave + lroll(wave, 4)
    pair = jnp.concatenate([field, wave] * 4, axis=0)

    def spread(i):
        out[i] = pair

    repeat(0, 64, spread, 8)


def swap(v, real):
    return jnp.where(real, lroll(v, -4), lroll(v, 4))


def coarse_kernel(idx, flat, out, f3, w3, ga3, gb3, ua3, ub3, f4, w4, s4, e3):
    ix, iy = idx[0], idx[1]
    lane = lanes(16)
    real = lane // 4 % 2 == 0
    sign = jnp.where(real, F32(SHIFT), F32(-SHIFT))
    xlow = lane // 2 % 2 == 0
    ylow = lane % 2 == 0
    zlow = lane // 8 % 2 == 0
    slot = lane % 4
    row = sublanes(16)
    zero16 = jnp.zeros((16, 128), F32)

    def y_pair(v):
        return jnp.where(row >= 1, sroll(v, 1), 0.0), jnp.where(row < 15, sroll(v, -1), 0.0)

    def packed_gain(w, scale):
        gr, gi = inverse(w, scale, 1.0)
        return gr, jnp.where(real, -gi, gi)

    def packed_misfit(f, w, v, nb, scale):
        return f - scale * (6.0 * v - nb) + w * (v + sign * swap(v, real))

    for at in (0, 1, 2, 19, 20, 21):
        for ref in (f3, w3, ga3, gb3):
            ref[at] = zero16
        for ref in (ua3, ub3):
            ref[at] = zero16
    for j in range(7):
        e3[j] = jnp.zeros((32, 128), F32)

    def start3(x):
        at = x + 3
        f3[at] = flat[pl.ds(32 * x, 16, 2), :]
        w = flat[pl.ds(32 * x + 1, 16, 2), :]
        w3[at] = w
        ga, gb = packed_gain(w, 1.0 / 64)
        ga3[at], gb3[at] = ga, gb
        ua3[at] = ga * f3[at] + gb * swap(f3[at], real)

    def miss3(ref, at):
        v = ref[at]
        down, up = y_pair(v)
        xs = jnp.where(xlow, lroll(ref[at - 1] + v, -2), lroll(v + ref[at + 1], 2))
        ys = jnp.where(ylow, lroll(v + down, -1), lroll(v + up, 1))
        return v, packed_misfit(f3[at], w3[at], v, xs + ys + z_sum(v, lane, 8), 1.0 / 64)

    def relaxed3(ref, at):
        v, m = miss3(ref, at)
        return v + ga3[at] * m + gb3[at] * swap(m, real)

    def relax3(at):
        ub3[at] = relaxed3(ua3, at)

    repeat(0, 16, start3, 8)
    repeat(3, 19, relax3, 8)

    first = (slot == 0) & zlow

    def eighth(v):
        v = v + lroll(v, -1)
        v = v + lroll(v, -2)
        return jnp.where(first, 0.125 * (v + lroll(v, -8)), 0.0)

    def halve3(r):
        f, w = zero16, zero16
        for k in range(4):
            at = 4 * k + r + 3
            fk, wk = eighth(miss3(ub3, at)[1]), eighth(w3[at])
            f = f + (lroll(fk, k) if k else fk)
            w = w + (lroll(wk, k) if k else wk)
        f4[r], w4[r] = f, w

    repeat(0, 4, halve3, 2)
    fs = [f4[r] for r in range(4)]
    ws = [w4[r] for r in range(4)]
    gs = [packed_gain(w, 1.0 / 256) for w in ws]

    def miss4(us):
        low = jnp.where(slot >= 1, lroll(us[3], 1), 0.0)
        high = jnp.where(slot < 3, lroll(us[0], -1), 0.0)
        wide = [low, *us, high]
        ms = []
        for r in range(4):
            down, up = y_pair(us[r])
            nb = wide[r] + wide[r + 2] + down + up + z_sum(us[r], lane, 16)
            ms.append(packed_misfit(fs[r], ws[r], us[r], nb, 1.0 / 256))
        return ms

    def relax4(_, us):
        ms = miss4(us)
        return tuple(u + g[0] * m + g[1] * swap(m, real) for u, g, m in zip(us, gs, ms))

    us = tuple(g[0] * f + g[1] * swap(f, real) for g, f in zip(gs, fs))
    us = lax.fori_loop(0, 5, relax4, us)
    ms = miss4(us)
    total_m = ms[0] + ms[1] + ms[2] + ms[3]
    total_w = ws[0] + ws[1] + ws[2] + ws[3]
    sum_r = jnp.sum(jnp.where(zlow & real, total_m, 0.0))
    sum_i = jnp.sum(jnp.where(zlow & ~real, total_m, 0.0))
    sum_w = jnp.sum(jnp.where(zlow & real, total_w, 0.0))
    numer = jnp.where(real, sum_r - SHIFT * sum_i, sum_i + SHIFT * sum_r)
    const = -numer / (jnp.full((16, 128), (1.0 + SHIFT * SHIFT), F32) * sum_w)
    for r in range(4):
        s4[r] = jnp.where(zlow, us[r] + const, 0.0)

    def spread4(j):
        x = ix - 4 + j
        inside = (x >= 0) & (x < 16)
        x = jnp.clip(x, 0, 15)
        k = x // 4
        t = jnp.where((slot == k) & inside, s4[x - 4 * k], 0.0)
        t = pltpu.roll(t, lax.rem(128 - k, 128), 1)
        t = t + lroll(t, 1)
        t = t + lroll(t, 2)
        t = t + lroll(t, 8)
        low, high = z_pair(t, lane, 16)
        t = 0.75 * t + 0.25 * jnp.where(zlow, low, high)
        down, up = y_pair(t)
        return 0.75 * t + 0.25 * jnp.where(ylow, down, up)

    wide = [spread4(j) for j in range(9)]
    for j in range(7):
        at = ix + j
        fix = 0.75 * wide[j + 1] + 0.25 * jnp.where(xlow, wide[j], wide[j + 2])
        fix = jnp.where((at >= 3) & (at < 19), fix, 0.0)
        ub3[at] = ub3[at] + fix

    def sweep3(_):
        new = [relaxed3(ub3, ix + j) for j in range(1, 6)]
        for j in range(1, 6):
            ub3[ix + j] = new[j - 1]

    repeat(0, 2, sweep3)
    for j in range(1, 6):
        e3[j, pl.ds(8, 16), :] = ub3[ix + j]

    for j in range(7):
        out[j] = e3[j, pl.ds(iy + 5, 8), :]


def up_kernel(
    idx, src0, gain0, ub0, src1, gain1, ub1, src2, near, out,
    gain2, u2, wide2, cell1, ua1, ut1, wide1, wide0, ua0, ut0,
):
    ix, iy = idx[0], idx[1]
    lane8 = lanes(8)
    lane24 = lanes(24)
    zero24 = jnp.zeros((24, 128), F32)
    for c in range(2):
        u2[c, 0] = zero24
        u2[c, 6] = zero24
    win2 = Window(src2, gain2, 0.0625, 1, functools.partial(near2, lane24))
    inside2 = row_mask(24, iy * 4 - 8, 64)
    keep2 = [inside2 * scalar_mask(ix - 2 + b, 16) for b in range(5)]
    for b in range(5):
        win2.start(b, keep2[b], u2)
    a_low = lane8 % 2 == 0
    b_low = lane8 // 4 % 2 == 0
    x_low = lane8 // 2 % 2 == 0

    def widen3(c):
        sides = []
        shift = jnp.where(c == 0, 4, 124)
        for yl in range(2):
            pick = (lane8 // 4 % 2 == c) & (lane8 % 2 == yl)
            cells = []
            for bb in range(7):
                t = jnp.where(pick, near[bb], 0.0)
                t = t + lroll(t, 1 - 2 * yl)
                t = t + pltpu.roll(t, shift, 1)
                low, high = z_pair(t, lane8, 8)
                cells.append(0.75 * t + 0.25 * jnp.where(b_low, low, high))
            blocks = []
            for b in range(1, 6):
                low = lroll(jnp.where(a_low, cells[b - 1], cells[b]), -2)
                high = lroll(jnp.where(a_low, cells[b], cells[b + 1]), 2)
                blocks.append(0.75 * cells[b] + 0.25 * jnp.where(x_low, low, high))
            sides.append(blocks)
        for b in range(5):
            t0, t1 = sides[0][b], sides[1][b]
            wide2[c, b, pl.ds(0, 8, 4), :] = 0.75 * t0 + 0.25 * sroll(t1, 1)
            wide2[c, b, pl.ds(1, 8, 4), :] = 0.75 * t0 + 0.25 * t1
            wide2[c, b, pl.ds(2, 8, 4), :] = 0.75 * t1 + 0.25 * t0
            wide2[c, b, pl.ds(3, 8, 4), :] = 0.75 * t1 + 0.25 * sroll(t0, -1)

    repeat(0, 2, widen3)

    def sweep2(i):
        add = jnp.where(i == 0, F32(1), F32(0))
        new = [win2.relaxed(b, u2) for b in range(5)]
        for b in range(5):
            for c in range(2):
                fix = wide2[c, b, pl.ds(4, 24), :] * (keep2[b] * add)
                u2[c, b + 1] = new[b][c] + fix

    repeat(0, 3, sweep2)

    lane16 = lanes(16)
    slot4 = lane16 % 4

    def widen2(b):
        for xl in range(4):
            for c in range(2):
                t = jnp.where(slot4 == xl, u2[c, b + 1, pl.ds(4, 16), :], 0.0)
                t = lroll(t, -xl) if xl else t
                t = t + lroll(t, 1)
                t = t + lroll(t, 2)
                low, high = z_pair(t, lane16, 4)
                cell1[c, 4 * b - 4 + xl] = 0.75 * t + 0.25 * jnp.where(slot4 < 2, low, high)

    repeat(1, 4, widen2)
    lane_even = lane16 % 2 == 0

    def mix2(q):
        for c in range(2):
            side = jnp.where(lane_even, cell1[c, q], cell1[c, q + 2])
            t = 0.75 * cell1[c, q + 1] + 0.25 * side
            wide1[c, q, pl.ds(0, 16, 2), :] = 0.75 * t + 0.25 * sroll(t, 1)
            wide1[c, q, pl.ds(1, 16, 2), :] = 0.75 * t + 0.25 * sroll(t, -1)

    repeat(1, 9, mix2, 4)
    for c in range(2):
        ua1[c, 1] = zero24
        ua1[c, 10] = zero24
    inside1 = row_mask(24, iy * 8 - 8, 128)

    def correct1(q):
        keep = inside1 * scalar_mask(ix * 4 - 3 + q, 64)
        for c in range(2):
            ua1[c, q + 1] = ub1[c, q + 1] + wide1[c, q, pl.ds(0, 24), :] * keep

    repeat(1, 9, correct1, 4)
    win1 = Window(src1, gain1, 0.25, 1, functools.partial(near1, lane24))

    repeat(1, 9, lambda q: win1.relax(q, ua1, ut1), 4)
    repeat(2, 8, lambda q: win1.relax(q, ut1, ua1), 3)

    def widen1(q):
        for c in range(2):
            t = ua1[c, q + 1, pl.ds(5, 16), :]
            up, down = lroll(t, 1), lroll(t, -1)
            for p in range(2):
                v = jnp.where(lane_even, t, up) if p == 0 else jnp.where(lane_even, down, t)
                low, high = z_pair(v, lane16, 2)
                v = 0.75 * v + 0.25 * jnp.where(lane_even, low, high)
                wide0[c, 2 * q + p, pl.ds(0, 16, 2), :] = 0.75 * v + 0.25 * sroll(v, 1)
                wide0[c, 2 * q + p, pl.ds(1, 16, 2), :] = 0.75 * v + 0.25 * sroll(v, -1)

    repeat(2, 8, widen1, 2)
    inside0 = row_mask(24, iy * 16 - 3, 256)

    def correct0(at):
        for c in range(2):
            low = wide0[c, at - 1, pl.ds(3, 24), :]
            mid = wide0[c, at, pl.ds(3, 24), :]
            high = wide0[c, at + 1, pl.ds(3, 24), :]
            for child, side in ((0, low), (1, high)):
                x = 2 * at - 9 + child
                keep = inside0 * scalar_mask(ix * 16 - 3 + x, 256)
                ua0[c, x] = ub0[c, x] + (0.75 * mid + 0.25 * side) * keep

    repeat(5, 15, correct0, 2)
    win0 = Window(src0, gain0, 1.0, 0, functools.partial(near0, lane24))
    repeat(2, 20, lambda x: win0.relax(x, ua0, ut0), 3)

    def finish0(x):
        new = win0.relaxed(x + 3, ut0)
        for c in range(2):
            ua0[c, x + 3] = new[c]
            out[c, x] = ua0[c, x + 3, pl.ds(3, 16), :]

    repeat(0, 16, finish0, 4)


def call(kernel, name, out_shape, scratch, *args, micros=2):
    vmem = pl.BlockSpec(memory_space=pltpu.VMEM)
    return pl.pallas_call(
        kernel,
        name=name,
        out_shape=[jax.ShapeDtypeStruct(shape, F32) for shape in out_shape],
        in_specs=[pl.BlockSpec(memory_space=pltpu.SMEM)] + [vmem] * (len(args) - 1),
        out_specs=[vmem] * len(out_shape),
        scratch_shapes=[pltpu.VMEM(shape, F32) for shape in scratch],
        cost_estimate=pl.CostEstimate(
            flops=0, bytes_accessed=micros * 3_500_000, transcendentals=0
        ),
        compiler_params=pltpu.CompilerParams(vmem_limit_bytes=40 * 1024 * 1024),
    )(*args)


BOTH = ("gx", "gy")


def partners(axis, first):
    counts = [lax.axis_size(name) for name in BOTH]
    along = BOTH.index(axis)
    pairs = []
    for i in range(counts[0]):
        for j in range(counts[1]):
            place = [i, j]
            other = ((place[along] + first) ^ 1) - first
            if 0 <= other < counts[along]:
                place[along] = other
            else:
                place[1 - along] ^= 1
            pairs.append((i * counts[1] + j, place[0] * counts[1] + place[1]))
    return pairs


def trade(to_low, to_high, axis):
    even = lax.axis_index(axis) % 2 == 0
    if to_low is to_high:
        one = two = to_low
    else:
        one = jnp.where(even, to_high, to_low)
        two = jnp.where(even, to_low, to_high)
    one = lax.ppermute(one, BOTH, partners(axis, 0))
    two = lax.ppermute(two, BOTH, partners(axis, 1))
    return jnp.where(even, two, one), jnp.where(even, one, two)


def body(residual_in, wave_sq):
    ix = lax.axis_index("gx")
    iy = lax.axis_index("gy")
    idx = jnp.stack([ix, iy]).astype(jnp.int32)

    own = jnp.concatenate([residual_in, wave_sq[None]], axis=0)
    low, high = trade(own[:, :3], own[:, 13:], "gx")
    strip = jnp.concatenate([low, own, high], axis=1)
    low, high = trade(
        strip[:, :, :3].transpose(0, 2, 1, 3).reshape(9, 22, 128),
        strip[:, :, 13:].transpose(0, 2, 1, 3).reshape(9, 22, 128),
        "gy",
    )
    low = low.reshape(3, 3, 22, 128).transpose(0, 2, 1, 3)
    high = high.reshape(3, 3, 22, 128).transpose(0, 2, 1, 3)
    src0 = jnp.concatenate([low, strip, high, jnp.zeros((3, 22, 2, 128), F32)], axis=2)

    n0 = (2, 22, 24, 128)
    n1 = (2, 12, 24, 128)
    own1, gain0, first0 = call(
        down0_kernel, "down0", [(3, 4, 8, 128), n0, n0], [n0, (3, 8, 24, 128)], idx, src0
    )
    low, high = trade(own1[:, :3], own1[:, 1:], "gx")
    strip = jnp.concatenate([low, own1, high], axis=1)
    low, high = trade(strip, strip, "gy")
    src1 = jnp.concatenate([low, strip, high], axis=2)

    part, own2, gain1, first1 = call(
        down1_kernel,
        "down1",
        [(64, 8, 128), (3, 3, 16, 128), (2, 10, 24, 128), n1],
        [n1, (3, 10, 32, 128), (2, 3, 16, 128), (2, 5, 16, 128), (2, 5, 16, 128)],
        idx,
        src1,
    )
    part = part.reshape(256, 2, 128)
    flat = lax.all_to_all(part, ("gx", "gy"), 0, 0).reshape(512, 128)
    low, high = trade(own2[:, 1:], own2[:, :2], "gx")
    strip = jnp.concatenate([low, own2[:, 1:2], high], axis=1)
    strip, flat = lax.optimization_barrier((strip, flat))
    low, high = trade(strip[:, :, 4:12], strip[:, :, :8], "gy")
    src2 = jnp.concatenate(
        [low, strip[:, :, 4:8], high, jnp.zeros((3, 5, 4, 128), F32)], axis=2
    )

    wide = (22, 16, 128)
    near = call(
        coarse_kernel,
        "coarse",
        [(7, 8, 128)],
        [wide, wide, wide, wide, wide, wide]
        + [(4, 16, 128), (4, 16, 128), (4, 16, 128), (7, 32, 128)],
        idx,
        flat,
        micros=5,
    )[0]
    return call(
        up_kernel,
        "up",
        [(2, 16, 16, 128)],
        [(2, 5, 24, 128), (2, 7, 24, 128), (2, 5, 32, 128)]
        + [(2, 12, 16, 128), n1, n1, (2, 10, 32, 128), (2, 16, 32, 128), n0, n0],
        idx,
        src0,
        gain0,
        first0,
        src1,
        gain1,
        first1,
        src2,
        near,
        micros=6,
    )[0]


def solution(mesh):
    placed = (P(None, "gx", "gy", None), P("gx", "gy", None))
    return jax.shard_map(
        body, mesh=mesh, in_specs=placed, out_specs=P(None, "gx", "gy", None), check_vma=False
    )
```

```python
import functools

import jax
import jax.numpy as jnp
from jax import lax
from jax.experimental import pallas as pl
from jax.experimental.pallas import tpu as pltpu
from jax.sharding import PartitionSpec as P

OMEGA = 0.6
SHIFT = 0.5
F32 = jnp.float32


def lroll(v, shift):
    return pltpu.roll(v, shift % v.shape[1], 1)


def sroll(v, shift):
    return pltpu.roll(v, shift % v.shape[0], 0)


def lanes(rows):
    return lax.broadcasted_iota(jnp.int32, (rows, 128), 1)


def sublanes(rows):
    return lax.broadcasted_iota(jnp.int32, (rows, 128), 0)


def row_mask(rows, first, count):
    place = sublanes(rows) + first
    return jnp.where((place >= 0) & (place < count), F32(1), F32(0))


def block_mask(rows, lane, x_first, y_first):
    x = lane % 4 + x_first
    y = sublanes(rows) + y_first
    return jnp.where((x >= 0) & (x < 64) & (y >= 0) & (y < 64), F32(1), F32(0))


def scalar_mask(place, count):
    return jnp.where((place >= 0) & (place < count), F32(1), F32(0))


def z_pair(v, lane, step):
    low = jnp.where(lane >= step, lroll(v, step), 0.0)
    high = jnp.where(lane < 128 - step, lroll(v, -step), 0.0)
    return low, high


def z_sum(v, lane, step):
    low, high = z_pair(v, lane, step)
    return low + high


def y_sum(v):
    return sroll(v, 1) + sroll(v, -1)


def inverse(w, scale, keep):
    real = 6.0 * scale - w
    imag = SHIFT * w
    factor = (OMEGA * keep) / (real * real + imag * imag)
    return real * factor, -imag * factor


def misfit(f, w, v, nb, scale):
    (fr, fi), (vr, vi), (nr, ni) = f, v, nb
    mr = fr - scale * (6.0 * vr - nr) + w * (vr + SHIFT * vi)
    mi = fi - scale * (6.0 * vi - ni) + w * (vi - SHIFT * vr)
    return mr, mi


def cmul(g, m):
    return g[0] * m[0] - g[1] * m[1], g[0] * m[1] + g[1] * m[0]


def repeat(low, high, step, unroll=1):
    def run(i, carry):
        step(i)
        return carry

    lax.fori_loop(low, high, run, 0, unroll=unroll)


class Window:
    def __init__(self, src, gain, scale, pad, neighbours):
        self.src, self.gain, self.scale, self.pad = src, gain, scale, pad
        self.neighbours = neighbours

    def start(self, row, keep, out):
        w = self.src[2, row]
        g = inverse(w, self.scale, keep)
        self.gain[0, row], self.gain[1, row] = g
        u = cmul(g, (self.src[0, row], self.src[1, row]))
        out[0, row + self.pad], out[1, row + self.pad] = u

    def misfit(self, row, field):
        at = row + self.pad
        v = (field[0, at], field[1, at])
        nb = tuple(self.neighbours(field, c, at, v[c]) for c in range(2))
        f = (self.src[0, row], self.src[1, row])
        return v, misfit(f, self.src[2, row], v, nb, self.scale)

    def relaxed(self, row, field):
        v, m = self.misfit(row, field)
        d = cmul((self.gain[0, row], self.gain[1, row]), m)
        return v[0] + d[0], v[1] + d[1]

    def relax(self, row, field, out):
        at = row + self.pad
        out[0, at], out[1, at] = self.relaxed(row, field)


def near0(lane, ref, c, at, v):
    return ref[c, at - 1] + ref[c, at + 1] + y_sum(v) + z_sum(v, lane, 1)


def near1(lane, ref, c, at, v):
    low = lroll(ref[c, at - 1] + v, -1)
    high = lroll(v + ref[c, at + 1], 1)
    return jnp.where(lane % 2 == 0, low, high) + y_sum(v) + z_sum(v, lane, 2)


def near2(lane, ref, c, at, v):
    slot = lane % 4
    low = jnp.where(slot == 0, lroll(ref[c, at - 1], -3), lroll(v, 1))
    high = jnp.where(slot == 3, lroll(ref[c, at + 1], 3), lroll(v, -1))
    return low + high + y_sum(v) + z_sum(v, lane, 4)


def level0(src, gain, first, ix, iy):
    lane = lanes(24)
    win = Window(src, gain, 1.0, 0, functools.partial(near0, lane))
    inside = row_mask(24, iy * 16 - 3, 256)
    repeat(0, 22, lambda x: win.start(x, inside * scalar_mask(ix * 16 - 3 + x, 256), first), 2)
    return win, inside


def down0_kernel(idx, src, out, gain, ub, ua, tmp):
    ix, iy = idx[0], idx[1]
    win, _ = level0(src, gain, ua, ix, iy)
    repeat(1, 21, lambda x: win.relax(x, ua, ub), 4)
    for c in range(2):
        for x in (0, 21):
            ub[c, x] = jnp.zeros((24, 128), F32)
    lane = lanes(8)
    even = lane % 2 == 0

    def halve(q):
        rows = []
        for half in range(2):
            x = 4 * q + 3 + 2 * half
            _, m0 = win.misfit(x, ub)
            _, m1 = win.misfit(x + 1, ub)
            parts = (m0[0] + m1[0], m0[1] + m1[1], src[2, x] + src[2, x + 1])
            got = []
            for c in range(3):
                tmp[c, 2 * q + half] = parts[c]
                t = tmp[c, 2 * q + half, pl.ds(3, 8, 2)] + tmp[c, 2 * q + half, pl.ds(4, 8, 2)]
                got.append(0.125 * (t + lroll(t, -1)))
            rows.append(got)
        for c in range(3):
            out[c, q] = jnp.where(even, rows[0][c], lroll(rows[1][c], 1))

    repeat(0, 4, halve)


def down1_kernel(idx, src, out, src2, gain, ub, ua, tmp, gain2, va, vb):
    ix, iy = idx[0], idx[1]
    lane24 = lanes(24)
    zero24 = jnp.zeros((24, 128), F32)
    for buf in (ua, ub):
        for c in range(2):
            buf[c, 0] = zero24
            buf[c, 11] = zero24
    win = Window(src, gain, 0.25, 1, functools.partial(near1, lane24))
    inside = row_mask(24, iy * 8 - 8, 128)
    repeat(0, 10, lambda q: win.start(q, inside * scalar_mask(ix * 4 - 3 + q, 64), ua), 5)
    repeat(0, 10, lambda q: win.relax(q, ua, ub), 5)
    lane = lanes(8)
    corner = lane % 4 == 0

    def halve(q):
        _, m = win.misfit(q, ub)
        parts = (m[0], m[1], src[2, q])
        for c in range(3):
            t = parts[c] + lroll(parts[c], -1)
            tmp[c, q] = t + lroll(t, -2)

    repeat(1, 9, halve, 4)

    def gather(b):
        for c in range(3):
            packed = jnp.zeros((8, 128), F32)
            for j in range(4):
                q = 4 * b + 1 + j
                t = tmp[c, q, pl.ds(4, 8, 2), :] + tmp[c, q, pl.ds(5, 8, 2), :]
                t = jnp.where(corner, 0.125 * t, 0.0)
                packed = packed + (lroll(t, j) if j else t)
            src2[c, b] = packed

    for b in range(2):
        gather(b)
    for buf in (va, vb):
        for c in range(2):
            buf[c, 0] = jnp.zeros((8, 128), F32)
            buf[c, 3] = jnp.zeros((8, 128), F32)
    win2 = Window(src2, gain2, 0.0625, 1, functools.partial(near2, lane))
    for b in range(2):
        win2.start(b, block_mask(8, lane, ix * 4 - 2 + 4 * b, iy * 4 - 2), va)
    for b in range(2):
        win2.relax(b, va, vb)
    m = [win2.misfit(b, vb)[1] for b in range(2)]

    def third(v0, v1):
        total = jnp.zeros((1, 128), F32)
        for v, slot, move in ((v0, 2, -2), (v1, 0, 2)):
            t = v + lroll(v, -1)
            t = t + lroll(t, -4)
            t = 0.125 * jnp.where(lane % 8 == slot, t + sroll(t, -1), 0.0)
            total = total + lroll(t[2:3], move) + lroll(t[4:5], move + 1)
        return total

    field = third(m[0][0], m[1][0]) + lroll(third(m[0][1], m[1][1]), 4)
    wave = third(src2[2, 0], src2[2, 1])
    wave = wave + lroll(wave, 4)
    pair = jnp.concatenate([field, wave] * 4, axis=0)

    def spread(i):
        out[i] = pair

    repeat(0, 64, spread, 8)


def swap(v, real):
    return jnp.where(real, lroll(v, -4), lroll(v, 4))


def up_kernel(
    idx, src0, gain0, ub0, src1, gain1, ub1, src2, flat, out,
    f3, w3, ga3, gb3, ua3, ub3, f4, w4, s4, e3, gain2, u2, wide2, cell1, ua1, ut1, wide1, wide0, ua0, ut0,
):
    ix, iy = idx[0], idx[1]
    lane = lanes(16)
    real = lane // 4 % 2 == 0
    sign = jnp.where(real, F32(SHIFT), F32(-SHIFT))
    xlow = lane // 2 % 2 == 0
    ylow = lane % 2 == 0
    zlow = lane // 8 % 2 == 0
    slot = lane % 4
    row = sublanes(16)
    zero16 = jnp.zeros((16, 128), F32)

    def y_pair(v):
        return jnp.where(row >= 1, sroll(v, 1), 0.0), jnp.where(row < 15, sroll(v, -1), 0.0)

    def packed_gain(w, scale):
        gr, gi = inverse(w, scale, 1.0)
        return gr, jnp.where(real, -gi, gi)

    def packed_misfit(f, w, v, nb, scale):
        return f - scale * (6.0 * v - nb) + w * (v + sign * swap(v, real))

    for at in (0, 1, 2, 19, 20, 21):
        for ref in (f3, w3, ga3, gb3):
            ref[at] = zero16
        for ref in (ua3, ub3):
            ref[at] = zero16
    for j in range(5):
        e3[j] = jnp.zeros((32, 128), F32)

    def start3(x):
        at = x + 3
        f3[at] = flat[pl.ds(32 * x, 16, 2), :]
        w = flat[pl.ds(32 * x + 1, 16, 2), :]
        w3[at] = w
        ga, gb = packed_gain(w, 1.0 / 64)
        ga3[at], gb3[at] = ga, gb
        ua3[at] = ga * f3[at] + gb * swap(f3[at], real)

    def miss3(ref, at):
        v = ref[at]
        down, up = y_pair(v)
        xs = jnp.where(xlow, lroll(ref[at - 1] + v, -2), lroll(v + ref[at + 1], 2))
        ys = jnp.where(ylow, lroll(v + down, -1), lroll(v + up, 1))
        return v, packed_misfit(f3[at], w3[at], v, xs + ys + z_sum(v, lane, 8), 1.0 / 64)

    def relaxed3(ref, at):
        v, m = miss3(ref, at)
        return v + ga3[at] * m + gb3[at] * swap(m, real)

    def relax3(at):
        ub3[at] = relaxed3(ua3, at)

    repeat(0, 16, start3, 8)
    repeat(3, 19, relax3, 8)

    first = (slot == 0) & zlow

    def eighth(v):
        v = v + lroll(v, -1)
        v = v + lroll(v, -2)
        return jnp.where(first, 0.125 * (v + lroll(v, -8)), 0.0)

    def halve3(r):
        f, w = zero16, zero16
        for k in range(4):
            at = 4 * k + r + 3
            fk, wk = eighth(miss3(ub3, at)[1]), eighth(w3[at])
            f = f + (lroll(fk, k) if k else fk)
            w = w + (lroll(wk, k) if k else wk)
        f4[r], w4[r] = f, w

    repeat(0, 4, halve3, 2)
    fs = [f4[r] for r in range(4)]
    ws = [w4[r] for r in range(4)]
    gs = [packed_gain(w, 1.0 / 256) for w in ws]

    def miss4(us):
        low = jnp.where(slot >= 1, lroll(us[3], 1), 0.0)
        high = jnp.where(slot < 3, lroll(us[0], -1), 0.0)
        wide = [low, *us, high]
        ms = []
        for r in range(4):
            down, up = y_pair(us[r])
            nb = wide[r] + wide[r + 2] + down + up + z_sum(us[r], lane, 16)
            ms.append(packed_misfit(fs[r], ws[r], us[r], nb, 1.0 / 256))
        return ms

    def relax4(_, us):
        ms = miss4(us)
        return tuple(u + g[0] * m + g[1] * swap(m, real) for u, g, m in zip(us, gs, ms))

    us = tuple(g[0] * f + g[1] * swap(f, real) for g, f in zip(gs, fs))
    us = lax.fori_loop(0, 5, relax4, us)
    ms = miss4(us)
    total_m = ms[0] + ms[1] + ms[2] + ms[3]
    total_w = ws[0] + ws[1] + ws[2] + ws[3]
    sum_r = jnp.sum(jnp.where(zlow & real, total_m, 0.0))
    sum_i = jnp.sum(jnp.where(zlow & ~real, total_m, 0.0))
    sum_w = jnp.sum(jnp.where(zlow & real, total_w, 0.0))
    numer = jnp.where(real, sum_r - SHIFT * sum_i, sum_i + SHIFT * sum_r)
    const = -numer / (jnp.full((16, 128), (1.0 + SHIFT * SHIFT), F32) * sum_w)
    for r in range(4):
        s4[r] = jnp.where(zlow, us[r] + const, 0.0)

    def spread4(j):
        x = ix - 4 + j
        inside = (x >= 0) & (x < 16)
        x = jnp.clip(x, 0, 15)
        k = x // 4
        t = jnp.where((slot == k) & inside, s4[x - 4 * k], 0.0)
        t = pltpu.roll(t, lax.rem(128 - k, 128), 1)
        t = t + lroll(t, 1)
        t = t + lroll(t, 2)
        t = t + lroll(t, 8)
        low, high = z_pair(t, lane, 16)
        t = 0.75 * t + 0.25 * jnp.where(zlow, low, high)
        down, up = y_pair(t)
        return 0.75 * t + 0.25 * jnp.where(ylow, down, up)

    wide = [spread4(j) for j in range(9)]
    for j in range(7):
        at = ix + j
        fix = 0.75 * wide[j + 1] + 0.25 * jnp.where(xlow, wide[j], wide[j + 2])
        fix = jnp.where((at >= 3) & (at < 19), fix, 0.0)
        ub3[at] = ub3[at] + fix

    def sweep3(_):
        new = [relaxed3(ub3, ix + j) for j in range(1, 6)]
        for j in range(1, 6):
            ub3[ix + j] = new[j - 1]

    repeat(0, 2, sweep3)
    for j in range(1, 6):
        e3[j - 1, pl.ds(8, 16), :] = ub3[ix + j]

    lane8 = lanes(8)
    lane24 = lanes(24)
    zero24 = jnp.zeros((24, 128), F32)
    for c in range(2):
        u2[c, 0] = zero16
        u2[c, 5] = zero16
    win2 = Window(src2, gain2, 0.0625, 1, functools.partial(near2, lane))
    keep2 = [block_mask(16, lane, ix * 4 - 6 + 4 * b, iy * 4 - 6) for b in range(4)]
    for b in range(4):
        win2.start(b, keep2[b], u2)
    a_low = lane8 % 2 == 0
    b_low = lane8 // 4 % 2 == 0
    h_low = lane8 // 2 % 2 == 0

    def widen3(c):
        sides = []
        shift = jnp.where(c == 0, 4, 124)
        for yl in range(2):
            pick = (lane8 // 4 % 2 == c) & (lane8 % 2 == yl)
            ups, downs = [], []
            for bb in range(5):
                t = jnp.where(pick, e3[bb, pl.ds(iy + 5, 8), :], 0.0)
                t = t + lroll(t, 1 - 2 * yl)
                t = t + pltpu.roll(t, shift, 1)
                low, high = z_pair(t, lane8, 8)
                t = 0.75 * t + 0.25 * jnp.where(b_low, low, high)
                ups.append(lroll(t, 2))
                downs.append(lroll(t, -2))
            cells = [ups[0]]
            cells += [jnp.where(h_low, downs[b], ups[b + 1]) for b in range(4)]
            cells += [downs[4]]
            blocks = []
            for b in range(1, 5):
                low = lroll(jnp.where(a_low, cells[b - 1], cells[b]), -2)
                high = lroll(jnp.where(a_low, cells[b], cells[b + 1]), 2)
                blocks.append(0.75 * cells[b] + 0.25 * jnp.where(h_low, low, high))
            sides.append(blocks)
        for b in range(4):
            t0, t1 = sides[0][b], sides[1][b]
            wide2[c, b, pl.ds(0, 8, 4), :] = 0.75 * t0 + 0.25 * sroll(t1, 1)
            wide2[c, b, pl.ds(1, 8, 4), :] = 0.75 * t0 + 0.25 * t1
            wide2[c, b, pl.ds(2, 8, 4), :] = 0.75 * t1 + 0.25 * t0
            wide2[c, b, pl.ds(3, 8, 4), :] = 0.75 * t1 + 0.25 * sroll(t0, -1)

    repeat(0, 2, widen3)

    def sweep2(i):
        add = jnp.where(i == 0, F32(1), F32(0))
        new = [win2.relaxed(b, u2) for b in range(4)]
        for b in range(4):
            for c in range(2):
                fix = wide2[c, b, pl.ds(6, 16), :] * (keep2[b] * add)
                u2[c, b + 1] = new[b][c] + fix

    repeat(0, 3, sweep2)

    slot4 = lane % 4

    def widen2(at, b, xl):
        for c in range(2):
            t = jnp.where(slot4 == xl, u2[c, b + 1], 0.0)
            t = lroll(t, -xl) if xl else t
            t = t + lroll(t, 1)
            t = t + lroll(t, 2)
            low, high = z_pair(t, lane, 4)
            cell1[c, at] = 0.75 * t + 0.25 * jnp.where(slot4 < 2, low, high)

    def widen_block(b):
        for xl in range(4):
            widen2(4 * b - 3 + xl, b, xl)

    widen2(0, 0, 3)
    repeat(1, 3, widen_block)
    widen2(9, 3, 0)
    lane_even = lane % 2 == 0

    def mix2(q):
        for c in range(2):
            side = jnp.where(lane_even, cell1[c, q - 1], cell1[c, q + 1])
            t = 0.75 * cell1[c, q] + 0.25 * side
            wide1[c, q, pl.ds(0, 16, 2), :] = 0.75 * t + 0.25 * sroll(t, 1)
            wide1[c, q, pl.ds(1, 16, 2), :] = 0.75 * t + 0.25 * sroll(t, -1)

    repeat(1, 9, mix2, 4)
    for c in range(2):
        ua1[c, 1] = zero24
        ua1[c, 10] = zero24
    inside1 = row_mask(24, iy * 8 - 8, 128)

    def correct1(q):
        keep = inside1 * scalar_mask(ix * 4 - 3 + q, 64)
        for c in range(2):
            ua1[c, q + 1] = ub1[c, q + 1] + wide1[c, q, pl.ds(4, 24), :] * keep

    repeat(1, 9, correct1, 4)
    win1 = Window(src1, gain1, 0.25, 1, functools.partial(near1, lane24))

    repeat(1, 9, lambda q: win1.relax(q, ua1, ut1), 4)
    repeat(2, 8, lambda q: win1.relax(q, ut1, ua1), 3)

    def widen1(q):
        for c in range(2):
            t = ua1[c, q + 1, pl.ds(5, 16), :]
            up, down = lroll(t, 1), lroll(t, -1)
            for p in range(2):
                v = jnp.where(lane_even, t, up) if p == 0 else jnp.where(lane_even, down, t)
                low, high = z_pair(v, lane, 2)
                v = 0.75 * v + 0.25 * jnp.where(lane_even, low, high)
                wide0[c, 2 * q + p, pl.ds(0, 16, 2), :] = 0.75 * v + 0.25 * sroll(v, 1)
                wide0[c, 2 * q + p, pl.ds(1, 16, 2), :] = 0.75 * v + 0.25 * sroll(v, -1)

    repeat(2, 8, widen1, 2)
    inside0 = row_mask(24, iy * 16 - 3, 256)

    def correct0(at):
        for c in range(2):
            low = wide0[c, at - 1, pl.ds(3, 24), :]
            mid = wide0[c, at, pl.ds(3, 24), :]
            high = wide0[c, at + 1, pl.ds(3, 24), :]
            for child, side in ((0, low), (1, high)):
                x = 2 * at - 9 + child
                keep = inside0 * scalar_mask(ix * 16 - 3 + x, 256)
                ua0[c, x] = ub0[c, x] + (0.75 * mid + 0.25 * side) * keep

    repeat(5, 15, correct0, 2)
    win0 = Window(src0, gain0, 1.0, 0, functools.partial(near0, lane24))
    repeat(2, 20, lambda x: win0.relax(x, ua0, ut0), 3)

    def finish0(x):
        new = win0.relaxed(x + 3, ut0)
        for c in range(2):
            ua0[c, x + 3] = new[c]
            out[c, x] = ua0[c, x + 3, pl.ds(3, 16), :]

    repeat(0, 16, finish0, 4)


def call(kernel, name, out_shape, scratch, *args, micros=2):
    vmem = pl.BlockSpec(memory_space=pltpu.VMEM)
    return pl.pallas_call(
        kernel,
        name=name,
        out_shape=[jax.ShapeDtypeStruct(shape, F32) for shape in out_shape],
        in_specs=[pl.BlockSpec(memory_space=pltpu.SMEM)] + [vmem] * (len(args) - 1),
        out_specs=[vmem] * len(out_shape),
        scratch_shapes=[pltpu.VMEM(shape, F32) for shape in scratch],
        cost_estimate=pl.CostEstimate(
            flops=0, bytes_accessed=micros * 3_500_000, transcendentals=0
        ),
        compiler_params=pltpu.CompilerParams(vmem_limit_bytes=40 * 1024 * 1024),
    )(*args)


BOTH = ("gx", "gy")


def partners(axis, first):
    counts = [lax.axis_size(name) for name in BOTH]
    along = BOTH.index(axis)
    pairs = []
    for i in range(counts[0]):
        for j in range(counts[1]):
            place = [i, j]
            other = ((place[along] + first) ^ 1) - first
            if 0 <= other < counts[along]:
                place[along] = other
            else:
                place[1 - along] ^= 1
            pairs.append((i * counts[1] + j, place[0] * counts[1] + place[1]))
    return pairs


def trade(to_low, to_high, axis):
    even = lax.axis_index(axis) % 2 == 0
    if to_low is to_high:
        one = two = to_low
    else:
        one = jnp.where(even, to_high, to_low)
        two = jnp.where(even, to_low, to_high)
    one = lax.ppermute(one, BOTH, partners(axis, 0))
    two = lax.ppermute(two, BOTH, partners(axis, 1))
    return jnp.where(even, two, one), jnp.where(even, one, two)


def body(residual_in, wave_sq):
    ix = lax.axis_index("gx")
    iy = lax.axis_index("gy")
    idx = jnp.stack([ix, iy]).astype(jnp.int32)

    own = jnp.concatenate([residual_in, wave_sq[None]], axis=0)
    low, high = trade(own[:, :3], own[:, 13:], "gx")
    strip = jnp.concatenate([low, own, high], axis=1)
    low, high = trade(
        strip[:, :, :3].transpose(0, 2, 1, 3).reshape(9, 22, 128),
        strip[:, :, 13:].transpose(0, 2, 1, 3).reshape(9, 22, 128),
        "gy",
    )
    low = low.reshape(3, 3, 22, 128).transpose(0, 2, 1, 3)
    high = high.reshape(3, 3, 22, 128).transpose(0, 2, 1, 3)
    src0 = jnp.concatenate([low, strip, high, jnp.zeros((3, 22, 2, 128), F32)], axis=2)

    n0 = (2, 22, 24, 128)
    n1 = (2, 12, 24, 128)
    own1, gain0, first0 = call(
        down0_kernel, "down0", [(3, 4, 8, 128), n0, n0], [n0, (3, 8, 24, 128)], idx, src0
    )
    low, high = trade(own1[:, :3], own1[:, 1:], "gx")
    strip = jnp.concatenate([low, own1, high], axis=1)
    low, high = trade(strip, strip, "gy")
    src1 = jnp.concatenate([low, strip, high], axis=2)

    part, own2, gain1, first1 = call(
        down1_kernel,
        "down1",
        [(64, 8, 128), (3, 2, 8, 128), (2, 10, 24, 128), n1],
        [n1, (3, 10, 24, 128), (2, 2, 8, 128), (2, 4, 8, 128), (2, 4, 8, 128)],
        idx,
        src1,
    )
    part = part.reshape(256, 2, 128)
    flat = lax.all_to_all(part, ("gx", "gy"), 0, 0).reshape(512, 128)
    low, high = trade(own2[:, 1:], own2[:, :1], "gx")
    strip = jnp.concatenate([low, own2, high], axis=1)
    low, high = trade(strip[:, :, 4:], strip[:, :, :4], "gy")
    src2 = jnp.concatenate([low, strip, high], axis=2)

    wide = (22, 16, 128)
    return call(
        up_kernel,
        "up",
        [(2, 16, 16, 128)],
        [wide, wide, wide, wide, wide, wide]
        + [(4, 16, 128), (4, 16, 128), (4, 16, 128), (5, 32, 128)]
        + [(2, 4, 16, 128), (2, 6, 16, 128), (2, 4, 32, 128)]
        + [(2, 10, 16, 128), n1, n1, (2, 10, 32, 128), (2, 16, 32, 128), n0, n0],
        idx,
        src0,
        gain0,
        first0,
        src1,
        gain1,
        first1,
        src2,
        flat,
        micros=10,
    )[0]


def solution(mesh):
    placed = (P(None, "gx", "gy", None), P("gx", "gy", None))
    return jax.shard_map(
        body, mesh=mesh, in_specs=placed, out_specs=P(None, "gx", "gy", None), check_vma=False
    )
```

```python
import functools

import jax
import jax.numpy as jnp
from jax import lax
from jax.experimental import pallas as pl
from jax.experimental.pallas import tpu as pltpu
from jax.sharding import PartitionSpec as P

OMEGA = 0.6
SHIFT = 0.5
F32 = jnp.float32


def lroll(v, shift):
    return pltpu.roll(v, shift % v.shape[1], 1)


def sroll(v, shift):
    return pltpu.roll(v, shift % v.shape[0], 0)


def lanes(rows):
    return lax.broadcasted_iota(jnp.int32, (rows, 128), 1)


def sublanes(rows):
    return lax.broadcasted_iota(jnp.int32, (rows, 128), 0)


def row_mask(rows, first, count):
    place = sublanes(rows) + first
    return jnp.where((place >= 0) & (place < count), F32(1), F32(0))


def block_mask(rows, lane, x_first, y_first):
    x = lane % 4 + x_first
    y = sublanes(rows) + y_first
    return jnp.where((x >= 0) & (x < 64) & (y >= 0) & (y < 64), F32(1), F32(0))


def scalar_mask(place, count):
    return jnp.where((place >= 0) & (place < count), F32(1), F32(0))


def z_pair(v, lane, step):
    low = jnp.where(lane >= step, lroll(v, step), 0.0)
    high = jnp.where(lane < 128 - step, lroll(v, -step), 0.0)
    return low, high


def z_sum(v, lane, step):
    low, high = z_pair(v, lane, step)
    return low + high


def y_sum(v):
    return sroll(v, 1) + sroll(v, -1)


def inverse(w, scale, keep):
    real = 6.0 * scale - w
    imag = SHIFT * w
    factor = (OMEGA * keep) / (real * real + imag * imag)
    return real * factor, -imag * factor


def misfit(f, w, v, nb, scale):
    (fr, fi), (vr, vi), (nr, ni) = f, v, nb
    mr = fr - scale * (6.0 * vr - nr) + w * (vr + SHIFT * vi)
    mi = fi - scale * (6.0 * vi - ni) + w * (vi - SHIFT * vr)
    return mr, mi


def cmul(g, m):
    return g[0] * m[0] - g[1] * m[1], g[0] * m[1] + g[1] * m[0]


def repeat(low, high, step, unroll=1):
    def run(i, carry):
        step(i)
        return carry

    lax.fori_loop(low, high, run, 0, unroll=unroll)


class Window:
    def __init__(self, src, gain, scale, pad, neighbours):
        self.src, self.gain, self.scale, self.pad = src, gain, scale, pad
        self.neighbours = neighbours

    def start(self, row, keep, out):
        w = self.src[2, row]
        g = inverse(w, self.scale, keep)
        self.gain[0, row], self.gain[1, row] = g
        u = cmul(g, (self.src[0, row], self.src[1, row]))
        out[0, row + self.pad], out[1, row + self.pad] = u

    def misfit(self, row, field):
        at = row + self.pad
        v = (field[0, at], field[1, at])
        nb = tuple(self.neighbours(field, c, at, v[c]) for c in range(2))
        f = (self.src[0, row], self.src[1, row])
        return v, misfit(f, self.src[2, row], v, nb, self.scale)

    def relaxed(self, row, field):
        v, m = self.misfit(row, field)
        d = cmul((self.gain[0, row], self.gain[1, row]), m)
        return v[0] + d[0], v[1] + d[1]

    def relax(self, row, field, out):
        at = row + self.pad
        out[0, at], out[1, at] = self.relaxed(row, field)


def near0(lane, ref, c, at, v):
    return ref[c, at - 1] + ref[c, at + 1] + y_sum(v) + z_sum(v, lane, 1)


def near1(lane, ref, c, at, v):
    low = lroll(ref[c, at - 1] + v, -1)
    high = lroll(v + ref[c, at + 1], 1)
    return jnp.where(lane % 2 == 0, low, high) + y_sum(v) + z_sum(v, lane, 2)


def near2(lane, ref, c, at, v):
    slot = lane % 4
    low = jnp.where(slot == 0, lroll(ref[c, at - 1], -3), lroll(v, 1))
    high = jnp.where(slot == 3, lroll(ref[c, at + 1], 3), lroll(v, -1))
    return low + high + y_sum(v) + z_sum(v, lane, 4)


def level0(src, gain, first, ix, iy):
    lane = lanes(24)
    win = Window(src, gain, 1.0, 0, functools.partial(near0, lane))
    inside = row_mask(24, iy * 16 - 3, 256)
    repeat(0, 22, lambda x: win.start(x, inside * scalar_mask(ix * 16 - 3 + x, 256), first), 2)
    return win, inside


def down0_kernel(idx, src, out, gain, ub, ua, tmp):
    ix, iy = idx[0], idx[1]
    win, _ = level0(src, gain, ua, ix, iy)
    repeat(1, 21, lambda x: win.relax(x, ua, ub), 4)
    for c in range(2):
        for x in (0, 21):
            ub[c, x] = jnp.zeros((24, 128), F32)
    lane = lanes(8)
    even = lane % 2 == 0

    def halve(q):
        rows = []
        for half in range(2):
            x = 4 * q + 3 + 2 * half
            _, m0 = win.misfit(x, ub)
            _, m1 = win.misfit(x + 1, ub)
            parts = (m0[0] + m1[0], m0[1] + m1[1], src[2, x] + src[2, x + 1])
            got = []
            for c in range(3):
                tmp[c, 2 * q + half] = parts[c]
                t = tmp[c, 2 * q + half, pl.ds(3, 8, 2)] + tmp[c, 2 * q + half, pl.ds(4, 8, 2)]
                got.append(0.125 * (t + lroll(t, -1)))
            rows.append(got)
        for c in range(3):
            out[c, q] = jnp.where(even, rows[0][c], lroll(rows[1][c], 1))

    repeat(0, 4, halve)


def down1_kernel(idx, src, out, src2, gain, ub, ua, tmp, gain2, va, vb):
    ix, iy = idx[0], idx[1]
    lane24 = lanes(24)
    zero24 = jnp.zeros((24, 128), F32)
    for buf in (ua, ub):
        for c in range(2):
            buf[c, 0] = zero24
            buf[c, 11] = zero24
    win = Window(src, gain, 0.25, 1, functools.partial(near1, lane24))
    inside = row_mask(24, iy * 8 - 8, 128)
    repeat(0, 10, lambda q: win.start(q, inside * scalar_mask(ix * 4 - 3 + q, 64), ua), 5)
    repeat(0, 10, lambda q: win.relax(q, ua, ub), 5)
    lane = lanes(8)
    corner = lane % 4 == 0

    def halve(q):
        _, m = win.misfit(q, ub)
        parts = (m[0], m[1], src[2, q])
        for c in range(3):
            t = parts[c] + lroll(parts[c], -1)
            tmp[c, q] = t + lroll(t, -2)

    repeat(1, 9, halve, 4)

    def gather(b):
        for c in range(3):
            packed = jnp.zeros((8, 128), F32)
            for j in range(4):
                q = 4 * b + 1 + j
                t = tmp[c, q, pl.ds(4, 8, 2), :] + tmp[c, q, pl.ds(5, 8, 2), :]
                t = jnp.where(corner, 0.125 * t, 0.0)
                packed = packed + (lroll(t, j) if j else t)
            src2[c, b] = packed

    for b in range(2):
        gather(b)
    for buf in (va, vb):
        for c in range(2):
            buf[c, 0] = jnp.zeros((8, 128), F32)
            buf[c, 3] = jnp.zeros((8, 128), F32)
    win2 = Window(src2, gain2, 0.0625, 1, functools.partial(near2, lane))
    for b in range(2):
        win2.start(b, block_mask(8, lane, ix * 4 - 2 + 4 * b, iy * 4 - 2), va)
    for b in range(2):
        win2.relax(b, va, vb)
    m = [win2.misfit(b, vb)[1] for b in range(2)]

    def third(v0, v1):
        total = jnp.zeros((1, 128), F32)
        for v, slot, move in ((v0, 2, -2), (v1, 0, 2)):
            t = v + lroll(v, -1)
            t = t + lroll(t, -4)
            t = 0.125 * jnp.where(lane % 8 == slot, t + sroll(t, -1), 0.0)
            total = total + lroll(t[2:3], move) + lroll(t[4:5], move + 1)
        return total

    field = third(m[0][0], m[1][0]) + lroll(third(m[0][1], m[1][1]), 4)
    wave = third(src2[2, 0], src2[2, 1])
    wave = wave + lroll(wave, 4)
    pair = jnp.concatenate([field, wave] * 4, axis=0)

    for i in range(4):
        out[i] = pair


def swap(v, real):
    return jnp.where(real, lroll(v, -4), lroll(v, 4))


def up_kernel(
    idx, src0, gain0, ub0, src1, gain1, ub1, src2, flat, out,
    f3, w3, ga3, gb3, ua3, ub3, f4, w4, s4, e3, gain2, u2, wide2, cell1, ua1, ut1, wide1, wide0, ua0, ut0,
):
    ix, iy = idx[0], idx[1]
    lane = lanes(16)
    real = lane // 4 % 2 == 0
    sign = jnp.where(real, F32(SHIFT), F32(-SHIFT))
    xlow = lane // 2 % 2 == 0
    ylow = lane % 2 == 0
    zlow = lane // 8 % 2 == 0
    slot = lane % 4
    row = sublanes(16)
    zero16 = jnp.zeros((16, 128), F32)

    def y_pair(v):
        return jnp.where(row >= 1, sroll(v, 1), 0.0), jnp.where(row < 15, sroll(v, -1), 0.0)

    def packed_gain(w, scale):
        gr, gi = inverse(w, scale, 1.0)
        return gr, jnp.where(real, -gi, gi)

    def packed_misfit(f, w, v, nb, scale):
        return f - scale * (6.0 * v - nb) + w * (v + sign * swap(v, real))

    for at in (0, 1, 2, 19, 20, 21):
        for ref in (f3, w3, ga3, gb3):
            ref[at] = zero16
        for ref in (ua3, ub3):
            ref[at] = zero16
    for j in range(5):
        e3[j] = jnp.zeros((32, 128), F32)

    def start3(x):
        at = x + 3
        f3[at] = flat[pl.ds(2 * x, 16, 32), :]
        w = flat[pl.ds(2 * x + 1, 16, 32), :]
        w3[at] = w
        ga, gb = packed_gain(w, 1.0 / 64)
        ga3[at], gb3[at] = ga, gb
        ua3[at] = ga * f3[at] + gb * swap(f3[at], real)

    def miss3(ref, at):
        v = ref[at]
        down, up = y_pair(v)
        xs = jnp.where(xlow, lroll(ref[at - 1] + v, -2), lroll(v + ref[at + 1], 2))
        ys = jnp.where(ylow, lroll(v + down, -1), lroll(v + up, 1))
        return v, packed_misfit(f3[at], w3[at], v, xs + ys + z_sum(v, lane, 8), 1.0 / 64)

    def relaxed3(ref, at):
        v, m = miss3(ref, at)
        return v + ga3[at] * m + gb3[at] * swap(m, real)

    def relax3(at):
        ub3[at] = relaxed3(ua3, at)

    repeat(0, 16, start3, 8)
    repeat(3, 19, relax3, 8)

    first = (slot == 0) & zlow

    def eighth(v):
        v = v + lroll(v, -1)
        v = v + lroll(v, -2)
        return jnp.where(first, 0.125 * (v + lroll(v, -8)), 0.0)

    def halve3(r):
        f, w = zero16, zero16
        for k in range(4):
            at = 4 * k + r + 3
            fk, wk = eighth(miss3(ub3, at)[1]), eighth(w3[at])
            f = f + (lroll(fk, k) if k else fk)
            w = w + (lroll(wk, k) if k else wk)
        f4[r], w4[r] = f, w

    repeat(0, 4, halve3, 2)
    fs = [f4[r] for r in range(4)]
    ws = [w4[r] for r in range(4)]
    gs = [packed_gain(w, 1.0 / 256) for w in ws]

    def miss4(us):
        low = jnp.where(slot >= 1, lroll(us[3], 1), 0.0)
        high = jnp.where(slot < 3, lroll(us[0], -1), 0.0)
        wide = [low, *us, high]
        ms = []
        for r in range(4):
            down, up = y_pair(us[r])
            nb = wide[r] + wide[r + 2] + down + up + z_sum(us[r], lane, 16)
            ms.append(packed_misfit(fs[r], ws[r], us[r], nb, 1.0 / 256))
        return ms

    def relax4(_, us):
        ms = miss4(us)
        return tuple(u + g[0] * m + g[1] * swap(m, real) for u, g, m in zip(us, gs, ms))

    us = tuple(g[0] * f + g[1] * swap(f, real) for g, f in zip(gs, fs))
    us = lax.fori_loop(0, 5, relax4, us)
    ms = miss4(us)
    total_m = ms[0] + ms[1] + ms[2] + ms[3]
    total_w = ws[0] + ws[1] + ws[2] + ws[3]
    sum_r = jnp.sum(jnp.where(zlow & real, total_m, 0.0))
    sum_i = jnp.sum(jnp.where(zlow & ~real, total_m, 0.0))
    sum_w = jnp.sum(jnp.where(zlow & real, total_w, 0.0))
    numer = jnp.where(real, sum_r - SHIFT * sum_i, sum_i + SHIFT * sum_r)
    const = -numer / (jnp.full((16, 128), (1.0 + SHIFT * SHIFT), F32) * sum_w)
    for r in range(4):
        s4[r] = jnp.where(zlow, us[r] + const, 0.0)

    def spread4(j):
        x = ix - 4 + j
        inside = (x >= 0) & (x < 16)
        x = jnp.clip(x, 0, 15)
        k = x // 4
        t = jnp.where((slot == k) & inside, s4[x - 4 * k], 0.0)
        t = pltpu.roll(t, lax.rem(128 - k, 128), 1)
        t = t + lroll(t, 1)
        t = t + lroll(t, 2)
        t = t + lroll(t, 8)
        low, high = z_pair(t, lane, 16)
        t = 0.75 * t + 0.25 * jnp.where(zlow, low, high)
        down, up = y_pair(t)
        return 0.75 * t + 0.25 * jnp.where(ylow, down, up)

    wide = [spread4(j) for j in range(9)]
    for j in range(7):
        at = ix + j
        fix = 0.75 * wide[j + 1] + 0.25 * jnp.where(xlow, wide[j], wide[j + 2])
        fix = jnp.where((at >= 3) & (at < 19), fix, 0.0)
        ub3[at] = ub3[at] + fix

    def sweep3(_):
        new = [relaxed3(ub3, ix + j) for j in range(1, 6)]
        for j in range(1, 6):
            ub3[ix + j] = new[j - 1]

    repeat(0, 2, sweep3)
    for j in range(1, 6):
        e3[j - 1, pl.ds(8, 16), :] = ub3[ix + j]

    lane8 = lanes(8)
    lane24 = lanes(24)
    zero24 = jnp.zeros((24, 128), F32)
    for c in range(2):
        u2[c, 0] = zero16
        u2[c, 5] = zero16
    win2 = Window(src2, gain2, 0.0625, 1, functools.partial(near2, lane))
    keep2 = [block_mask(16, lane, ix * 4 - 6 + 4 * b, iy * 4 - 6) for b in range(4)]
    for b in range(4):
        win2.start(b, keep2[b], u2)
    a_low = lane8 % 2 == 0
    b_low = lane8 // 4 % 2 == 0
    h_low = lane8 // 2 % 2 == 0

    def widen3(c):
        sides = []
        shift = jnp.where(c == 0, 4, 124)
        for yl in range(2):
            pick = (lane8 // 4 % 2 == c) & (lane8 % 2 == yl)
            ups, downs = [], []
            for bb in range(5):
                t = jnp.where(pick, e3[bb, pl.ds(iy + 5, 8), :], 0.0)
                t = t + lroll(t, 1 - 2 * yl)
                t = t + pltpu.roll(t, shift, 1)
                low, high = z_pair(t, lane8, 8)
                t = 0.75 * t + 0.25 * jnp.where(b_low, low, high)
                ups.append(lroll(t, 2))
                downs.append(lroll(t, -2))
            cells = [ups[0]]
            cells += [jnp.where(h_low, downs[b], ups[b + 1]) for b in range(4)]
            cells += [downs[4]]
            blocks = []
            for b in range(1, 5):
                low = lroll(jnp.where(a_low, cells[b - 1], cells[b]), -2)
                high = lroll(jnp.where(a_low, cells[b], cells[b + 1]), 2)
                blocks.append(0.75 * cells[b] + 0.25 * jnp.where(h_low, low, high))
            sides.append(blocks)
        for b in range(4):
            t0, t1 = sides[0][b], sides[1][b]
            wide2[c, b, pl.ds(0, 8, 4), :] = 0.75 * t0 + 0.25 * sroll(t1, 1)
            wide2[c, b, pl.ds(1, 8, 4), :] = 0.75 * t0 + 0.25 * t1
            wide2[c, b, pl.ds(2, 8, 4), :] = 0.75 * t1 + 0.25 * t0
            wide2[c, b, pl.ds(3, 8, 4), :] = 0.75 * t1 + 0.25 * sroll(t0, -1)

    repeat(0, 2, widen3)

    def sweep2(i):
        add = jnp.where(i == 0, F32(1), F32(0))
        new = [win2.relaxed(b, u2) for b in range(4)]
        for b in range(4):
            for c in range(2):
                fix = wide2[c, b, pl.ds(6, 16), :] * (keep2[b] * add)
                u2[c, b + 1] = new[b][c] + fix

    repeat(0, 3, sweep2)

    slot4 = lane % 4

    def widen2(at, b, xl):
        for c in range(2):
            t = jnp.where(slot4 == xl, u2[c, b + 1], 0.0)
            t = lroll(t, -xl) if xl else t
            t = t + lroll(t, 1)
            t = t + lroll(t, 2)
            low, high = z_pair(t, lane, 4)
            cell1[c, at] = 0.75 * t + 0.25 * jnp.where(slot4 < 2, low, high)

    def widen_block(b):
        for xl in range(4):
            widen2(4 * b - 3 + xl, b, xl)

    widen2(0, 0, 3)
    repeat(1, 3, widen_block)
    widen2(9, 3, 0)
    lane_even = lane % 2 == 0

    def mix2(q):
        for c in range(2):
            side = jnp.where(lane_even, cell1[c, q - 1], cell1[c, q + 1])
            t = 0.75 * cell1[c, q] + 0.25 * side
            wide1[c, q, pl.ds(0, 16, 2), :] = 0.75 * t + 0.25 * sroll(t, 1)
            wide1[c, q, pl.ds(1, 16, 2), :] = 0.75 * t + 0.25 * sroll(t, -1)

    repeat(1, 9, mix2, 4)
    for c in range(2):
        ua1[c, 1] = zero24
        ua1[c, 10] = zero24
    inside1 = row_mask(24, iy * 8 - 8, 128)

    def correct1(q):
        keep = inside1 * scalar_mask(ix * 4 - 3 + q, 64)
        for c in range(2):
            ua1[c, q + 1] = ub1[c, q + 1] + wide1[c, q, pl.ds(4, 24), :] * keep

    repeat(1, 9, correct1, 4)
    win1 = Window(src1, gain1, 0.25, 1, functools.partial(near1, lane24))

    repeat(1, 9, lambda q: win1.relax(q, ua1, ut1), 4)
    repeat(2, 8, lambda q: win1.relax(q, ut1, ua1), 3)

    def widen1(q):
        for c in range(2):
            t = ua1[c, q + 1, pl.ds(5, 16), :]
            up, down = lroll(t, 1), lroll(t, -1)
            for p in range(2):
                v = jnp.where(lane_even, t, up) if p == 0 else jnp.where(lane_even, down, t)
                low, high = z_pair(v, lane, 2)
                v = 0.75 * v + 0.25 * jnp.where(lane_even, low, high)
                wide0[c, 2 * q + p, pl.ds(0, 16, 2), :] = 0.75 * v + 0.25 * sroll(v, 1)
                wide0[c, 2 * q + p, pl.ds(1, 16, 2), :] = 0.75 * v + 0.25 * sroll(v, -1)

    repeat(2, 8, widen1, 2)
    inside0 = row_mask(24, iy * 16 - 3, 256)

    def correct0(at):
        for c in range(2):
            low = wide0[c, at - 1, pl.ds(3, 24), :]
            mid = wide0[c, at, pl.ds(3, 24), :]
            high = wide0[c, at + 1, pl.ds(3, 24), :]
            for child, side in ((0, low), (1, high)):
                x = 2 * at - 9 + child
                keep = inside0 * scalar_mask(ix * 16 - 3 + x, 256)
                ua0[c, x] = ub0[c, x] + (0.75 * mid + 0.25 * side) * keep

    repeat(5, 15, correct0, 2)
    win0 = Window(src0, gain0, 1.0, 0, functools.partial(near0, lane24))
    repeat(2, 20, lambda x: win0.relax(x, ua0, ut0), 3)

    def finish0(x):
        new = win0.relaxed(x + 3, ut0)
        for c in range(2):
            ua0[c, x + 3] = new[c]
            out[c, x] = ua0[c, x + 3, pl.ds(3, 16), :]

    repeat(0, 16, finish0, 4)


def call(kernel, name, out_shape, scratch, *args, micros=2):
    vmem = pl.BlockSpec(memory_space=pltpu.VMEM)
    return pl.pallas_call(
        kernel,
        name=name,
        out_shape=[jax.ShapeDtypeStruct(shape, F32) for shape in out_shape],
        in_specs=[pl.BlockSpec(memory_space=pltpu.SMEM)] + [vmem] * (len(args) - 1),
        out_specs=[vmem] * len(out_shape),
        scratch_shapes=[pltpu.VMEM(shape, F32) for shape in scratch],
        cost_estimate=pl.CostEstimate(
            flops=0, bytes_accessed=micros * 3_500_000, transcendentals=0
        ),
        compiler_params=pltpu.CompilerParams(vmem_limit_bytes=40 * 1024 * 1024),
    )(*args)


BOTH = ("gx", "gy")


def partners(axis, first):
    counts = [lax.axis_size(name) for name in BOTH]
    along = BOTH.index(axis)
    pairs = []
    for i in range(counts[0]):
        for j in range(counts[1]):
            place = [i, j]
            other = ((place[along] + first) ^ 1) - first
            if 0 <= other < counts[along]:
                place[along] = other
            else:
                place[1 - along] ^= 1
            pairs.append((i * counts[1] + j, place[0] * counts[1] + place[1]))
    return pairs


def trade(to_low, to_high, axis):
    even = lax.axis_index(axis) % 2 == 0
    if to_low is to_high:
        one = two = to_low
    else:
        one = jnp.where(even, to_high, to_low)
        two = jnp.where(even, to_low, to_high)
    one = lax.ppermute(one, BOTH, partners(axis, 0))
    two = lax.ppermute(two, BOTH, partners(axis, 1))
    return jnp.where(even, two, one), jnp.where(even, one, two)


def body(residual_in, wave_sq):
    ix = lax.axis_index("gx")
    iy = lax.axis_index("gy")
    idx = jnp.stack([ix, iy]).astype(jnp.int32)

    own = jnp.concatenate([residual_in, wave_sq[None]], axis=0)
    low, high = trade(own[:, :3], own[:, 13:], "gx")
    strip = jnp.concatenate([low, own, high], axis=1)
    low, high = trade(
        strip[:, :, :3].transpose(0, 2, 1, 3).reshape(9, 22, 128),
        strip[:, :, 13:].transpose(0, 2, 1, 3).reshape(9, 22, 128),
        "gy",
    )
    low = low.reshape(3, 3, 22, 128).transpose(0, 2, 1, 3)
    high = high.reshape(3, 3, 22, 128).transpose(0, 2, 1, 3)
    src0 = jnp.concatenate([low, strip, high, jnp.zeros((3, 22, 2, 128), F32)], axis=2)

    n0 = (2, 22, 24, 128)
    n1 = (2, 12, 24, 128)
    own1, gain0, first0 = call(
        down0_kernel, "down0", [(3, 4, 8, 128), n0, n0], [n0, (3, 8, 24, 128)], idx, src0
    )
    low, high = trade(own1[:, :3], own1[:, 1:], "gx")
    strip = jnp.concatenate([low, own1, high], axis=1)
    low, high = trade(strip, strip, "gy")
    src1 = jnp.concatenate([low, strip, high], axis=2)

    part, own2, gain1, first1 = call(
        down1_kernel,
        "down1",
        [(4, 8, 128), (3, 2, 8, 128), (2, 10, 24, 128), n1],
        [n1, (3, 10, 24, 128), (2, 2, 8, 128), (2, 4, 8, 128), (2, 4, 8, 128)],
        idx,
        src1,
    )
    line = lax.all_to_all(part.reshape(16, 2, 128), "gx", 0, 0).reshape(1, 32, 128)
    line = jnp.broadcast_to(line, (16, 32, 128))
    flat = lax.all_to_all(line, "gy", 0, 0).reshape(512, 128)
    low, high = trade(own2[:, 1:], own2[:, :1], "gx")
    strip = jnp.concatenate([low, own2, high], axis=1)
    low, high = trade(strip[:, :, 4:], strip[:, :, :4], "gy")
    src2 = jnp.concatenate([low, strip, high], axis=2)

    wide = (22, 16, 128)
    return call(
        up_kernel,
        "up",
        [(2, 16, 16, 128)],
        [wide, wide, wide, wide, wide, wide]
        + [(4, 16, 128), (4, 16, 128), (4, 16, 128), (5, 32, 128)]
        + [(2, 4, 16, 128), (2, 6, 16, 128), (2, 4, 32, 128)]
        + [(2, 10, 16, 128), n1, n1, (2, 10, 32, 128), (2, 16, 32, 128), n0, n0],
        idx,
        src0,
        gain0,
        first0,
        src1,
        gain1,
        first1,
        src2,
        flat,
        micros=10,
    )[0]


def solution(mesh):
    placed = (P(None, "gx", "gy", None), P("gx", "gy", None))
    return jax.shard_map(
        body, mesh=mesh, in_specs=placed, out_specs=P(None, "gx", "gy", None), check_vma=False
    )
```

```python
import functools

import jax
import jax.numpy as jnp
from jax import lax
from jax.experimental import pallas as pl
from jax.experimental.pallas import tpu as pltpu
from jax.sharding import PartitionSpec as P

OMEGA = 0.6
SHIFT = 0.5
F32 = jnp.float32


def lroll(v, shift):
    return pltpu.roll(v, shift % v.shape[1], 1)


def sroll(v, shift):
    return pltpu.roll(v, shift % v.shape[0], 0)


def lanes(rows):
    return lax.broadcasted_iota(jnp.int32, (rows, 128), 1)


def sublanes(rows):
    return lax.broadcasted_iota(jnp.int32, (rows, 128), 0)


def row_mask(rows, first, count):
    place = sublanes(rows) + first
    return jnp.where((place >= 0) & (place < count), F32(1), F32(0))


def block_mask(rows, lane, x_first, y_first):
    x = lane % 4 + x_first
    y = sublanes(rows) + y_first
    return jnp.where((x >= 0) & (x < 64) & (y >= 0) & (y < 64), F32(1), F32(0))


def scalar_mask(place, count):
    return jnp.where((place >= 0) & (place < count), F32(1), F32(0))


def z_pair(v, lane, step):
    low = jnp.where(lane >= step, lroll(v, step), 0.0)
    high = jnp.where(lane < 128 - step, lroll(v, -step), 0.0)
    return low, high


def z_sum(v, lane, step):
    low, high = z_pair(v, lane, step)
    return low + high


def y_sum(v):
    return sroll(v, 1) + sroll(v, -1)


def inverse(w, scale, keep):
    real = 6.0 * scale - w
    imag = SHIFT * w
    factor = (OMEGA * keep) / (real * real + imag * imag)
    return real * factor, -imag * factor


def misfit(f, w, v, nb, scale):
    (fr, fi), (vr, vi), (nr, ni) = f, v, nb
    mr = fr - scale * (6.0 * vr - nr) + w * (vr + SHIFT * vi)
    mi = fi - scale * (6.0 * vi - ni) + w * (vi - SHIFT * vr)
    return mr, mi


def cmul(g, m):
    return g[0] * m[0] - g[1] * m[1], g[0] * m[1] + g[1] * m[0]


def repeat(low, high, step, unroll=1):
    def run(i, carry):
        step(i)
        return carry

    lax.fori_loop(low, high, run, 0, unroll=unroll)


class Window:
    def __init__(self, src, gain, scale, pad, neighbours):
        self.src, self.gain, self.scale, self.pad = src, gain, scale, pad
        self.neighbours = neighbours

    def start(self, row, keep, out):
        w = self.src[2, row]
        g = inverse(w, self.scale, keep)
        self.gain[0, row], self.gain[1, row] = g
        u = cmul(g, (self.src[0, row], self.src[1, row]))
        out[0, row + self.pad], out[1, row + self.pad] = u

    def misfit(self, row, field):
        at = row + self.pad
        v = (field[0, at], field[1, at])
        nb = tuple(self.neighbours(field, c, at, v[c]) for c in range(2))
        f = (self.src[0, row], self.src[1, row])
        return v, misfit(f, self.src[2, row], v, nb, self.scale)

    def relaxed(self, row, field):
        v, m = self.misfit(row, field)
        d = cmul((self.gain[0, row], self.gain[1, row]), m)
        return v[0] + d[0], v[1] + d[1]

    def relax(self, row, field, out):
        at = row + self.pad
        out[0, at], out[1, at] = self.relaxed(row, field)


def near0(lane, ref, c, at, v):
    return ref[c, at - 1] + ref[c, at + 1] + y_sum(v) + z_sum(v, lane, 1)


def near1(lane, ref, c, at, v):
    low = lroll(ref[c, at - 1] + v, -1)
    high = lroll(v + ref[c, at + 1], 1)
    return jnp.where(lane % 2 == 0, low, high) + y_sum(v) + z_sum(v, lane, 2)


def near2(lane, ref, c, at, v):
    slot = lane % 4
    low = jnp.where(slot == 0, lroll(ref[c, at - 1], -3), lroll(v, 1))
    high = jnp.where(slot == 3, lroll(ref[c, at + 1], 3), lroll(v, -1))
    return low + high + y_sum(v) + z_sum(v, lane, 4)


def level0(src, gain, first, ix, iy):
    lane = lanes(24)
    win = Window(src, gain, 1.0, 0, functools.partial(near0, lane))
    inside = row_mask(24, iy * 16 - 3, 256)
    repeat(0, 22, lambda x: win.start(x, inside * scalar_mask(ix * 16 - 3 + x, 256), first), 2)
    return win, inside


def down0_kernel(idx, src, out, gain, ub, ua, tmp):
    ix, iy = idx[0], idx[1]
    win, _ = level0(src, gain, ua, ix, iy)
    repeat(1, 21, lambda x: win.relax(x, ua, ub), 10)
    for c in range(2):
        for x in (0, 21):
            ub[c, x] = jnp.zeros((24, 128), F32)
    lane = lanes(8)
    even = lane % 2 == 0

    def halve(q):
        rows = []
        for half in range(2):
            x = 4 * q + 3 + 2 * half
            _, m0 = win.misfit(x, ub)
            _, m1 = win.misfit(x + 1, ub)
            parts = (m0[0] + m1[0], m0[1] + m1[1], src[2, x] + src[2, x + 1])
            got = []
            for c in range(3):
                tmp[c, 2 * q + half] = parts[c]
                t = tmp[c, 2 * q + half, pl.ds(3, 8, 2)] + tmp[c, 2 * q + half, pl.ds(4, 8, 2)]
                got.append(0.125 * (t + lroll(t, -1)))
            rows.append(got)
        for c in range(3):
            out[c, q] = jnp.where(even, rows[0][c], lroll(rows[1][c], 1))

    repeat(0, 4, halve, 2)


def down1_kernel(idx, src, out, src2, gain, ub, ua, tmp, gain2, va, vb):
    ix, iy = idx[0], idx[1]
    lane24 = lanes(24)
    zero24 = jnp.zeros((24, 128), F32)
    for buf in (ua, ub):
        for c in range(2):
            buf[c, 0] = zero24
            buf[c, 11] = zero24
    win = Window(src, gain, 0.25, 1, functools.partial(near1, lane24))
    inside = row_mask(24, iy * 8 - 8, 128)
    repeat(0, 10, lambda q: win.start(q, inside * scalar_mask(ix * 4 - 3 + q, 64), ua), 5)
    repeat(0, 10, lambda q: win.relax(q, ua, ub), 10)
    lane = lanes(8)
    corner = lane % 4 == 0

    def halve(q):
        _, m = win.misfit(q, ub)
        parts = (m[0], m[1], src[2, q])
        for c in range(3):
            t = parts[c] + lroll(parts[c], -1)
            tmp[c, q] = t + lroll(t, -2)

    repeat(1, 9, halve, 8)

    def gather(b):
        for c in range(3):
            packed = jnp.zeros((8, 128), F32)
            for j in range(4):
                q = 4 * b + 1 + j
                t = tmp[c, q, pl.ds(4, 8, 2), :] + tmp[c, q, pl.ds(5, 8, 2), :]
                t = jnp.where(corner, 0.125 * t, 0.0)
                packed = packed + (lroll(t, j) if j else t)
            src2[c, b] = packed

    for b in range(2):
        gather(b)
    for buf in (va, vb):
        for c in range(2):
            buf[c, 0] = jnp.zeros((8, 128), F32)
            buf[c, 3] = jnp.zeros((8, 128), F32)
    win2 = Window(src2, gain2, 0.0625, 1, functools.partial(near2, lane))
    for b in range(2):
        win2.start(b, block_mask(8, lane, ix * 4 - 2 + 4 * b, iy * 4 - 2), va)
    for b in range(2):
        win2.relax(b, va, vb)
    m = [win2.misfit(b, vb)[1] for b in range(2)]

    def third(v0, v1):
        total = jnp.zeros((1, 128), F32)
        for v, slot, move in ((v0, 2, -2), (v1, 0, 2)):
            t = v + lroll(v, -1)
            t = t + lroll(t, -4)
            t = 0.125 * jnp.where(lane % 8 == slot, t + sroll(t, -1), 0.0)
            total = total + lroll(t[2:3], move) + lroll(t[4:5], move + 1)
        return total

    field = third(m[0][0], m[1][0]) + lroll(third(m[0][1], m[1][1]), 4)
    wave = third(src2[2, 0], src2[2, 1])
    wave = wave + lroll(wave, 4)
    pair = jnp.concatenate([field, wave] * 4, axis=0)

    def spread(i):
        out[i] = pair

    repeat(0, 64, spread, 8)


def swap(v, real):
    return jnp.where(real, lroll(v, -4), lroll(v, 4))


def up_kernel(
    idx, src0, gain0, ub0, src1, gain1, ub1, src2, flat, out,
    f3, w3, ga3, gb3, ua3, ub3, f4, w4, s4, e3, gain2, u2, wide2, cell1, ua1, ut1, wide1, wide0, ua0, ut0,
):
    ix, iy = idx[0], idx[1]
    lane = lanes(16)
    real = lane // 4 % 2 == 0
    sign = jnp.where(real, F32(SHIFT), F32(-SHIFT))
    xlow = lane // 2 % 2 == 0
    ylow = lane % 2 == 0
    zlow = lane // 8 % 2 == 0
    slot = lane % 4
    row = sublanes(16)
    zero16 = jnp.zeros((16, 128), F32)

    def y_pair(v):
        return jnp.where(row >= 1, sroll(v, 1), 0.0), jnp.where(row < 15, sroll(v, -1), 0.0)

    def packed_gain(w, scale):
        gr, gi = inverse(w, scale, 1.0)
        return gr, jnp.where(real, -gi, gi)

    def packed_misfit(f, w, v, nb, scale):
        return f - scale * (6.0 * v - nb) + w * (v + sign * swap(v, real))

    for at in (0, 1, 2, 19, 20, 21):
        for ref in (f3, w3, ga3, gb3):
            ref[at] = zero16
        for ref in (ua3, ub3):
            ref[at] = zero16
    for j in range(5):
        e3[j] = jnp.zeros((32, 128), F32)

    def start3(x):
        at = x + 3
        f3[at] = flat[pl.ds(32 * x, 16, 2), :]
        w = flat[pl.ds(32 * x + 1, 16, 2), :]
        w3[at] = w
        ga, gb = packed_gain(w, 1.0 / 64)
        ga3[at], gb3[at] = ga, gb
        ua3[at] = ga * f3[at] + gb * swap(f3[at], real)

    def miss3(ref, at):
        v = ref[at]
        down, up = y_pair(v)
        xs = jnp.where(xlow, lroll(ref[at - 1] + v, -2), lroll(v + ref[at + 1], 2))
        ys = jnp.where(ylow, lroll(v + down, -1), lroll(v + up, 1))
        return v, packed_misfit(f3[at], w3[at], v, xs + ys + z_sum(v, lane, 8), 1.0 / 64)

    def relaxed3(ref, at):
        v, m = miss3(ref, at)
        return v + ga3[at] * m + gb3[at] * swap(m, real)

    def relax3(at):
        ub3[at] = relaxed3(ua3, at)

    repeat(0, 16, start3, 8)
    repeat(3, 19, relax3, 8)

    first = (slot == 0) & zlow

    def eighth(v):
        v = v + lroll(v, -1)
        v = v + lroll(v, -2)
        return jnp.where(first, 0.125 * (v + lroll(v, -8)), 0.0)

    def halve3(r):
        f, w = zero16, zero16
        for k in range(4):
            at = 4 * k + r + 3
            fk, wk = eighth(miss3(ub3, at)[1]), eighth(w3[at])
            f = f + (lroll(fk, k) if k else fk)
            w = w + (lroll(wk, k) if k else wk)
        f4[r], w4[r] = f, w

    repeat(0, 4, halve3, 2)
    fs = [f4[r] for r in range(4)]
    ws = [w4[r] for r in range(4)]
    gs = [packed_gain(w, 1.0 / 256) for w in ws]

    def miss4(us):
        low = jnp.where(slot >= 1, lroll(us[3], 1), 0.0)
        high = jnp.where(slot < 3, lroll(us[0], -1), 0.0)
        wide = [low, *us, high]
        ms = []
        for r in range(4):
            down, up = y_pair(us[r])
            nb = wide[r] + wide[r + 2] + down + up + z_sum(us[r], lane, 16)
            ms.append(packed_misfit(fs[r], ws[r], us[r], nb, 1.0 / 256))
        return ms

    def relax4(_, us):
        ms = miss4(us)
        return tuple(u + g[0] * m + g[1] * swap(m, real) for u, g, m in zip(us, gs, ms))

    us = tuple(g[0] * f + g[1] * swap(f, real) for g, f in zip(gs, fs))
    us = lax.fori_loop(0, 5, relax4, us)
    ms = miss4(us)
    total_m = ms[0] + ms[1] + ms[2] + ms[3]
    total_w = ws[0] + ws[1] + ws[2] + ws[3]
    sum_r = jnp.sum(jnp.where(zlow & real, total_m, 0.0))
    sum_i = jnp.sum(jnp.where(zlow & ~real, total_m, 0.0))
    sum_w = jnp.sum(jnp.where(zlow & real, total_w, 0.0))
    numer = jnp.where(real, sum_r - SHIFT * sum_i, sum_i + SHIFT * sum_r)
    const = -numer / (jnp.full((16, 128), (1.0 + SHIFT * SHIFT), F32) * sum_w)
    for r in range(4):
        s4[r] = jnp.where(zlow, us[r] + const, 0.0)

    def spread4(j):
        x = ix - 4 + j
        inside = (x >= 0) & (x < 16)
        x = jnp.clip(x, 0, 15)
        k = x // 4
        t = jnp.where((slot == k) & inside, s4[x - 4 * k], 0.0)
        t = pltpu.roll(t, lax.rem(128 - k, 128), 1)
        t = t + lroll(t, 1)
        t = t + lroll(t, 2)
        t = t + lroll(t, 8)
        low, high = z_pair(t, lane, 16)
        t = 0.75 * t + 0.25 * jnp.where(zlow, low, high)
        down, up = y_pair(t)
        return 0.75 * t + 0.25 * jnp.where(ylow, down, up)

    wide = [spread4(j) for j in range(9)]
    for j in range(7):
        at = ix + j
        fix = 0.75 * wide[j + 1] + 0.25 * jnp.where(xlow, wide[j], wide[j + 2])
        fix = jnp.where((at >= 3) & (at < 19), fix, 0.0)
        ub3[at] = ub3[at] + fix

    def sweep3(_):
        new = [relaxed3(ub3, ix + j) for j in range(1, 6)]
        for j in range(1, 6):
            ub3[ix + j] = new[j - 1]

    repeat(0, 2, sweep3)
    for j in range(1, 6):
        e3[j - 1, pl.ds(8, 16), :] = ub3[ix + j]

    lane8 = lanes(8)
    lane24 = lanes(24)
    zero24 = jnp.zeros((24, 128), F32)
    for c in range(2):
        u2[c, 0] = zero16
        u2[c, 5] = zero16
    win2 = Window(src2, gain2, 0.0625, 1, functools.partial(near2, lane))
    keep2 = [block_mask(16, lane, ix * 4 - 6 + 4 * b, iy * 4 - 6) for b in range(4)]
    for b in range(4):
        win2.start(b, keep2[b], u2)
    a_low = lane8 % 2 == 0
    b_low = lane8 // 4 % 2 == 0
    h_low = lane8 // 2 % 2 == 0

    def widen3(c):
        sides = []
        shift = jnp.where(c == 0, 4, 124)
        for yl in range(2):
            pick = (lane8 // 4 % 2 == c) & (lane8 % 2 == yl)
            ups, downs = [], []
            for bb in range(5):
                t = jnp.where(pick, e3[bb, pl.ds(iy + 5, 8), :], 0.0)
                t = t + lroll(t, 1 - 2 * yl)
                t = t + pltpu.roll(t, shift, 1)
                low, high = z_pair(t, lane8, 8)
                t = 0.75 * t + 0.25 * jnp.where(b_low, low, high)
                ups.append(lroll(t, 2))
                downs.append(lroll(t, -2))
            cells = [ups[0]]
            cells += [jnp.where(h_low, downs[b], ups[b + 1]) for b in range(4)]
            cells += [downs[4]]
            blocks = []
            for b in range(1, 5):
                low = lroll(jnp.where(a_low, cells[b - 1], cells[b]), -2)
                high = lroll(jnp.where(a_low, cells[b], cells[b + 1]), 2)
                blocks.append(0.75 * cells[b] + 0.25 * jnp.where(h_low, low, high))
            sides.append(blocks)
        for b in range(4):
            t0, t1 = sides[0][b], sides[1][b]
            wide2[c, b, pl.ds(0, 8, 4), :] = 0.75 * t0 + 0.25 * sroll(t1, 1)
            wide2[c, b, pl.ds(1, 8, 4), :] = 0.75 * t0 + 0.25 * t1
            wide2[c, b, pl.ds(2, 8, 4), :] = 0.75 * t1 + 0.25 * t0
            wide2[c, b, pl.ds(3, 8, 4), :] = 0.75 * t1 + 0.25 * sroll(t0, -1)

    repeat(0, 2, widen3)

    def sweep2(i):
        add = jnp.where(i == 0, F32(1), F32(0))
        new = [win2.relaxed(b, u2) for b in range(4)]
        for b in range(4):
            for c in range(2):
                fix = wide2[c, b, pl.ds(6, 16), :] * (keep2[b] * add)
                u2[c, b + 1] = new[b][c] + fix

    repeat(0, 3, sweep2)

    slot4 = lane % 4

    def widen2(at, b, xl):
        for c in range(2):
            t = jnp.where(slot4 == xl, u2[c, b + 1], 0.0)
            t = lroll(t, -xl) if xl else t
            t = t + lroll(t, 1)
            t = t + lroll(t, 2)
            low, high = z_pair(t, lane, 4)
            cell1[c, at] = 0.75 * t + 0.25 * jnp.where(slot4 < 2, low, high)

    def widen_block(b):
        for xl in range(4):
            widen2(4 * b - 3 + xl, b, xl)

    widen2(0, 0, 3)
    repeat(1, 3, widen_block)
    widen2(9, 3, 0)
    lane_even = lane % 2 == 0

    def mix2(q):
        for c in range(2):
            side = jnp.where(lane_even, cell1[c, q - 1], cell1[c, q + 1])
            t = 0.75 * cell1[c, q] + 0.25 * side
            wide1[c, q, pl.ds(0, 16, 2), :] = 0.75 * t + 0.25 * sroll(t, 1)
            wide1[c, q, pl.ds(1, 16, 2), :] = 0.75 * t + 0.25 * sroll(t, -1)

    repeat(1, 9, mix2, 8)
    for c in range(2):
        ua1[c, 1] = zero24
        ua1[c, 10] = zero24
    inside1 = row_mask(24, iy * 8 - 8, 128)

    def correct1(q):
        keep = inside1 * scalar_mask(ix * 4 - 3 + q, 64)
        for c in range(2):
            ua1[c, q + 1] = ub1[c, q + 1] + wide1[c, q, pl.ds(4, 24), :] * keep

    repeat(1, 9, correct1, 4)
    win1 = Window(src1, gain1, 0.25, 1, functools.partial(near1, lane24))

    repeat(1, 9, lambda q: win1.relax(q, ua1, ut1), 8)
    repeat(2, 8, lambda q: win1.relax(q, ut1, ua1), 6)

    def widen1(q):
        for c in range(2):
            t = ua1[c, q + 1, pl.ds(5, 16), :]
            up, down = lroll(t, 1), lroll(t, -1)
            for p in range(2):
                v = jnp.where(lane_even, t, up) if p == 0 else jnp.where(lane_even, down, t)
                low, high = z_pair(v, lane, 2)
                v = 0.75 * v + 0.25 * jnp.where(lane_even, low, high)
                wide0[c, 2 * q + p, pl.ds(0, 16, 2), :] = 0.75 * v + 0.25 * sroll(v, 1)
                wide0[c, 2 * q + p, pl.ds(1, 16, 2), :] = 0.75 * v + 0.25 * sroll(v, -1)

    repeat(2, 8, widen1, 3)
    inside0 = row_mask(24, iy * 16 - 3, 256)

    def correct0(at):
        for c in range(2):
            low = wide0[c, at - 1, pl.ds(3, 24), :]
            mid = wide0[c, at, pl.ds(3, 24), :]
            high = wide0[c, at + 1, pl.ds(3, 24), :]
            for child, side in ((0, low), (1, high)):
                x = 2 * at - 9 + child
                keep = inside0 * scalar_mask(ix * 16 - 3 + x, 256)
                ua0[c, x] = ub0[c, x] + (0.75 * mid + 0.25 * side) * keep

    repeat(5, 15, correct0, 2)
    win0 = Window(src0, gain0, 1.0, 0, functools.partial(near0, lane24))
    repeat(2, 20, lambda x: win0.relax(x, ua0, ut0), 6)

    def finish0(x):
        new = win0.relaxed(x + 3, ut0)
        for c in range(2):
            ua0[c, x + 3] = new[c]
            out[c, x] = ua0[c, x + 3, pl.ds(3, 16), :]

    repeat(0, 16, finish0, 4)


def call(kernel, name, out_shape, scratch, *args, micros=2):
    vmem = pl.BlockSpec(memory_space=pltpu.VMEM)
    return pl.pallas_call(
        kernel,
        name=name,
        out_shape=[jax.ShapeDtypeStruct(shape, F32) for shape in out_shape],
        in_specs=[pl.BlockSpec(memory_space=pltpu.SMEM)] + [vmem] * (len(args) - 1),
        out_specs=[vmem] * len(out_shape),
        scratch_shapes=[pltpu.VMEM(shape, F32) for shape in scratch],
        cost_estimate=pl.CostEstimate(
            flops=0, bytes_accessed=micros * 3_500_000, transcendentals=0
        ),
        compiler_params=pltpu.CompilerParams(vmem_limit_bytes=40 * 1024 * 1024),
    )(*args)


BOTH = ("gx", "gy")


def partners(axis, first):
    counts = [lax.axis_size(name) for name in BOTH]
    along = BOTH.index(axis)
    pairs = []
    for i in range(counts[0]):
        for j in range(counts[1]):
            place = [i, j]
            other = ((place[along] + first) ^ 1) - first
            if 0 <= other < counts[along]:
                place[along] = other
            else:
                place[1 - along] ^= 1
            pairs.append((i * counts[1] + j, place[0] * counts[1] + place[1]))
    return pairs


def trade(to_low, to_high, axis):
    even = lax.axis_index(axis) % 2 == 0
    if to_low is to_high:
        one = two = to_low
    else:
        one = jnp.where(even, to_high, to_low)
        two = jnp.where(even, to_low, to_high)
    one = lax.ppermute(one, BOTH, partners(axis, 0))
    two = lax.ppermute(two, BOTH, partners(axis, 1))
    return jnp.where(even, two, one), jnp.where(even, one, two)


def body(residual_in, wave_sq):
    ix = lax.axis_index("gx")
    iy = lax.axis_index("gy")
    idx = jnp.stack([ix, iy]).astype(jnp.int32)

    own = jnp.concatenate([residual_in, wave_sq[None]], axis=0)
    low, high = trade(own[:, :3], own[:, 13:], "gx")
    strip = jnp.concatenate([low, own, high], axis=1)
    low, high = trade(
        strip[:, :, :3].transpose(0, 2, 1, 3).reshape(9, 22, 128),
        strip[:, :, 13:].transpose(0, 2, 1, 3).reshape(9, 22, 128),
        "gy",
    )
    low = low.reshape(3, 3, 22, 128).transpose(0, 2, 1, 3)
    high = high.reshape(3, 3, 22, 128).transpose(0, 2, 1, 3)
    src0 = jnp.concatenate([low, strip, high, jnp.zeros((3, 22, 2, 128), F32)], axis=2)

    n0 = (2, 22, 24, 128)
    n1 = (2, 12, 24, 128)
    own1, gain0, first0 = call(
        down0_kernel, "down0", [(3, 4, 8, 128), n0, n0], [n0, (3, 8, 24, 128)], idx, src0
    )
    low, high = trade(own1[:, :3], own1[:, 1:], "gx")
    strip = jnp.concatenate([low, own1, high], axis=1)
    low, high = trade(strip, strip, "gy")
    src1 = jnp.concatenate([low, strip, high], axis=2)

    part, own2, gain1, first1 = call(
        down1_kernel,
        "down1",
        [(64, 8, 128), (3, 2, 8, 128), (2, 10, 24, 128), n1],
        [n1, (3, 10, 24, 128), (2, 2, 8, 128), (2, 4, 8, 128), (2, 4, 8, 128)],
        idx,
        src1,
    )
    part = part.reshape(256, 2, 128)
    flat = lax.all_to_all(part, ("gx", "gy"), 0, 0).reshape(512, 128)
    low, high = trade(own2[:, 1:], own2[:, :1], "gx")
    strip = jnp.concatenate([low, own2, high], axis=1)
    low, high = trade(strip[:, :, 4:], strip[:, :, :4], "gy")
    src2 = jnp.concatenate([low, strip, high], axis=2)

    wide = (22, 16, 128)
    return call(
        up_kernel,
        "up",
        [(2, 16, 16, 128)],
        [wide, wide, wide, wide, wide, wide]
        + [(4, 16, 128), (4, 16, 128), (4, 16, 128), (5, 32, 128)]
        + [(2, 4, 16, 128), (2, 6, 16, 128), (2, 4, 32, 128)]
        + [(2, 10, 16, 128), n1, n1, (2, 10, 32, 128), (2, 16, 32, 128), n0, n0],
        idx,
        src0,
        gain0,
        first0,
        src1,
        gain1,
        first1,
        src2,
        flat,
        micros=10,
    )[0]


def solution(mesh):
    placed = (P(None, "gx", "gy", None), P("gx", "gy", None))
    return jax.shard_map(
        body, mesh=mesh, in_specs=placed, out_specs=P(None, "gx", "gy", None), check_vma=False
    )
```

```python
import functools

import jax
import jax.numpy as jnp
from jax import lax
from jax.experimental import pallas as pl
from jax.experimental.pallas import tpu as pltpu
from jax.sharding import PartitionSpec as P

OMEGA = 0.6
SHIFT = 0.5
F32 = jnp.float32


def lroll(v, shift):
    return pltpu.roll(v, shift % v.shape[1], 1)


def sroll(v, shift):
    return pltpu.roll(v, shift % v.shape[0], 0)


def lanes(rows):
    return lax.broadcasted_iota(jnp.int32, (rows, 128), 1)


def sublanes(rows):
    return lax.broadcasted_iota(jnp.int32, (rows, 128), 0)


def row_mask(rows, first, count):
    place = sublanes(rows) + first
    return jnp.where((place >= 0) & (place < count), F32(1), F32(0))


def block_mask(rows, lane, x_first, y_first):
    x = lane % 4 + x_first
    y = sublanes(rows) + y_first
    return jnp.where((x >= 0) & (x < 64) & (y >= 0) & (y < 64), F32(1), F32(0))


def scalar_mask(place, count):
    return jnp.where((place >= 0) & (place < count), F32(1), F32(0))


def z_pair(v, lane, step):
    low = jnp.where(lane >= step, lroll(v, step), 0.0)
    high = jnp.where(lane < 128 - step, lroll(v, -step), 0.0)
    return low, high


def z_sum(v, lane, step):
    low, high = z_pair(v, lane, step)
    return low + high


def y_sum(v):
    return sroll(v, 1) + sroll(v, -1)


def inverse(w, scale, keep):
    real = 6.0 * scale - w
    imag = SHIFT * w
    factor = (OMEGA * keep) / (real * real + imag * imag)
    return real * factor, -imag * factor


def misfit(f, w, v, nb, scale):
    (fr, fi), (vr, vi), (nr, ni) = f, v, nb
    mr = fr - scale * (6.0 * vr - nr) + w * (vr + SHIFT * vi)
    mi = fi - scale * (6.0 * vi - ni) + w * (vi - SHIFT * vr)
    return mr, mi


def cmul(g, m):
    return g[0] * m[0] - g[1] * m[1], g[0] * m[1] + g[1] * m[0]


def repeat(low, high, step, unroll=1):
    def run(i, carry):
        step(i)
        return carry

    lax.fori_loop(low, high, run, 0, unroll=unroll)


class Window:
    def __init__(self, src, gain, scale, pad, neighbours):
        self.src, self.gain, self.scale, self.pad = src, gain, scale, pad
        self.neighbours = neighbours

    def start(self, row, keep, out):
        w = self.src[2, row]
        g = inverse(w, self.scale, keep)
        self.gain[0, row], self.gain[1, row] = g
        u = cmul(g, (self.src[0, row], self.src[1, row]))
        out[0, row + self.pad], out[1, row + self.pad] = u

    def misfit(self, row, field):
        at = row + self.pad
        v = (field[0, at], field[1, at])
        nb = tuple(self.neighbours(field, c, at, v[c]) for c in range(2))
        f = (self.src[0, row], self.src[1, row])
        return v, misfit(f, self.src[2, row], v, nb, self.scale)

    def relaxed(self, row, field):
        v, m = self.misfit(row, field)
        d = cmul((self.gain[0, row], self.gain[1, row]), m)
        return v[0] + d[0], v[1] + d[1]

    def relax(self, row, field, out):
        at = row + self.pad
        out[0, at], out[1, at] = self.relaxed(row, field)


def near0(lane, ref, c, at, v):
    return ref[c, at - 1] + ref[c, at + 1] + y_sum(v) + z_sum(v, lane, 1)


def near1(lane, ref, c, at, v):
    low = lroll(ref[c, at - 1] + v, -1)
    high = lroll(v + ref[c, at + 1], 1)
    return jnp.where(lane % 2 == 0, low, high) + y_sum(v) + z_sum(v, lane, 2)


def near2(lane, ref, c, at, v):
    slot = lane % 4
    low = jnp.where(slot == 0, lroll(ref[c, at - 1], -3), lroll(v, 1))
    high = jnp.where(slot == 3, lroll(ref[c, at + 1], 3), lroll(v, -1))
    return low + high + y_sum(v) + z_sum(v, lane, 4)


def level0(src, gain, first, ix, iy):
    lane = lanes(24)
    win = Window(src, gain, 1.0, 0, functools.partial(near0, lane))
    inside = row_mask(24, iy * 16 - 3, 256)
    repeat(0, 22, lambda x: win.start(x, inside * scalar_mask(ix * 16 - 3 + x, 256), first), 2)
    return win, inside


def down0_kernel(idx, src, out, gain, ub, ua, tmp):
    ix, iy = idx[0], idx[1]
    win, _ = level0(src, gain, ua, ix, iy)
    repeat(1, 21, lambda x: win.relax(x, ua, ub), 10)
    for c in range(2):
        for x in (0, 21):
            ub[c, x] = jnp.zeros((24, 128), F32)
    lane = lanes(8)
    even = lane % 2 == 0

    def halve(q):
        rows = []
        for half in range(2):
            x = 4 * q + 3 + 2 * half
            _, m0 = win.misfit(x, ub)
            _, m1 = win.misfit(x + 1, ub)
            parts = (m0[0] + m1[0], m0[1] + m1[1], src[2, x] + src[2, x + 1])
            got = []
            for c in range(3):
                tmp[c, 2 * q + half] = parts[c]
                t = tmp[c, 2 * q + half, pl.ds(3, 8, 2)] + tmp[c, 2 * q + half, pl.ds(4, 8, 2)]
                got.append(0.125 * (t + lroll(t, -1)))
            rows.append(got)
        for c in range(3):
            out[c, q] = jnp.where(even, rows[0][c], lroll(rows[1][c], 1))

    repeat(0, 4, halve, 2)


def down1_kernel(idx, src, out, src2, gain, ub, ua, tmp, gain2, va, vb):
    ix, iy = idx[0], idx[1]
    lane24 = lanes(24)
    zero24 = jnp.zeros((24, 128), F32)
    for buf in (ua, ub):
        for c in range(2):
            buf[c, 0] = zero24
            buf[c, 11] = zero24
    win = Window(src, gain, 0.25, 1, functools.partial(near1, lane24))
    inside = row_mask(24, iy * 8 - 8, 128)
    repeat(0, 10, lambda q: win.start(q, inside * scalar_mask(ix * 4 - 3 + q, 64), ua), 10)
    repeat(0, 10, lambda q: win.relax(q, ua, ub), 10)
    lane = lanes(8)
    corner = lane % 4 == 0

    def halve(q):
        _, m = win.misfit(q, ub)
        parts = (m[0], m[1], src[2, q])
        for c in range(3):
            t = parts[c]
            tmp[c, q] = (t + lroll(t, -1)) + (lroll(t, -2) + lroll(t, -3))

    repeat(1, 9, halve, 8)

    def gather(b):
        for c in range(3):
            packed = jnp.zeros((8, 128), F32)
            for j in range(4):
                q = 4 * b + 1 + j
                t = tmp[c, q, pl.ds(4, 8, 2), :] + tmp[c, q, pl.ds(5, 8, 2), :]
                t = jnp.where(corner, 0.125 * t, 0.0)
                packed = packed + (lroll(t, j) if j else t)
            src2[c, b] = packed

    for b in range(2):
        gather(b)
    for buf in (va, vb):
        for c in range(2):
            buf[c, 0] = jnp.zeros((8, 128), F32)
            buf[c, 3] = jnp.zeros((8, 128), F32)
    win2 = Window(src2, gain2, 0.0625, 1, functools.partial(near2, lane))
    for b in range(2):
        win2.start(b, block_mask(8, lane, ix * 4 - 2 + 4 * b, iy * 4 - 2), va)
    for b in range(2):
        win2.relax(b, va, vb)
    m = [win2.misfit(b, vb)[1] for b in range(2)]

    def third(v0, v1, moves):
        total = jnp.zeros((1, 128), F32)
        for v, slot, move in ((v0, 2, -2), (v1, 0, 2)):
            t = (v + lroll(v, -1)) + (lroll(v, -4) + lroll(v, -5))
            t = 0.125 * jnp.where(lane % 8 == slot, t + sroll(t, -1), 0.0)
            for extra in moves:
                total = total + lroll(t[2:3], move + extra) + lroll(t[4:5], move + extra + 1)
        return total

    field = third(m[0][0], m[1][0], (0,)) + third(m[0][1], m[1][1], (4,))
    wave = third(src2[2, 0], src2[2, 1], (0, 4))
    pair = jnp.concatenate([field, wave] * 4, axis=0)

    def spread(i):
        out[i] = pair

    repeat(0, 64, spread, 8)


def swap(v, real):
    return jnp.where(real, lroll(v, -4), lroll(v, 4))


def up_kernel(
    idx, src0, gain0, ub0, src1, gain1, ub1, src2, flat, out,
    f3, w3, ga3, gb3, ua3, ub3, f4, w4, s4, e3, gain2, u2, wide2, cell1, ua1, ut1, wide1, wide0, ua0, ut0,
):
    ix, iy = idx[0], idx[1]
    lane = lanes(16)
    real = lane // 4 % 2 == 0
    sign = jnp.where(real, F32(SHIFT), F32(-SHIFT))
    xlow = lane // 2 % 2 == 0
    ylow = lane % 2 == 0
    zlow = lane // 8 % 2 == 0
    slot = lane % 4
    row = sublanes(16)
    zero16 = jnp.zeros((16, 128), F32)

    def y_pair(v):
        return jnp.where(row >= 1, sroll(v, 1), 0.0), jnp.where(row < 15, sroll(v, -1), 0.0)

    def packed_gain(w, scale):
        gr, gi = inverse(w, scale, 1.0)
        return gr, jnp.where(real, -gi, gi)

    def packed_misfit(f, w, v, nb, scale):
        return f - scale * (6.0 * v - nb) + w * (v + sign * swap(v, real))

    for at in (0, 1, 2, 19, 20, 21):
        for ref in (f3, w3, ga3, gb3):
            ref[at] = zero16
        for ref in (ua3, ub3):
            ref[at] = zero16
    for j in range(5):
        e3[j] = jnp.zeros((32, 128), F32)

    def start3(x):
        at = x + 3
        f3[at] = flat[pl.ds(32 * x, 16, 2), :]
        w = flat[pl.ds(32 * x + 1, 16, 2), :]
        w3[at] = w
        ga, gb = packed_gain(w, 1.0 / 64)
        ga3[at], gb3[at] = ga, gb
        ua3[at] = ga * f3[at] + gb * swap(f3[at], real)

    def miss3(ref, at):
        v = ref[at]
        down, up = y_pair(v)
        xs = jnp.where(xlow, lroll(ref[at - 1] + v, -2), lroll(v + ref[at + 1], 2))
        ys = jnp.where(ylow, lroll(v + down, -1), lroll(v + up, 1))
        return v, packed_misfit(f3[at], w3[at], v, xs + ys + z_sum(v, lane, 8), 1.0 / 64)

    def relaxed3(ref, at):
        v, m = miss3(ref, at)
        return v + ga3[at] * m + gb3[at] * swap(m, real)

    def relax3(at):
        ub3[at] = relaxed3(ua3, at)

    repeat(0, 16, start3, 8)
    repeat(3, 19, relax3, 8)

    first, second = (slot == 0) & zlow, (slot == 0) & ~zlow

    def eighth(v, k):
        v = 0.125 * ((v + lroll(v, -1)) + (lroll(v, -2) + lroll(v, -3)))
        low = jnp.where(first, v, 0.0)
        return (lroll(low, k) if k else low) + lroll(jnp.where(second, v, 0.0), k - 8)

    def halve3(r):
        f, w = zero16, zero16
        for k in range(4):
            at = 4 * k + r + 3
            f = f + eighth(miss3(ub3, at)[1], k)
            w = w + eighth(w3[at], k)
        f4[r], w4[r] = f, w

    repeat(0, 4, halve3, 1)
    fs = [f4[r] for r in range(4)]
    ws = [w4[r] for r in range(4)]
    gs = [packed_gain(w, 1.0 / 256) for w in ws]

    swapped = [swap(f, real) for f in fs]

    def near4(us):
        low = jnp.where(slot >= 1, lroll(us[3], 1), 0.0)
        high = jnp.where(slot < 3, lroll(us[0], -1), 0.0)
        wide = [low, *us, high]
        nbs = []
        for r in range(4):
            down, up = y_pair(us[r])
            nbs.append(wide[r] + wide[r + 2] + down + up + z_sum(us[r], lane, 16))
        return nbs

    def miss4(f, w, v, other, nb, turn):
        return f - (6.0 * v - nb) * (1.0 / 256) + w * (v + turn * other)

    def relax4(_, both):
        us, vs = both
        nus, nvs = near4(us), near4(vs)
        new = []
        for r in range(4):
            m = miss4(fs[r], ws[r], us[r], vs[r], nus[r], sign)
            n = miss4(swapped[r], ws[r], vs[r], us[r], nvs[r], -sign)
            ga, gb = gs[r]
            new.append((us[r] + ga * m + gb * n, vs[r] + ga * n - gb * m))
        return tuple(x for x, _ in new), tuple(x for _, x in new)

    us = tuple(g[0] * f + g[1] * h for g, f, h in zip(gs, fs, swapped))
    vs = tuple(g[0] * h - g[1] * f for g, f, h in zip(gs, fs, swapped))
    us, vs = lax.fori_loop(0, 5, relax4, (us, vs))
    nus = near4(us)
    ms = [miss4(fs[r], ws[r], us[r], vs[r], nus[r], sign) for r in range(4)]
    total_m = ms[0] + ms[1] + ms[2] + ms[3]
    total_w = ws[0] + ws[1] + ws[2] + ws[3]
    sum_r = jnp.sum(jnp.where(zlow & real, total_m, 0.0))
    sum_i = jnp.sum(jnp.where(zlow & ~real, total_m, 0.0))
    sum_w = jnp.sum(jnp.where(zlow & real, total_w, 0.0))
    numer = jnp.where(real, sum_r - SHIFT * sum_i, sum_i + SHIFT * sum_r)
    const = -numer / (jnp.full((16, 128), (1.0 + SHIFT * SHIFT), F32) * sum_w)
    for r in range(4):
        s4[r] = jnp.where(zlow, us[r] + const, 0.0)

    def spread4(j):
        x = ix - 4 + j
        inside = (x >= 0) & (x < 16)
        x = jnp.clip(x, 0, 15)
        k = x // 4
        t = jnp.where((slot == k) & inside, s4[x - 4 * k], 0.0)
        t = [pltpu.roll(t, lax.rem(128 - k + d, 128), 1) for d in range(4)]
        t = (t[0] + t[1]) + (t[2] + t[3])
        above = lroll(jnp.where(lane < 112, t, 0.0), 16)
        below = lroll(jnp.where(lane >= 16, t, 0.0), -8)
        t = 0.75 * (t + lroll(t, 8)) + 0.25 * (above + below)
        down, up = y_pair(t)
        return 0.75 * t + 0.25 * jnp.where(ylow, down, up)

    wide = [spread4(j) for j in range(9)]
    for j in range(7):
        at = ix + j
        fix = 0.75 * wide[j + 1] + 0.25 * jnp.where(xlow, wide[j], wide[j + 2])
        fix = jnp.where((at >= 3) & (at < 19), fix, 0.0)
        ub3[at] = ub3[at] + fix

    def sweep3(_):
        new = [relaxed3(ub3, ix + j) for j in range(1, 6)]
        for j in range(1, 6):
            ub3[ix + j] = new[j - 1]

    repeat(0, 2, sweep3, 2)
    for j in range(1, 6):
        e3[j - 1, pl.ds(8, 16), :] = ub3[ix + j]

    lane8 = lanes(8)
    lane24 = lanes(24)
    zero24 = jnp.zeros((24, 128), F32)
    for c in range(2):
        u2[c, 0] = zero16
        u2[c, 5] = zero16
    win2 = Window(src2, gain2, 0.0625, 1, functools.partial(near2, lane))
    keep2 = [block_mask(16, lane, ix * 4 - 6 + 4 * b, iy * 4 - 6) for b in range(4)]
    for b in range(4):
        win2.start(b, keep2[b], u2)
    a_low = lane8 % 2 == 0
    h_low = lane8 // 2 % 2 == 0

    def widen3(c):
        sides = []
        for yl in range(2):
            pick = (lane8 // 4 % 2 == c) & (lane8 % 2 == yl)
            ups, downs = [], []
            for bb in range(5):
                t = jnp.where(pick, e3[bb, pl.ds(iy + 5, 8), :], 0.0)
                t = t + lroll(t, 1 - 2 * yl)
                above = lroll(jnp.where(lane8 < 120, t, 0.0), 8 - 4 * c)
                below = lroll(jnp.where(lane8 >= 8, t, 0.0), -4 - 4 * c)
                t = 0.75 * (t + lroll(t, 4 - 8 * c)) + 0.25 * (above + below)
                ups.append(lroll(t, 2))
                downs.append(lroll(t, -2))
            cells = [ups[0]]
            cells += [jnp.where(h_low, downs[b], ups[b + 1]) for b in range(4)]
            cells += [downs[4]]
            blocks = []
            for b in range(1, 5):
                low = lroll(jnp.where(a_low, cells[b - 1], cells[b]), -2)
                high = lroll(jnp.where(a_low, cells[b], cells[b + 1]), 2)
                blocks.append(0.75 * cells[b] + 0.25 * jnp.where(h_low, low, high))
            sides.append(blocks)
        for b in range(4):
            t0, t1 = sides[0][b], sides[1][b]
            wide2[c, b, pl.ds(0, 8, 4), :] = 0.75 * t0 + 0.25 * sroll(t1, 1)
            wide2[c, b, pl.ds(1, 8, 4), :] = 0.75 * t0 + 0.25 * t1
            wide2[c, b, pl.ds(2, 8, 4), :] = 0.75 * t1 + 0.25 * t0
            wide2[c, b, pl.ds(3, 8, 4), :] = 0.75 * t1 + 0.25 * sroll(t0, -1)

    for c in range(2):
        widen3(c)

    def sweep2(i):
        add = jnp.where(i == 0, F32(1), F32(0))
        new = [win2.relaxed(b, u2) for b in range(4)]
        for b in range(4):
            for c in range(2):
                fix = wide2[c, b, pl.ds(6, 16), :] * (keep2[b] * add)
                u2[c, b + 1] = new[b][c] + fix

    repeat(0, 3, sweep2, 3)


    def widen2(at, b, xl):
        for c in range(2):
            t = jnp.where(slot == xl, u2[c, b + 1], 0.0)
            t = lroll(t, -xl) if xl else t
            t = t + lroll(t, 1)
            above = lroll(jnp.where(lane < 124, t, 0.0), 4)
            below = lroll(jnp.where(lane >= 4, t, 0.0), -2)
            cell1[c, at] = 0.75 * (t + lroll(t, 2)) + 0.25 * (above + below)

    for at in range(10):
        widen2(at, (at + 3) // 4, (at + 3) % 4)
    lane_even = lane % 2 == 0

    def mix2(q):
        for c in range(2):
            side = jnp.where(lane_even, cell1[c, q - 1], cell1[c, q + 1])
            t = 0.75 * cell1[c, q] + 0.25 * side
            wide1[c, q, pl.ds(0, 16, 2), :] = 0.75 * t + 0.25 * sroll(t, 1)
            wide1[c, q, pl.ds(1, 16, 2), :] = 0.75 * t + 0.25 * sroll(t, -1)

    repeat(1, 9, mix2, 8)
    for c in range(2):
        ua1[c, 1] = zero24
        ua1[c, 10] = zero24
    inside1 = row_mask(24, iy * 8 - 8, 128)

    def correct1(q):
        keep = inside1 * scalar_mask(ix * 4 - 3 + q, 64)
        for c in range(2):
            ua1[c, q + 1] = ub1[c, q + 1] + wide1[c, q, pl.ds(4, 24), :] * keep

    repeat(1, 9, correct1, 4)
    win1 = Window(src1, gain1, 0.25, 1, functools.partial(near1, lane24))

    repeat(1, 9, lambda q: win1.relax(q, ua1, ut1), 8)
    repeat(2, 8, lambda q: win1.relax(q, ut1, ua1), 6)

    def widen1(q):
        for c in range(2):
            t = ua1[c, q + 1, pl.ds(5, 16), :]
            for p in range(2):
                v = jnp.where(lane_even, t, 0.0) if p == 0 else jnp.where(lane_even, 0.0, t)
                above = lroll(jnp.where(lane < 126, v, 0.0), 2 - p)
                below = lroll(jnp.where(lane >= 2, v, 0.0), -1 - p)
                v = 0.75 * (v + lroll(v, 1 - 2 * p)) + 0.25 * (above + below)
                wide0[c, 2 * q + p, pl.ds(0, 16, 2), :] = 0.75 * v + 0.25 * sroll(v, 1)
                wide0[c, 2 * q + p, pl.ds(1, 16, 2), :] = 0.75 * v + 0.25 * sroll(v, -1)

    repeat(2, 8, widen1, 6)
    inside0 = row_mask(24, iy * 16 - 3, 256)

    def correct0(at):
        for c in range(2):
            low = wide0[c, at - 1, pl.ds(3, 24), :]
            mid = wide0[c, at, pl.ds(3, 24), :]
            high = wide0[c, at + 1, pl.ds(3, 24), :]
            for child, side in ((0, low), (1, high)):
                x = 2 * at - 9 + child
                keep = inside0 * scalar_mask(ix * 16 - 3 + x, 256)
                ua0[c, x] = ub0[c, x] + (0.75 * mid + 0.25 * side) * keep

    repeat(5, 15, correct0, 5)
    win0 = Window(src0, gain0, 1.0, 0, functools.partial(near0, lane24))
    repeat(2, 20, lambda x: win0.relax(x, ua0, ut0), 9)

    def finish0(x):
        new = win0.relaxed(x + 3, ut0)
        for c in range(2):
            ua0[c, x + 3] = new[c]
            out[c, x] = ua0[c, x + 3, pl.ds(3, 16), :]

    repeat(0, 16, finish0, 8)


def call(kernel, name, out_shape, scratch, *args, micros=2):
    vmem = pl.BlockSpec(memory_space=pltpu.VMEM)
    return pl.pallas_call(
        kernel,
        name=name,
        out_shape=[jax.ShapeDtypeStruct(shape, F32) for shape in out_shape],
        in_specs=[pl.BlockSpec(memory_space=pltpu.SMEM)] + [vmem] * (len(args) - 1),
        out_specs=[vmem] * len(out_shape),
        scratch_shapes=[pltpu.VMEM(shape, F32) for shape in scratch],
        cost_estimate=pl.CostEstimate(
            flops=0, bytes_accessed=micros * 3_500_000, transcendentals=0
        ),
        compiler_params=pltpu.CompilerParams(vmem_limit_bytes=40 * 1024 * 1024),
    )(*args)


BOTH = ("gx", "gy")


def partners(axis, first):
    counts = [lax.axis_size(name) for name in BOTH]
    along = BOTH.index(axis)
    pairs = []
    for i in range(counts[0]):
        for j in range(counts[1]):
            place = [i, j]
            other = ((place[along] + first) ^ 1) - first
            if 0 <= other < counts[along]:
                place[along] = other
            else:
                place[1 - along] ^= 1
            pairs.append((i * counts[1] + j, place[0] * counts[1] + place[1]))
    return pairs


def trade(to_low, to_high, axis):
    even = lax.axis_index(axis) % 2 == 0
    if to_low is to_high:
        one = two = to_low
    else:
        one = jnp.where(even, to_high, to_low)
        two = jnp.where(even, to_low, to_high)
    one = lax.ppermute(one, BOTH, partners(axis, 0))
    two = lax.ppermute(two, BOTH, partners(axis, 1))
    return jnp.where(even, two, one), jnp.where(even, one, two)


def body(residual_in, wave_sq):
    ix = lax.axis_index("gx")
    iy = lax.axis_index("gy")
    idx = jnp.stack([ix, iy]).astype(jnp.int32)

    own = jnp.concatenate([residual_in, wave_sq[None]], axis=0)
    low, high = trade(own[:, :3], own[:, 13:], "gx")
    strip = jnp.concatenate([low, own, high], axis=1)
    low, high = trade(
        strip[:, :, :3].transpose(0, 2, 1, 3).reshape(9, 22, 128),
        strip[:, :, 13:].transpose(0, 2, 1, 3).reshape(9, 22, 128),
        "gy",
    )
    low = low.reshape(3, 3, 22, 128).transpose(0, 2, 1, 3)
    high = high.reshape(3, 3, 22, 128).transpose(0, 2, 1, 3)
    src0 = jnp.concatenate([low, strip, high, jnp.zeros((3, 22, 2, 128), F32)], axis=2)

    n0 = (2, 22, 24, 128)
    n1 = (2, 12, 24, 128)
    own1, gain0, first0 = call(
        down0_kernel, "down0", [(3, 4, 8, 128), n0, n0], [n0, (3, 8, 24, 128)], idx, src0
    )
    low, high = trade(own1[:, :3], own1[:, 1:], "gx")
    strip = jnp.concatenate([low, own1, high], axis=1)
    low, high = trade(strip, strip, "gy")
    src1 = jnp.concatenate([low, strip, high], axis=2)

    part, own2, gain1, first1 = call(
        down1_kernel,
        "down1",
        [(64, 8, 128), (3, 2, 8, 128), (2, 10, 24, 128), n1],
        [n1, (3, 10, 24, 128), (2, 2, 8, 128), (2, 4, 8, 128), (2, 4, 8, 128)],
        idx,
        src1,
    )
    part = part.reshape(256, 2, 128)
    flat = lax.all_to_all(part, ("gx", "gy"), 0, 0).reshape(512, 128)
    low, high = trade(own2[:, 1:], own2[:, :1], "gx")
    strip = jnp.concatenate([low, own2, high], axis=1)
    low, high = trade(strip[:, :, 4:], strip[:, :, :4], "gy")
    src2 = jnp.concatenate([low, strip, high], axis=2)

    wide = (22, 16, 128)
    return call(
        up_kernel,
        "up",
        [(2, 16, 16, 128)],
        [wide, wide, wide, wide, wide, wide]
        + [(4, 16, 128), (4, 16, 128), (4, 16, 128), (5, 32, 128)]
        + [(2, 4, 16, 128), (2, 6, 16, 128), (2, 4, 32, 128)]
        + [(2, 10, 16, 128), n1, n1, (2, 10, 32, 128), (2, 16, 32, 128), n0, n0],
        idx,
        src0,
        gain0,
        first0,
        src1,
        gain1,
        first1,
        src2,
        flat,
        micros=10,
    )[0]


def solution(mesh):
    placed = (P(None, "gx", "gy", None), P("gx", "gy", None))
    return jax.shard_map(
        body, mesh=mesh, in_specs=placed, out_specs=P(None, "gx", "gy", None), check_vma=False
    )
```

```python
import functools

import jax
import jax.numpy as jnp
from jax import lax
from jax.experimental import pallas as pl
from jax.experimental.pallas import tpu as pltpu
from jax.sharding import PartitionSpec as P

OMEGA = 0.6
SHIFT = 0.5
F32 = jnp.float32


def lroll(v, shift):
    return pltpu.roll(v, shift % v.shape[1], 1)


def sroll(v, shift):
    return pltpu.roll(v, shift % v.shape[0], 0)


def lanes(rows):
    return lax.broadcasted_iota(jnp.int32, (rows, 128), 1)


def sublanes(rows):
    return lax.broadcasted_iota(jnp.int32, (rows, 128), 0)


def row_mask(rows, first, count):
    place = sublanes(rows) + first
    return jnp.where((place >= 0) & (place < count), F32(1), F32(0))


def block_mask(rows, lane, x_first, y_first):
    x = lane % 4 + x_first
    y = sublanes(rows) + y_first
    return jnp.where((x >= 0) & (x < 64) & (y >= 0) & (y < 64), F32(1), F32(0))


def scalar_mask(place, count):
    return jnp.where((place >= 0) & (place < count), F32(1), F32(0))


def z_pair(v, lane, step):
    low = jnp.where(lane >= step, lroll(v, step), 0.0)
    high = jnp.where(lane < 128 - step, lroll(v, -step), 0.0)
    return low, high


def z_sum(v, lane, step):
    low, high = z_pair(v, lane, step)
    return low + high


def y_sum(v):
    return sroll(v, 1) + sroll(v, -1)


def inverse(w, scale, keep):
    real = 6.0 * scale - w
    imag = SHIFT * w
    factor = (OMEGA * keep) / (real * real + imag * imag)
    return real * factor, -imag * factor


def misfit(f, w, v, nb, scale):
    (fr, fi), (vr, vi), (nr, ni) = f, v, nb
    mr = fr - scale * (6.0 * vr - nr) + w * (vr + SHIFT * vi)
    mi = fi - scale * (6.0 * vi - ni) + w * (vi - SHIFT * vr)
    return mr, mi


def cmul(g, m):
    return g[0] * m[0] - g[1] * m[1], g[0] * m[1] + g[1] * m[0]


def repeat(low, high, step, unroll=1):
    def run(i, carry):
        step(i)
        return carry

    lax.fori_loop(low, high, run, 0, unroll=unroll)


class Window:
    def __init__(self, src, gain, scale, pad, neighbours):
        self.src, self.gain, self.scale, self.pad = src, gain, scale, pad
        self.neighbours = neighbours

    def start(self, row, keep, out):
        w = self.src[2, row]
        g = inverse(w, self.scale, keep)
        self.gain[0, row], self.gain[1, row] = g
        u = cmul(g, (self.src[0, row], self.src[1, row]))
        out[0, row + self.pad], out[1, row + self.pad] = u

    def misfit(self, row, field):
        at = row + self.pad
        v = (field[0, at], field[1, at])
        nb = tuple(self.neighbours(field, c, at, v[c]) for c in range(2))
        f = (self.src[0, row], self.src[1, row])
        return v, misfit(f, self.src[2, row], v, nb, self.scale)

    def relaxed(self, row, field):
        v, m = self.misfit(row, field)
        d = cmul((self.gain[0, row], self.gain[1, row]), m)
        return v[0] + d[0], v[1] + d[1]

    def relax(self, row, field, out):
        at = row + self.pad
        out[0, at], out[1, at] = self.relaxed(row, field)


def near0(lane, ref, c, at, v):
    return ref[c, at - 1] + ref[c, at + 1] + y_sum(v) + z_sum(v, lane, 1)


def near1(lane, ref, c, at, v):
    low = lroll(ref[c, at - 1] + v, -1)
    high = lroll(v + ref[c, at + 1], 1)
    return jnp.where(lane % 2 == 0, low, high) + y_sum(v) + z_sum(v, lane, 2)


def near2(lane, ref, c, at, v):
    slot = lane % 4
    low = jnp.where(slot == 0, lroll(ref[c, at - 1], -3), lroll(v, 1))
    high = jnp.where(slot == 3, lroll(ref[c, at + 1], 3), lroll(v, -1))
    return low + high + y_sum(v) + z_sum(v, lane, 4)


def level0(src, gain, first, ix, iy):
    lane = lanes(24)
    win = Window(src, gain, 1.0, 0, functools.partial(near0, lane))
    inside = row_mask(24, iy * 16 - 3, 256)
    repeat(0, 22, lambda x: win.start(x, inside * scalar_mask(ix * 16 - 3 + x, 256), first), 2)
    return win, inside


def down0_kernel(idx, src, out, gain, ub, ua, tmp):
    ix, iy = idx[0], idx[1]
    win, _ = level0(src, gain, ua, ix, iy)
    repeat(1, 21, lambda x: win.relax(x, ua, ub), 10)
    for c in range(2):
        for x in (0, 21):
            ub[c, x] = jnp.zeros((24, 128), F32)
    lane = lanes(8)
    even = lane % 2 == 0

    def halve(q):
        rows = []
        for half in range(2):
            x = 4 * q + 3 + 2 * half
            _, m0 = win.misfit(x, ub)
            _, m1 = win.misfit(x + 1, ub)
            parts = (m0[0] + m1[0], m0[1] + m1[1], src[2, x] + src[2, x + 1])
            got = []
            for c in range(3):
                tmp[c, 2 * q + half] = parts[c]
                t = tmp[c, 2 * q + half, pl.ds(3, 8, 2)] + tmp[c, 2 * q + half, pl.ds(4, 8, 2)]
                got.append(0.125 * (t + lroll(t, -1)))
            rows.append(got)
        for c in range(3):
            out[c, q] = jnp.where(even, rows[0][c], lroll(rows[1][c], 1))

    repeat(0, 4, halve, 2)


def down1_kernel(idx, src, out, src2, gain, ub, ua, tmp, gain2, va, vb):
    ix, iy = idx[0], idx[1]
    lane24 = lanes(24)
    zero24 = jnp.zeros((24, 128), F32)
    for buf in (ua, ub):
        for c in range(2):
            buf[c, 0] = zero24
            buf[c, 11] = zero24
    win = Window(src, gain, 0.25, 1, functools.partial(near1, lane24))
    inside = row_mask(24, iy * 8 - 8, 128)
    repeat(0, 10, lambda q: win.start(q, inside * scalar_mask(ix * 4 - 3 + q, 64), ua), 10)
    repeat(0, 10, lambda q: win.relax(q, ua, ub), 10)
    lane = lanes(8)
    corner = lane % 4 == 0

    def halve(q):
        _, m = win.misfit(q, ub)
        parts = (m[0], m[1], src[2, q])
        for c in range(3):
            t = parts[c]
            tmp[c, q] = (t + lroll(t, -1)) + (lroll(t, -2) + lroll(t, -3))

    repeat(1, 9, halve, 8)

    def gather(b):
        for c in range(3):
            packed = jnp.zeros((8, 128), F32)
            for j in range(4):
                q = 4 * b + 1 + j
                t = tmp[c, q, pl.ds(4, 8, 2), :] + tmp[c, q, pl.ds(5, 8, 2), :]
                t = jnp.where(corner, 0.125 * t, 0.0)
                packed = packed + (lroll(t, j) if j else t)
            src2[c, b] = packed

    for b in range(2):
        gather(b)
    for buf in (va, vb):
        for c in range(2):
            buf[c, 0] = jnp.zeros((8, 128), F32)
            buf[c, 3] = jnp.zeros((8, 128), F32)
    win2 = Window(src2, gain2, 0.0625, 1, functools.partial(near2, lane))
    for b in range(2):
        win2.start(b, block_mask(8, lane, ix * 4 - 2 + 4 * b, iy * 4 - 2), va)
    for b in range(2):
        win2.relax(b, va, vb)
    m = [win2.misfit(b, vb)[1] for b in range(2)]

    def third(v0, v1, moves):
        total = jnp.zeros((1, 128), F32)
        for v, slot, move in ((v0, 2, -2), (v1, 0, 2)):
            t = (v + lroll(v, -1)) + (lroll(v, -4) + lroll(v, -5))
            t = 0.125 * jnp.where(lane % 8 == slot, t + sroll(t, -1), 0.0)
            for extra in moves:
                total = total + lroll(t[2:3], move + extra) + lroll(t[4:5], move + extra + 1)
        return total

    field = third(m[0][0], m[1][0], (0,)) + third(m[0][1], m[1][1], (4,))
    wave = third(src2[2, 0], src2[2, 1], (0, 4))
    pair = jnp.concatenate([field, wave] * 4, axis=0)

    def spread(i):
        out[i] = pair

    repeat(0, 64, spread, 8)


def swap(v, real):
    return jnp.where(real, lroll(v, -4), lroll(v, 4))


def up_kernel(
    idx, src0, gain0, ub0, src1, gain1, ub1, src2, flat, out,
    f3, w3, ga3, gb3, ua3, ub3, f4, w4, s4, e3, gain2, u2, wide2, cell1, ua1, ut1, wide1, wide0, ua0, ut0,
):
    ix, iy = idx[0], idx[1]
    lane = lanes(16)
    real = lane // 4 % 2 == 0
    sign = jnp.where(real, F32(SHIFT), F32(-SHIFT))
    xlow = lane // 2 % 2 == 0
    ylow = lane % 2 == 0
    zlow = lane // 8 % 2 == 0
    slot = lane % 4
    row = sublanes(16)
    zero16 = jnp.zeros((16, 128), F32)

    def y_pair(v):
        return jnp.where(row >= 1, sroll(v, 1), 0.0), jnp.where(row < 15, sroll(v, -1), 0.0)

    def packed_gain(w, scale):
        gr, gi = inverse(w, scale, 1.0)
        return gr, jnp.where(real, -gi, gi)

    def packed_misfit(f, w, v, nb, scale):
        return f - scale * (6.0 * v - nb) + w * (v + sign * swap(v, real))

    for at in (0, 1, 2, 19, 20, 21):
        for ref in (f3, w3, ga3, gb3):
            ref[at] = zero16
        for ref in (ua3, ub3):
            ref[at] = zero16
    for j in range(5):
        e3[j] = jnp.zeros((32, 128), F32)

    def start3(x):
        at = x + 3
        f3[at] = flat[pl.ds(32 * x, 16, 2), :]
        w = flat[pl.ds(32 * x + 1, 16, 2), :]
        w3[at] = w
        ga, gb = packed_gain(w, 1.0 / 64)
        ga3[at], gb3[at] = ga, gb
        ua3[at] = ga * f3[at] + gb * swap(f3[at], real)

    def miss3(ref, at):
        v = ref[at]
        down, up = y_pair(v)
        xs = jnp.where(xlow, lroll(ref[at - 1] + v, -2), lroll(v + ref[at + 1], 2))
        ys = jnp.where(ylow, lroll(v + down, -1), lroll(v + up, 1))
        return v, packed_misfit(f3[at], w3[at], v, xs + ys + z_sum(v, lane, 8), 1.0 / 64)

    def relaxed3(ref, at):
        v, m = miss3(ref, at)
        return v + ga3[at] * m + gb3[at] * swap(m, real)

    def relax3(at):
        ub3[at] = relaxed3(ua3, at)

    repeat(0, 16, start3, 8)
    repeat(3, 19, relax3, 8)

    first, second = (slot == 0) & zlow, (slot == 0) & ~zlow

    def eighth(v, k):
        v = 0.125 * ((v + lroll(v, -1)) + (lroll(v, -2) + lroll(v, -3)))
        low = jnp.where(first, v, 0.0)
        return (lroll(low, k) if k else low) + lroll(jnp.where(second, v, 0.0), k - 8)

    def halve3(r):
        f, w = zero16, zero16
        for k in range(4):
            at = 4 * k + r + 3
            f = f + eighth(miss3(ub3, at)[1], k)
            w = w + eighth(w3[at], k)
        f4[r], w4[r] = f, w

    repeat(0, 4, halve3, 1)
    fs = [f4[r] for r in range(4)]
    ws = [w4[r] for r in range(4)]
    gs = [packed_gain(w, 1.0 / 256) for w in ws]

    swapped = [swap(f, real) for f in fs]

    def near4(us):
        low = jnp.where(slot >= 1, lroll(us[3], 1), 0.0)
        high = jnp.where(slot < 3, lroll(us[0], -1), 0.0)
        wide = [low, *us, high]
        nbs = []
        for r in range(4):
            down, up = y_pair(us[r])
            nbs.append(wide[r] + wide[r + 2] + down + up + z_sum(us[r], lane, 16))
        return nbs

    def miss4(f, w, v, other, nb, turn):
        return f - (6.0 * v - nb) * (1.0 / 256) + w * (v + turn * other)

    def relax4(_, both):
        us, vs = both
        nus, nvs = near4(us), near4(vs)
        new = []
        for r in range(4):
            m = miss4(fs[r], ws[r], us[r], vs[r], nus[r], sign)
            n = miss4(swapped[r], ws[r], vs[r], us[r], nvs[r], -sign)
            ga, gb = gs[r]
            new.append((us[r] + ga * m + gb * n, vs[r] + ga * n - gb * m))
        return tuple(x for x, _ in new), tuple(x for _, x in new)

    us = tuple(g[0] * f + g[1] * h for g, f, h in zip(gs, fs, swapped))
    vs = tuple(g[0] * h - g[1] * f for g, f, h in zip(gs, fs, swapped))
    us, vs = lax.fori_loop(0, 5, relax4, (us, vs))
    nus = near4(us)
    ms = [miss4(fs[r], ws[r], us[r], vs[r], nus[r], sign) for r in range(4)]
    total_m = ms[0] + ms[1] + ms[2] + ms[3]
    total_w = ws[0] + ws[1] + ws[2] + ws[3]
    sum_r = jnp.sum(jnp.where(zlow & real, total_m, 0.0))
    sum_i = jnp.sum(jnp.where(zlow & ~real, total_m, 0.0))
    sum_w = jnp.sum(jnp.where(zlow & real, total_w, 0.0))
    numer = jnp.where(real, sum_r - SHIFT * sum_i, sum_i + SHIFT * sum_r)
    const = -numer / (jnp.full((16, 128), (1.0 + SHIFT * SHIFT), F32) * sum_w)
    for r in range(4):
        s4[r] = jnp.where(zlow, us[r] + const, 0.0)

    def spread4(j):
        x = ix - 4 + j
        inside = (x >= 0) & (x < 16)
        x = jnp.clip(x, 0, 15)
        k = x // 4
        t = jnp.where((slot == k) & inside, s4[x - 4 * k], 0.0)
        t = [pltpu.roll(t, lax.rem(128 - k + d, 128), 1) for d in range(4)]
        t = (t[0] + t[1]) + (t[2] + t[3])
        above = lroll(jnp.where(lane < 112, t, 0.0), 16)
        below = lroll(jnp.where(lane >= 16, t, 0.0), -8)
        t = 0.75 * (t + lroll(t, 8)) + 0.25 * (above + below)
        down, up = y_pair(t)
        return 0.75 * t + 0.25 * jnp.where(ylow, down, up)

    wide = [spread4(j) for j in range(9)]
    for j in range(7):
        at = ix + j
        fix = 0.75 * wide[j + 1] + 0.25 * jnp.where(xlow, wide[j], wide[j + 2])
        fix = jnp.where((at >= 3) & (at < 19), fix, 0.0)
        ub3[at] = ub3[at] + fix

    def sweep3(_):
        new = [relaxed3(ub3, ix + j) for j in range(1, 6)]
        for j in range(1, 6):
            ub3[ix + j] = new[j - 1]

    repeat(0, 2, sweep3, 2)
    for j in range(1, 6):
        e3[j - 1, pl.ds(8, 16), :] = ub3[ix + j]

    lane8 = lanes(8)
    lane24 = lanes(24)
    zero24 = jnp.zeros((24, 128), F32)
    for c in range(2):
        u2[c, 0] = zero16
        u2[c, 5] = zero16
    win2 = Window(src2, gain2, 0.0625, 1, functools.partial(near2, lane))
    keep2 = [block_mask(16, lane, ix * 4 - 6 + 4 * b, iy * 4 - 6) for b in range(4)]
    for b in range(4):
        win2.start(b, keep2[b], u2)
    a_low = lane8 % 2 == 0
    h_low = lane8 // 2 % 2 == 0

    def widen3(c):
        sides = []
        for yl in range(2):
            pick = (lane8 // 4 % 2 == c) & (lane8 % 2 == yl)
            ups, downs = [], []
            for bb in range(5):
                t = jnp.where(pick, e3[bb, pl.ds(iy + 5, 8), :], 0.0)
                t = t + lroll(t, 1 - 2 * yl)
                above = lroll(jnp.where(lane8 < 120, t, 0.0), 8 - 4 * c)
                below = lroll(jnp.where(lane8 >= 8, t, 0.0), -4 - 4 * c)
                t = 0.75 * (t + lroll(t, 4 - 8 * c)) + 0.25 * (above + below)
                ups.append(lroll(t, 2))
                downs.append(lroll(t, -2))
            cells = [ups[0]]
            cells += [jnp.where(h_low, downs[b], ups[b + 1]) for b in range(4)]
            cells += [downs[4]]
            blocks = []
            for b in range(1, 5):
                low = lroll(jnp.where(a_low, cells[b - 1], cells[b]), -2)
                high = lroll(jnp.where(a_low, cells[b], cells[b + 1]), 2)
                blocks.append(0.75 * cells[b] + 0.25 * jnp.where(h_low, low, high))
            sides.append(blocks)
        for b in range(4):
            t0, t1 = sides[0][b], sides[1][b]
            wide2[c, b, pl.ds(0, 8, 4), :] = 0.75 * t0 + 0.25 * sroll(t1, 1)
            wide2[c, b, pl.ds(1, 8, 4), :] = 0.75 * t0 + 0.25 * t1
            wide2[c, b, pl.ds(2, 8, 4), :] = 0.75 * t1 + 0.25 * t0
            wide2[c, b, pl.ds(3, 8, 4), :] = 0.75 * t1 + 0.25 * sroll(t0, -1)

    for c in range(2):
        widen3(c)

    def sweep2(i):
        add = jnp.where(i == 0, F32(1), F32(0))
        new = [win2.relaxed(b, u2) for b in range(4)]
        for b in range(4):
            for c in range(2):
                fix = wide2[c, b, pl.ds(6, 16), :] * (keep2[b] * add)
                u2[c, b + 1] = new[b][c] + fix

    repeat(0, 3, sweep2, 3)


    def widen2(at, b, xl):
        for c in range(2):
            t = jnp.where(slot == xl, u2[c, b + 1], 0.0)
            t = lroll(t, -xl) if xl else t
            t = t + lroll(t, 1)
            above = lroll(jnp.where(lane < 124, t, 0.0), 4)
            below = lroll(jnp.where(lane >= 4, t, 0.0), -2)
            cell1[c, at] = 0.75 * (t + lroll(t, 2)) + 0.25 * (above + below)

    for at in range(10):
        widen2(at, (at + 3) // 4, (at + 3) % 4)
    lane_even = lane % 2 == 0

    def mix2(q):
        for c in range(2):
            side = jnp.where(lane_even, cell1[c, q - 1], cell1[c, q + 1])
            t = 0.75 * cell1[c, q] + 0.25 * side
            wide1[c, q, pl.ds(0, 16, 2), :] = 0.75 * t + 0.25 * sroll(t, 1)
            wide1[c, q, pl.ds(1, 16, 2), :] = 0.75 * t + 0.25 * sroll(t, -1)

    repeat(1, 9, mix2, 8)
    for c in range(2):
        ua1[c, 1] = zero24
        ua1[c, 10] = zero24
    inside1 = row_mask(24, iy * 8 - 8, 128)

    def correct1(q):
        keep = inside1 * scalar_mask(ix * 4 - 3 + q, 64)
        for c in range(2):
            ua1[c, q + 1] = ub1[c, q + 1] + wide1[c, q, pl.ds(4, 24), :] * keep

    repeat(1, 9, correct1, 4)
    win1 = Window(src1, gain1, 0.25, 1, functools.partial(near1, lane24))

    repeat(1, 9, lambda q: win1.relax(q, ua1, ut1), 8)
    repeat(2, 8, lambda q: win1.relax(q, ut1, ua1), 6)

    def widen1(q):
        for c in range(2):
            t = ua1[c, q + 1, pl.ds(5, 16), :]
            for p in range(2):
                v = jnp.where(lane_even, t, 0.0) if p == 0 else jnp.where(lane_even, 0.0, t)
                above = lroll(jnp.where(lane < 126, v, 0.0), 2 - p)
                below = lroll(jnp.where(lane >= 2, v, 0.0), -1 - p)
                v = 0.75 * (v + lroll(v, 1 - 2 * p)) + 0.25 * (above + below)
                wide0[c, 2 * q + p, pl.ds(0, 16, 2), :] = 0.75 * v + 0.25 * sroll(v, 1)
                wide0[c, 2 * q + p, pl.ds(1, 16, 2), :] = 0.75 * v + 0.25 * sroll(v, -1)

    repeat(2, 8, widen1, 6)
    inside0 = row_mask(24, iy * 16 - 3, 256)

    def correct0(at):
        for c in range(2):
            low = wide0[c, at - 1, pl.ds(3, 24), :]
            mid = wide0[c, at, pl.ds(3, 24), :]
            high = wide0[c, at + 1, pl.ds(3, 24), :]
            for child, side in ((0, low), (1, high)):
                x = 2 * at - 9 + child
                keep = inside0 * scalar_mask(ix * 16 - 3 + x, 256)
                ua0[c, x] = ub0[c, x] + (0.75 * mid + 0.25 * side) * keep

    repeat(5, 15, correct0, 5)
    win0 = Window(src0, gain0, 1.0, 0, functools.partial(near0, lane24))
    repeat(2, 20, lambda x: win0.relax(x, ua0, ut0), 9)

    def finish0(x):
        new = win0.relaxed(x + 3, ut0)
        for c in range(2):
            ua0[c, x + 3] = new[c]
            out[c, x] = ua0[c, x + 3, pl.ds(3, 16), :]

    repeat(0, 16, finish0, 8)


def call(kernel, name, out_shape, scratch, *args, micros=2):
    vmem = pl.BlockSpec(memory_space=pltpu.VMEM)
    return pl.pallas_call(
        kernel,
        name=name,
        out_shape=[jax.ShapeDtypeStruct(shape, F32) for shape in out_shape],
        in_specs=[pl.BlockSpec(memory_space=pltpu.SMEM)] + [vmem] * (len(args) - 1),
        out_specs=[vmem] * len(out_shape),
        scratch_shapes=[pltpu.VMEM(shape, F32) for shape in scratch],
        cost_estimate=pl.CostEstimate(
            flops=0, bytes_accessed=micros * 3_500_000, transcendentals=0
        ),
        compiler_params=pltpu.CompilerParams(vmem_limit_bytes=40 * 1024 * 1024),
    )(*args)


BOTH = ("gx", "gy")


def partners(axis, first):
    counts = [lax.axis_size(name) for name in BOTH]
    along = BOTH.index(axis)
    pairs = []
    for i in range(counts[0]):
        for j in range(counts[1]):
            place = [i, j]
            other = ((place[along] + first) ^ 1) - first
            if 0 <= other < counts[along]:
                place[along] = other
            else:
                place[1 - along] ^= 1
            pairs.append((i * counts[1] + j, place[0] * counts[1] + place[1]))
    return pairs


def trade(to_low, to_high, axis, near=None):
    even = lax.axis_index(axis) % 2 == 0
    if to_low is to_high:
        one = two = to_low
    else:
        low, high = near or (to_low, to_high)
        one = jnp.where(even, high, low)
        two = jnp.where(even, to_low, to_high)
    two = lax.ppermute(two, BOTH, partners(axis, 1))
    one = lax.ppermute(one, BOTH, partners(axis, 0))
    one, two = lax.optimization_barrier((one, two))
    return jnp.where(even, two, one), jnp.where(even, one, two)


def body(residual_in, wave_sq):
    ix = lax.axis_index("gx")
    iy = lax.axis_index("gy")
    idx = jnp.stack([ix, iy]).astype(jnp.int32)

    own = jnp.concatenate([residual_in, wave_sq[None]], axis=0)
    near_f, near_w = lax.optimization_barrier((residual_in, wave_sq))
    near = jnp.concatenate([near_f, near_w[None]], axis=0)
    low, high = trade(own[:, :3], own[:, 13:], "gx", (near[:, :3], near[:, 13:]))
    strip = jnp.concatenate([low, own, high], axis=1)
    low, high = trade(
        strip[:, :, :3].transpose(0, 2, 1, 3).reshape(9, 22, 128),
        strip[:, :, 13:].transpose(0, 2, 1, 3).reshape(9, 22, 128),
        "gy",
    )
    low = low.reshape(3, 3, 22, 128).transpose(0, 2, 1, 3)
    high = high.reshape(3, 3, 22, 128).transpose(0, 2, 1, 3)
    src0 = jnp.concatenate([low, strip, high, jnp.zeros((3, 22, 2, 128), F32)], axis=2)

    n0 = (2, 22, 24, 128)
    n1 = (2, 12, 24, 128)
    own1, gain0, first0 = call(
        down0_kernel, "down0", [(3, 4, 8, 128), n0, n0], [n0, (3, 8, 24, 128)], idx, src0
    )
    low, high = trade(own1[:, :3], own1[:, 1:], "gx")
    strip = jnp.concatenate([low, own1, high], axis=1)
    low, high = trade(strip, strip, "gy")
    src1 = jnp.concatenate([low, strip, high], axis=2)

    part, own2, gain1, first1 = call(
        down1_kernel,
        "down1",
        [(64, 8, 128), (3, 2, 8, 128), (2, 10, 24, 128), n1],
        [n1, (3, 10, 24, 128), (2, 2, 8, 128), (2, 4, 8, 128), (2, 4, 8, 128)],
        idx,
        src1,
    )
    part = part.reshape(256, 2, 128)
    flat = lax.all_to_all(part, ("gx", "gy"), 0, 0).reshape(512, 128)
    low, high = trade(own2[:, 1:], own2[:, :1], "gx")
    strip = jnp.concatenate([low, own2, high], axis=1)
    low, high = trade(strip[:, :, 4:], strip[:, :, :4], "gy")
    src2 = jnp.concatenate([low, strip, high], axis=2)

    wide = (22, 16, 128)
    return call(
        up_kernel,
        "up",
        [(2, 16, 16, 128)],
        [wide, wide, wide, wide, wide, wide]
        + [(4, 16, 128), (4, 16, 128), (4, 16, 128), (5, 32, 128)]
        + [(2, 4, 16, 128), (2, 6, 16, 128), (2, 4, 32, 128)]
        + [(2, 10, 16, 128), n1, n1, (2, 10, 32, 128), (2, 16, 32, 128), n0, n0],
        idx,
        src0,
        gain0,
        first0,
        src1,
        gain1,
        first1,
        src2,
        flat,
        micros=10,
    )[0]


def solution(mesh):
    placed = (P(None, "gx", "gy", None), P("gx", "gy", None))
    return jax.shard_map(
        body, mesh=mesh, in_specs=placed, out_specs=P(None, "gx", "gy", None), check_vma=False
    )
```

```python
import functools

import jax
import jax.numpy as jnp
from jax import lax
from jax.experimental import pallas as pl
from jax.experimental.pallas import tpu as pltpu
from jax.sharding import PartitionSpec as P

OMEGA = 0.6
SHIFT = 0.5
F32 = jnp.float32


def lroll(v, shift):
    return pltpu.roll(v, shift % v.shape[1], 1)


def sroll(v, shift):
    return pltpu.roll(v, shift % v.shape[0], 0)


def lanes(rows):
    return lax.broadcasted_iota(jnp.int32, (rows, 128), 1)


def sublanes(rows):
    return lax.broadcasted_iota(jnp.int32, (rows, 128), 0)


def row_mask(rows, first, count):
    place = sublanes(rows) + first
    return jnp.where((place >= 0) & (place < count), F32(1), F32(0))


def block_mask(rows, lane, x_first, y_first):
    x = lane % 4 + x_first
    y = sublanes(rows) + y_first
    return jnp.where((x >= 0) & (x < 64) & (y >= 0) & (y < 64), F32(1), F32(0))


def scalar_mask(place, count):
    return jnp.where((place >= 0) & (place < count), F32(1), F32(0))


def z_pair(v, lane, step):
    low = jnp.where(lane >= step, lroll(v, step), 0.0)
    high = jnp.where(lane < 128 - step, lroll(v, -step), 0.0)
    return low, high


def z_sum(v, lane, step):
    low, high = z_pair(v, lane, step)
    return low + high


def y_sum(v):
    return sroll(v, 1) + sroll(v, -1)


def inverse(w, scale, keep):
    real = 6.0 * scale - w
    imag = SHIFT * w
    factor = (OMEGA * keep) / (real * real + imag * imag)
    return real * factor, -imag * factor


def misfit(f, w, v, nb, scale):
    (fr, fi), (vr, vi), (nr, ni) = f, v, nb
    mr = fr - scale * (6.0 * vr - nr) + w * (vr + SHIFT * vi)
    mi = fi - scale * (6.0 * vi - ni) + w * (vi - SHIFT * vr)
    return mr, mi


def cmul(g, m):
    return g[0] * m[0] - g[1] * m[1], g[0] * m[1] + g[1] * m[0]


def repeat(low, high, step, unroll=1):
    def run(i, carry):
        step(i)
        return carry

    lax.fori_loop(low, high, run, 0, unroll=unroll)


class Window:
    def __init__(self, src, gain, scale, pad, neighbours):
        self.src, self.gain, self.scale, self.pad = src, gain, scale, pad
        self.neighbours = neighbours

    def start(self, row, keep, out):
        w = self.src[2, row]
        g = inverse(w, self.scale, keep)
        self.gain[0, row], self.gain[1, row] = g
        u = cmul(g, (self.src[0, row], self.src[1, row]))
        out[0, row + self.pad], out[1, row + self.pad] = u

    def misfit(self, row, field):
        at = row + self.pad
        v = (field[0, at], field[1, at])
        nb = tuple(self.neighbours(field, c, at, v[c]) for c in range(2))
        f = (self.src[0, row], self.src[1, row])
        return v, misfit(f, self.src[2, row], v, nb, self.scale)

    def relaxed(self, row, field):
        v, m = self.misfit(row, field)
        d = cmul((self.gain[0, row], self.gain[1, row]), m)
        return v[0] + d[0], v[1] + d[1]

    def relax(self, row, field, out):
        at = row + self.pad
        out[0, at], out[1, at] = self.relaxed(row, field)


def near0(lane, ref, c, at, v):
    return ref[c, at - 1] + ref[c, at + 1] + y_sum(v) + z_sum(v, lane, 1)


def near1(lane, ref, c, at, v):
    low = lroll(ref[c, at - 1] + v, -1)
    high = lroll(v + ref[c, at + 1], 1)
    return jnp.where(lane % 2 == 0, low, high) + y_sum(v) + z_sum(v, lane, 2)


def near2(lane, ref, c, at, v):
    slot = lane % 4
    low = jnp.where(slot == 0, lroll(ref[c, at - 1], -3), lroll(v, 1))
    high = jnp.where(slot == 3, lroll(ref[c, at + 1], 3), lroll(v, -1))
    return low + high + y_sum(v) + z_sum(v, lane, 4)


def level0(src, gain, first, ix, iy):
    lane = lanes(24)
    win = Window(src, gain, 1.0, 0, functools.partial(near0, lane))
    inside = row_mask(24, iy * 16 - 3, 256)
    repeat(0, 22, lambda x: win.start(x, inside * scalar_mask(ix * 16 - 3 + x, 256), first), 2)
    return win, inside


def down0_kernel(idx, src, out, gain, ub, ua, tmp):
    ix, iy = idx[0], idx[1]
    win, _ = level0(src, gain, ua, ix, iy)
    repeat(1, 21, lambda x: win.relax(x, ua, ub), 20)
    for c in range(2):
        for x in (0, 21):
            ub[c, x] = jnp.zeros((24, 128), F32)
    lane = lanes(8)
    even = lane % 2 == 0

    def halve(q):
        rows = []
        for half in range(2):
            x = 4 * q + 3 + 2 * half
            _, m0 = win.misfit(x, ub)
            _, m1 = win.misfit(x + 1, ub)
            parts = (m0[0] + m1[0], m0[1] + m1[1], src[2, x] + src[2, x + 1])
            got = []
            for c in range(3):
                tmp[c, 2 * q + half] = parts[c]
                t = tmp[c, 2 * q + half, pl.ds(3, 8, 2)] + tmp[c, 2 * q + half, pl.ds(4, 8, 2)]
                got.append(0.125 * (t + lroll(t, -1)))
            rows.append(got)
        for c in range(3):
            out[c, q] = jnp.where(even, rows[0][c], lroll(rows[1][c], 1))

    repeat(0, 4, halve, 2)


def down1_kernel(idx, src, out, src2, gain, ub, ua, tmp, gain2, va, vb):
    ix, iy = idx[0], idx[1]
    lane24 = lanes(24)
    zero24 = jnp.zeros((24, 128), F32)
    for buf in (ua, ub):
        for c in range(2):
            buf[c, 0] = zero24
            buf[c, 11] = zero24
    win = Window(src, gain, 0.25, 1, functools.partial(near1, lane24))
    inside = row_mask(24, iy * 8 - 8, 128)
    repeat(0, 10, lambda q: win.start(q, inside * scalar_mask(ix * 4 - 3 + q, 64), ua), 10)
    repeat(0, 10, lambda q: win.relax(q, ua, ub), 10)
    lane = lanes(8)
    corner = lane % 4 == 0

    def halve(q):
        _, m = win.misfit(q, ub)
        parts = (m[0], m[1], src[2, q])
        for c in range(3):
            t = parts[c]
            tmp[c, q] = (t + lroll(t, -1)) + (lroll(t, -2) + lroll(t, -3))

    repeat(1, 9, halve, 8)

    def gather(b):
        for c in range(3):
            packed = jnp.zeros((8, 128), F32)
            for j in range(4):
                q = 4 * b + 1 + j
                t = tmp[c, q, pl.ds(4, 8, 2), :] + tmp[c, q, pl.ds(5, 8, 2), :]
                t = jnp.where(corner, 0.125 * t, 0.0)
                packed = packed + (lroll(t, j) if j else t)
            src2[c, b] = packed

    for b in range(2):
        gather(b)
    for buf in (va, vb):
        for c in range(2):
            buf[c, 0] = jnp.zeros((8, 128), F32)
            buf[c, 3] = jnp.zeros((8, 128), F32)
    win2 = Window(src2, gain2, 0.0625, 1, functools.partial(near2, lane))
    for b in range(2):
        win2.start(b, block_mask(8, lane, ix * 4 - 2 + 4 * b, iy * 4 - 2), va)
    for b in range(2):
        win2.relax(b, va, vb)
    m = [win2.misfit(b, vb)[1] for b in range(2)]

    def third(v0, v1, moves):
        total = jnp.zeros((1, 128), F32)
        for v, slot, move in ((v0, 2, -2), (v1, 0, 2)):
            t = (v + lroll(v, -1)) + (lroll(v, -4) + lroll(v, -5))
            t = 0.125 * jnp.where(lane % 8 == slot, t + sroll(t, -1), 0.0)
            for extra in moves:
                total = total + lroll(t[2:3], move + extra) + lroll(t[4:5], move + extra + 1)
        return total

    field = third(m[0][0], m[1][0], (0,)) + third(m[0][1], m[1][1], (4,))
    wave = third(src2[2, 0], src2[2, 1], (0, 4))
    pair = jnp.concatenate([field, wave] * 4, axis=0)

    def spread(i):
        out[i] = pair

    repeat(0, 64, spread, 8)


def swap(v, real):
    return jnp.where(real, lroll(v, -4), lroll(v, 4))


def up_kernel(
    idx, src0, gain0, ub0, src1, gain1, ub1, src2, shared, out,
    flat, f3, w3, ga3, gb3, ua3, ub3, f4, w4, s4, e3, gain2, u2, wide2, cell1, ua1, ut1, wide1, wide0, ua0, ut0,
):
    ix, iy = idx[0], idx[1]
    lane = lanes(16)
    real = lane // 4 % 2 == 0
    sign = jnp.where(real, F32(SHIFT), F32(-SHIFT))
    xlow = lane // 2 % 2 == 0
    ylow = lane % 2 == 0
    zlow = lane // 8 % 2 == 0
    slot = lane % 4
    row = sublanes(16)
    zero16 = jnp.zeros((16, 128), F32)

    def y_pair(v):
        return jnp.where(row >= 1, sroll(v, 1), 0.0), jnp.where(row < 15, sroll(v, -1), 0.0)

    def packed_gain(w, scale):
        gr, gi = inverse(w, scale, 1.0)
        return gr, jnp.where(real, -gi, gi)

    def packed_misfit(f, w, v, nb, scale):
        return f - scale * (6.0 * v - nb) + w * (v + sign * swap(v, real))

    flat[pl.ds(0, 512), :] = shared[...]

    for at in (0, 1, 2, 19, 20, 21):
        for ref in (f3, w3, ga3, gb3):
            ref[at] = zero16
        for ref in (ua3, ub3):
            ref[at] = zero16
    for j in range(5):
        e3[j] = jnp.zeros((32, 128), F32)

    def start3(x):
        at = x + 3
        f3[at] = flat[pl.ds(32 * x, 16, 2), :]
        w = flat[pl.ds(32 * x + 1, 16, 2), :]
        w3[at] = w
        ga, gb = packed_gain(w, 1.0 / 64)
        ga3[at], gb3[at] = ga, gb
        ua3[at] = ga * f3[at] + gb * swap(f3[at], real)

    def miss3(ref, at):
        v = ref[at]
        down, up = y_pair(v)
        xs = jnp.where(xlow, lroll(ref[at - 1] + v, -2), lroll(v + ref[at + 1], 2))
        ys = jnp.where(ylow, lroll(v + down, -1), lroll(v + up, 1))
        return v, packed_misfit(f3[at], w3[at], v, xs + ys + z_sum(v, lane, 8), 1.0 / 64)

    def relaxed3(ref, at):
        v, m = miss3(ref, at)
        return v + ga3[at] * m + gb3[at] * swap(m, real)

    def relax3(at):
        ub3[at] = relaxed3(ua3, at)

    repeat(0, 16, start3, 8)
    repeat(3, 19, relax3, 8)

    first, second = (slot == 0) & zlow, (slot == 0) & ~zlow

    def eighth(v, k):
        v = 0.125 * ((v + lroll(v, -1)) + (lroll(v, -2) + lroll(v, -3)))
        low = jnp.where(first, v, 0.0)
        return (lroll(low, k) if k else low) + lroll(jnp.where(second, v, 0.0), k - 8)

    def halve3(r):
        f, w = zero16, zero16
        for k in range(4):
            at = 4 * k + r + 3
            f = f + eighth(miss3(ub3, at)[1], k)
            w = w + eighth(w3[at], k)
        f4[r], w4[r] = f, w

    repeat(0, 4, halve3, 1)
    fs = [f4[r] for r in range(4)]
    ws = [w4[r] for r in range(4)]
    gs = [packed_gain(w, 1.0 / 256) for w in ws]

    swapped = [swap(f, real) for f in fs]

    def near4(us):
        low = jnp.where(slot >= 1, lroll(us[3], 1), 0.0)
        high = jnp.where(slot < 3, lroll(us[0], -1), 0.0)
        wide = [low, *us, high]
        nbs = []
        for r in range(4):
            down, up = y_pair(us[r])
            nbs.append(wide[r] + wide[r + 2] + down + up + z_sum(us[r], lane, 16))
        return nbs

    def miss4(f, w, v, other, nb, turn):
        return f - (6.0 * v - nb) * (1.0 / 256) + w * (v + turn * other)

    def relax4(_, both):
        us, vs = both
        nus, nvs = near4(us), near4(vs)
        new = []
        for r in range(4):
            m = miss4(fs[r], ws[r], us[r], vs[r], nus[r], sign)
            n = miss4(swapped[r], ws[r], vs[r], us[r], nvs[r], -sign)
            ga, gb = gs[r]
            new.append((us[r] + ga * m + gb * n, vs[r] + ga * n - gb * m))
        return tuple(x for x, _ in new), tuple(x for _, x in new)

    us = tuple(g[0] * f + g[1] * h for g, f, h in zip(gs, fs, swapped))
    vs = tuple(g[0] * h - g[1] * f for g, f, h in zip(gs, fs, swapped))
    us, vs = lax.fori_loop(0, 5, relax4, (us, vs))
    nus = near4(us)
    ms = [miss4(fs[r], ws[r], us[r], vs[r], nus[r], sign) for r in range(4)]
    total_m = ms[0] + ms[1] + ms[2] + ms[3]
    total_w = ws[0] + ws[1] + ws[2] + ws[3]
    sum_r = jnp.sum(jnp.where(zlow & real, total_m, 0.0))
    sum_i = jnp.sum(jnp.where(zlow & ~real, total_m, 0.0))
    sum_w = jnp.sum(jnp.where(zlow & real, total_w, 0.0))
    numer = jnp.where(real, sum_r - SHIFT * sum_i, sum_i + SHIFT * sum_r)
    const = -numer / (jnp.full((16, 128), (1.0 + SHIFT * SHIFT), F32) * sum_w)
    for r in range(4):
        s4[r] = jnp.where(zlow, us[r] + const, 0.0)

    def spread4(j):
        x = ix - 4 + j
        inside = (x >= 0) & (x < 16)
        x = jnp.clip(x, 0, 15)
        k = x // 4
        t = jnp.where((slot == k) & inside, s4[x - 4 * k], 0.0)
        t = [pltpu.roll(t, lax.rem(128 - k + d, 128), 1) for d in range(4)]
        t = (t[0] + t[1]) + (t[2] + t[3])
        above = lroll(jnp.where(lane < 112, t, 0.0), 16)
        below = lroll(jnp.where(lane >= 16, t, 0.0), -8)
        t = 0.75 * (t + lroll(t, 8)) + 0.25 * (above + below)
        down, up = y_pair(t)
        return 0.75 * t + 0.25 * jnp.where(ylow, down, up)

    wide = [spread4(j) for j in range(9)]
    for j in range(7):
        at = ix + j
        fix = 0.75 * wide[j + 1] + 0.25 * jnp.where(xlow, wide[j], wide[j + 2])
        fix = jnp.where((at >= 3) & (at < 19), fix, 0.0)
        ub3[at] = ub3[at] + fix

    def sweep3(_):
        new = [relaxed3(ub3, ix + j) for j in range(1, 6)]
        for j in range(1, 6):
            ub3[ix + j] = new[j - 1]

    repeat(0, 2, sweep3, 2)
    for j in range(1, 6):
        e3[j - 1, pl.ds(8, 16), :] = ub3[ix + j]

    lane8 = lanes(8)
    lane24 = lanes(24)
    zero24 = jnp.zeros((24, 128), F32)
    for c in range(2):
        u2[c, 0] = zero16
        u2[c, 5] = zero16
    win2 = Window(src2, gain2, 0.0625, 1, functools.partial(near2, lane))
    keep2 = [block_mask(16, lane, ix * 4 - 6 + 4 * b, iy * 4 - 6) for b in range(4)]
    for b in range(4):
        win2.start(b, keep2[b], u2)
    a_low = lane8 % 2 == 0
    h_low = lane8 // 2 % 2 == 0

    def widen3(c):
        sides = []
        for yl in range(2):
            pick = (lane8 // 4 % 2 == c) & (lane8 % 2 == yl)
            ups, downs = [], []
            for bb in range(5):
                t = jnp.where(pick, e3[bb, pl.ds(iy + 5, 8), :], 0.0)
                t = t + lroll(t, 1 - 2 * yl)
                above = lroll(jnp.where(lane8 < 120, t, 0.0), 8 - 4 * c)
                below = lroll(jnp.where(lane8 >= 8, t, 0.0), -4 - 4 * c)
                t = 0.75 * (t + lroll(t, 4 - 8 * c)) + 0.25 * (above + below)
                ups.append(lroll(t, 2))
                downs.append(lroll(t, -2))
            cells = [ups[0]]
            cells += [jnp.where(h_low, downs[b], ups[b + 1]) for b in range(4)]
            cells += [downs[4]]
            blocks = []
            for b in range(1, 5):
                low = lroll(jnp.where(a_low, cells[b - 1], cells[b]), -2)
                high = lroll(jnp.where(a_low, cells[b], cells[b + 1]), 2)
                blocks.append(0.75 * cells[b] + 0.25 * jnp.where(h_low, low, high))
            sides.append(blocks)
        for b in range(4):
            t0, t1 = sides[0][b], sides[1][b]
            wide2[c, b, pl.ds(0, 8, 4), :] = 0.75 * t0 + 0.25 * sroll(t1, 1)
            wide2[c, b, pl.ds(1, 8, 4), :] = 0.75 * t0 + 0.25 * t1
            wide2[c, b, pl.ds(2, 8, 4), :] = 0.75 * t1 + 0.25 * t0
            wide2[c, b, pl.ds(3, 8, 4), :] = 0.75 * t1 + 0.25 * sroll(t0, -1)

    for c in range(2):
        widen3(c)

    def sweep2(i):
        add = jnp.where(i == 0, F32(1), F32(0))
        new = [win2.relaxed(b, u2) for b in range(4)]
        for b in range(4):
            for c in range(2):
                fix = wide2[c, b, pl.ds(6, 16), :] * (keep2[b] * add)
                u2[c, b + 1] = new[b][c] + fix

    repeat(0, 3, sweep2, 3)


    def widen2(at, b, xl):
        for c in range(2):
            t = jnp.where(slot == xl, u2[c, b + 1], 0.0)
            t = lroll(t, -xl) if xl else t
            t = t + lroll(t, 1)
            above = lroll(jnp.where(lane < 124, t, 0.0), 4)
            below = lroll(jnp.where(lane >= 4, t, 0.0), -2)
            cell1[c, at] = 0.75 * (t + lroll(t, 2)) + 0.25 * (above + below)

    for at in range(10):
        widen2(at, (at + 3) // 4, (at + 3) % 4)
    lane_even = lane % 2 == 0

    def mix2(q):
        for c in range(2):
            side = jnp.where(lane_even, cell1[c, q - 1], cell1[c, q + 1])
            t = 0.75 * cell1[c, q] + 0.25 * side
            wide1[c, q, pl.ds(0, 16, 2), :] = 0.75 * t + 0.25 * sroll(t, 1)
            wide1[c, q, pl.ds(1, 16, 2), :] = 0.75 * t + 0.25 * sroll(t, -1)

    repeat(1, 9, mix2, 8)
    for c in range(2):
        ua1[c, 1] = zero24
        ua1[c, 10] = zero24
    inside1 = row_mask(24, iy * 8 - 8, 128)

    def correct1(q):
        keep = inside1 * scalar_mask(ix * 4 - 3 + q, 64)
        for c in range(2):
            ua1[c, q + 1] = ub1[c, q + 1] + wide1[c, q, pl.ds(4, 24), :] * keep

    repeat(1, 9, correct1, 4)
    win1 = Window(src1, gain1, 0.25, 1, functools.partial(near1, lane24))

    repeat(1, 9, lambda q: win1.relax(q, ua1, ut1), 8)
    repeat(2, 8, lambda q: win1.relax(q, ut1, ua1), 6)

    def widen1(q):
        for c in range(2):
            t = ua1[c, q + 1, pl.ds(5, 16), :]
            for p in range(2):
                v = jnp.where(lane_even, t, 0.0) if p == 0 else jnp.where(lane_even, 0.0, t)
                above = lroll(jnp.where(lane < 126, v, 0.0), 2 - p)
                below = lroll(jnp.where(lane >= 2, v, 0.0), -1 - p)
                v = 0.75 * (v + lroll(v, 1 - 2 * p)) + 0.25 * (above + below)
                wide0[c, 2 * q + p, pl.ds(0, 16, 2), :] = 0.75 * v + 0.25 * sroll(v, 1)
                wide0[c, 2 * q + p, pl.ds(1, 16, 2), :] = 0.75 * v + 0.25 * sroll(v, -1)

    repeat(2, 8, widen1, 6)
    inside0 = row_mask(24, iy * 16 - 3, 256)

    def correct0(at):
        for c in range(2):
            low = wide0[c, at - 1, pl.ds(3, 24), :]
            mid = wide0[c, at, pl.ds(3, 24), :]
            high = wide0[c, at + 1, pl.ds(3, 24), :]
            for child, side in ((0, low), (1, high)):
                x = 2 * at - 9 + child
                keep = inside0 * scalar_mask(ix * 16 - 3 + x, 256)
                ua0[c, x] = ub0[c, x] + (0.75 * mid + 0.25 * side) * keep

    repeat(5, 15, correct0, 10)
    win0 = Window(src0, gain0, 1.0, 0, functools.partial(near0, lane24))
    repeat(2, 20, lambda x: win0.relax(x, ua0, ut0), 18)

    def finish0(x):
        new = win0.relaxed(x + 3, ut0)
        for c in range(2):
            ua0[c, x + 3] = new[c]
            out[c, x] = ua0[c, x + 3, pl.ds(3, 16), :]

    repeat(0, 16, finish0, 16)


def call(kernel, name, out_shape, scratch, *args, micros=2):
    vmem = pl.BlockSpec(memory_space=pltpu.VMEM)
    return pl.pallas_call(
        kernel,
        name=name,
        out_shape=[jax.ShapeDtypeStruct(shape, F32) for shape in out_shape],
        in_specs=[pl.BlockSpec(memory_space=pltpu.SMEM)] + [vmem] * (len(args) - 1),
        out_specs=[vmem] * len(out_shape),
        scratch_shapes=[pltpu.VMEM(shape, F32) for shape in scratch],
        cost_estimate=pl.CostEstimate(
            flops=0, bytes_accessed=micros * 3_500_000, transcendentals=0
        ),
        compiler_params=pltpu.CompilerParams(vmem_limit_bytes=40 * 1024 * 1024),
    )(*args)


BOTH = ("gx", "gy")


def partners(axis, first):
    counts = [lax.axis_size(name) for name in BOTH]
    along = BOTH.index(axis)
    pairs = []
    for i in range(counts[0]):
        for j in range(counts[1]):
            place = [i, j]
            other = ((place[along] + first) ^ 1) - first
            if 0 <= other < counts[along]:
                place[along] = other
            else:
                place[1 - along] ^= 1
            pairs.append((i * counts[1] + j, place[0] * counts[1] + place[1]))
    return pairs


def trade(to_low, to_high, axis, near=None):
    even = lax.axis_index(axis) % 2 == 0
    if to_low is to_high:
        one = two = to_low
    else:
        low, high = near or (to_low, to_high)
        one = jnp.where(even, high, low)
        two = jnp.where(even, to_low, to_high)
    two = lax.ppermute(two, BOTH, partners(axis, 1))
    one = lax.ppermute(one, BOTH, partners(axis, 0))
    one, two = lax.optimization_barrier((one, two))
    return jnp.where(even, two, one), jnp.where(even, one, two)


def body(residual_in, wave_sq):
    ix = lax.axis_index("gx")
    iy = lax.axis_index("gy")
    idx = jnp.stack([ix, iy]).astype(jnp.int32)

    own = jnp.concatenate([residual_in, wave_sq[None]], axis=0)
    near_f, near_w = lax.optimization_barrier((residual_in, wave_sq))
    near = jnp.concatenate([near_f, near_w[None]], axis=0)
    low, high = trade(own[:, :3], own[:, 13:], "gx", (near[:, :3], near[:, 13:]))
    strip = jnp.concatenate([low, own, high], axis=1)
    low, high = trade(
        strip[:, :, :3].transpose(0, 2, 1, 3).reshape(9, 22, 128),
        strip[:, :, 13:].transpose(0, 2, 1, 3).reshape(9, 22, 128),
        "gy",
    )
    low = low.reshape(3, 3, 22, 128).transpose(0, 2, 1, 3)
    high = high.reshape(3, 3, 22, 128).transpose(0, 2, 1, 3)
    src0 = jnp.concatenate([low, strip, high, jnp.zeros((3, 22, 2, 128), F32)], axis=2)

    n0 = (2, 22, 24, 128)
    n1 = (2, 12, 24, 128)
    own1, gain0, first0 = call(
        down0_kernel, "down0", [(3, 4, 8, 128), n0, n0], [n0, (3, 8, 24, 128)], idx, src0
    )
    low, high = trade(own1[:, :3], own1[:, 1:], "gx")
    strip = jnp.concatenate([low, own1, high], axis=1)
    low, high = trade(strip, strip, "gy")
    src1 = jnp.concatenate([low, strip, high], axis=2)

    part, own2, gain1, first1 = call(
        down1_kernel,
        "down1",
        [(64, 8, 128), (3, 2, 8, 128), (2, 10, 24, 128), n1],
        [n1, (3, 10, 24, 128), (2, 2, 8, 128), (2, 4, 8, 128), (2, 4, 8, 128)],
        idx,
        src1,
    )
    part = part.reshape(256, 2, 128)
    flat = lax.all_to_all(part, ("gx", "gy"), 0, 0).reshape(512, 128)
    low, high = trade(own2[:, 1:], own2[:, :1], "gx")
    strip = jnp.concatenate([low, own2, high], axis=1)
    low, high = trade(strip[:, :, 4:], strip[:, :, :4], "gy")
    src2 = jnp.concatenate([low, strip, high], axis=2)

    wide = (22, 16, 128)
    return call(
        up_kernel,
        "up",
        [(2, 16, 16, 128)],
        [(520, 128), wide, wide, wide, wide, wide, wide]
        + [(4, 16, 128), (4, 16, 128), (4, 16, 128), (5, 32, 128)]
        + [(2, 4, 16, 128), (2, 6, 16, 128), (2, 4, 40, 128)]
        + [(2, 10, 16, 128), n1, n1, (2, 10, 40, 128), (2, 16, 40, 128), n0, n0],
        idx,
        src0,
        gain0,
        first0,
        src1,
        gain1,
        first1,
        src2,
        flat,
        micros=10,
    )[0]


def solution(mesh):
    placed = (P(None, "gx", "gy", None), P("gx", "gy", None))
    return jax.shard_map(
        body, mesh=mesh, in_specs=placed, out_specs=P(None, "gx", "gy", None), check_vma=False
    )
```

```python
import functools

import jax
import jax.numpy as jnp
from jax import lax
from jax.experimental import pallas as pl
from jax.experimental.pallas import tpu as pltpu
from jax.sharding import PartitionSpec as P

OMEGA = 0.6
SHIFT = 0.5
F32 = jnp.float32


def lroll(v, shift):
    return pltpu.roll(v, shift % v.shape[1], 1)


def sroll(v, shift):
    return pltpu.roll(v, shift % v.shape[0], 0)


def lanes(rows):
    return lax.broadcasted_iota(jnp.int32, (rows, 128), 1)


def sublanes(rows):
    return lax.broadcasted_iota(jnp.int32, (rows, 128), 0)


def row_mask(rows, first, count):
    place = sublanes(rows) + first
    return jnp.where((place >= 0) & (place < count), F32(1), F32(0))


def block_mask(rows, lane, x_first, y_first):
    x = lane % 4 + x_first
    y = sublanes(rows) + y_first
    return jnp.where((x >= 0) & (x < 64) & (y >= 0) & (y < 64), F32(1), F32(0))


def scalar_mask(place, count):
    return jnp.where((place >= 0) & (place < count), F32(1), F32(0))


def z_pair(v, lane, step):
    low = jnp.where(lane >= step, lroll(v, step), 0.0)
    high = jnp.where(lane < 128 - step, lroll(v, -step), 0.0)
    return low, high


def z_sum(v, lane, step):
    low, high = z_pair(v, lane, step)
    return low + high


def y_sum(v):
    return sroll(v, 1) + sroll(v, -1)


def inverse(w, scale, keep):
    real = 6.0 * scale - w
    imag = SHIFT * w
    factor = (OMEGA * keep) / (real * real + imag * imag)
    return real * factor, -imag * factor


def misfit(f, w, v, nb, scale):
    (fr, fi), (vr, vi), (nr, ni) = f, v, nb
    mr = fr - scale * (6.0 * vr - nr) + w * (vr + SHIFT * vi)
    mi = fi - scale * (6.0 * vi - ni) + w * (vi - SHIFT * vr)
    return mr, mi


def cmul(g, m):
    return g[0] * m[0] - g[1] * m[1], g[0] * m[1] + g[1] * m[0]


def repeat(low, high, step, unroll=1):
    def run(i, carry):
        step(i)
        return carry

    lax.fori_loop(low, high, run, 0, unroll=unroll)


class Window:
    def __init__(self, src, gain, scale, pad, neighbours):
        self.src, self.gain, self.scale, self.pad = src, gain, scale, pad
        self.neighbours = neighbours

    def start(self, row, keep, out):
        w = self.src[2, row]
        g = inverse(w, self.scale, keep)
        self.gain[0, row], self.gain[1, row] = g
        u = cmul(g, (self.src[0, row], self.src[1, row]))
        out[0, row + self.pad], out[1, row + self.pad] = u

    def misfit(self, row, field):
        at = row + self.pad
        v = (field[0, at], field[1, at])
        nb = tuple(self.neighbours(field, c, at, v[c]) for c in range(2))
        f = (self.src[0, row], self.src[1, row])
        return v, misfit(f, self.src[2, row], v, nb, self.scale)

    def relaxed(self, row, field):
        v, m = self.misfit(row, field)
        d = cmul((self.gain[0, row], self.gain[1, row]), m)
        return v[0] + d[0], v[1] + d[1]

    def relax(self, row, field, out):
        at = row + self.pad
        out[0, at], out[1, at] = self.relaxed(row, field)


def near0(lane, ref, c, at, v):
    return ref[c, at - 1] + ref[c, at + 1] + y_sum(v) + z_sum(v, lane, 1)


def near1(lane, ref, c, at, v):
    low = lroll(ref[c, at - 1] + v, -1)
    high = lroll(v + ref[c, at + 1], 1)
    return jnp.where(lane % 2 == 0, low, high) + y_sum(v) + z_sum(v, lane, 2)


def near2(lane, ref, c, at, v):
    slot = lane % 4
    low = jnp.where(slot == 0, lroll(ref[c, at - 1], -3), lroll(v, 1))
    high = jnp.where(slot == 3, lroll(ref[c, at + 1], 3), lroll(v, -1))
    return low + high + y_sum(v) + z_sum(v, lane, 4)


def level0(src, gain, first, ix, iy):
    lane = lanes(24)
    win = Window(src, gain, 1.0, 0, functools.partial(near0, lane))
    inside = row_mask(24, iy * 16 - 3, 256)
    repeat(0, 22, lambda x: win.start(x, inside * scalar_mask(ix * 16 - 3 + x, 256), first), 2)
    return win, inside


def down0_kernel(idx, src, out, gain, ub, ua, tmp):
    ix, iy = idx[0], idx[1]
    win, _ = level0(src, gain, ua, ix, iy)
    repeat(1, 21, lambda x: win.relax(x, ua, ub), 20)
    for c in range(2):
        for x in (0, 21):
            ub[c, x] = jnp.zeros((24, 128), F32)
    lane = lanes(8)
    even = lane % 2 == 0

    def halve(q):
        rows = []
        for half in range(2):
            x = 4 * q + 3 + 2 * half
            _, m0 = win.misfit(x, ub)
            _, m1 = win.misfit(x + 1, ub)
            parts = (m0[0] + m1[0], m0[1] + m1[1], src[2, x] + src[2, x + 1])
            got = []
            for c in range(3):
                tmp[c, 2 * q + half] = parts[c]
                t = tmp[c, 2 * q + half, pl.ds(3, 8, 2)] + tmp[c, 2 * q + half, pl.ds(4, 8, 2)]
                got.append(0.125 * (t + lroll(t, -1)))
            rows.append(got)
        for c in range(3):
            out[c, q] = jnp.where(even, rows[0][c], lroll(rows[1][c], 1))

    repeat(0, 4, halve, 2)


def down1_kernel(idx, src, out, src2, gain, ub, ua, tmp, gain2, va, vb):
    ix, iy = idx[0], idx[1]
    lane24 = lanes(24)
    zero24 = jnp.zeros((24, 128), F32)
    for buf in (ua, ub):
        for c in range(2):
            buf[c, 0] = zero24
            buf[c, 11] = zero24
    win = Window(src, gain, 0.25, 1, functools.partial(near1, lane24))
    inside = row_mask(24, iy * 8 - 8, 128)
    repeat(0, 10, lambda q: win.start(q, inside * scalar_mask(ix * 4 - 3 + q, 64), ua), 10)
    repeat(0, 10, lambda q: win.relax(q, ua, ub), 10)
    lane = lanes(8)
    corner = lane % 4 == 0

    def halve(q):
        _, m = win.misfit(q, ub)
        parts = (m[0], m[1], src[2, q])
        for c in range(3):
            t = parts[c]
            tmp[c, q] = (t + lroll(t, -1)) + (lroll(t, -2) + lroll(t, -3))

    repeat(1, 9, halve, 8)

    def gather(b):
        for c in range(3):
            packed = jnp.zeros((8, 128), F32)
            for j in range(4):
                q = 4 * b + 1 + j
                t = tmp[c, q, pl.ds(4, 8, 2), :] + tmp[c, q, pl.ds(5, 8, 2), :]
                t = jnp.where(corner, 0.125 * t, 0.0)
                packed = packed + (lroll(t, j) if j else t)
            src2[c, b] = packed

    for b in range(2):
        gather(b)
    for buf in (va, vb):
        for c in range(2):
            buf[c, 0] = jnp.zeros((8, 128), F32)
            buf[c, 3] = jnp.zeros((8, 128), F32)
    win2 = Window(src2, gain2, 0.0625, 1, functools.partial(near2, lane))
    for b in range(2):
        win2.start(b, block_mask(8, lane, ix * 4 - 2 + 4 * b, iy * 4 - 2), va)
    for b in range(2):
        win2.relax(b, va, vb)
    m = [win2.misfit(b, vb)[1] for b in range(2)]

    def third(v0, v1, moves):
        total = jnp.zeros((1, 128), F32)
        for v, slot, move in ((v0, 2, -2), (v1, 0, 2)):
            t = (v + lroll(v, -1)) + (lroll(v, -4) + lroll(v, -5))
            t = 0.125 * jnp.where(lane % 8 == slot, t + sroll(t, -1), 0.0)
            for extra in moves:
                total = total + lroll(t[2:3], move + extra) + lroll(t[4:5], move + extra + 1)
        return total

    field = third(m[0][0], m[1][0], (0,)) + third(m[0][1], m[1][1], (4,))
    wave = third(src2[2, 0], src2[2, 1], (0, 4))
    pair = jnp.concatenate([field, wave] * 4, axis=0)

    def spread(i):
        out[i] = pair

    repeat(0, 64, spread, 8)


def swap(v, real):
    return jnp.where(real, lroll(v, -4), lroll(v, 4))


def up_kernel(
    idx, src0, gain0, ub0, src1, gain1, ub1, src2, shared, out,
    flat, f3, w3, ga3, gb3, ua3, ub3, f4, w4, s4, e3, gain2, u2, wide2, cell1, ua1, ut1, wide1, wide0, ua0, ut0, done, sems,
):
    ix, iy = idx[0], idx[1]
    lane = lanes(16)
    real = lane // 4 % 2 == 0
    sign = jnp.where(real, F32(SHIFT), F32(-SHIFT))
    xlow = lane // 2 % 2 == 0
    ylow = lane % 2 == 0
    zlow = lane // 8 % 2 == 0
    slot = lane % 4
    row = sublanes(16)
    zero16 = jnp.zeros((16, 128), F32)

    def y_pair(v):
        return jnp.where(row >= 1, sroll(v, 1), 0.0), jnp.where(row < 15, sroll(v, -1), 0.0)

    def packed_gain(w, scale):
        gr, gi = inverse(w, scale, 1.0)
        return gr, jnp.where(real, -gi, gi)

    def packed_misfit(f, w, v, nb, scale):
        return f - scale * (6.0 * v - nb) + w * (v + sign * swap(v, real))

    flat[pl.ds(0, 512), :] = shared[...]

    for at in (0, 1, 2, 19, 20, 21):
        for ref in (f3, w3, ga3, gb3):
            ref[at] = zero16
        for ref in (ua3, ub3):
            ref[at] = zero16
    for j in range(5):
        e3[j] = jnp.zeros((32, 128), F32)

    def start3(x):
        at = x + 3
        f3[at] = flat[pl.ds(32 * x, 16, 2), :]
        w = flat[pl.ds(32 * x + 1, 16, 2), :]
        w3[at] = w
        ga, gb = packed_gain(w, 1.0 / 64)
        ga3[at], gb3[at] = ga, gb
        ua3[at] = ga * f3[at] + gb * swap(f3[at], real)

    def miss3(ref, at):
        v = ref[at]
        down, up = y_pair(v)
        xs = jnp.where(xlow, lroll(ref[at - 1] + v, -2), lroll(v + ref[at + 1], 2))
        ys = jnp.where(ylow, lroll(v + down, -1), lroll(v + up, 1))
        return v, packed_misfit(f3[at], w3[at], v, xs + ys + z_sum(v, lane, 8), 1.0 / 64)

    def relaxed3(ref, at):
        v, m = miss3(ref, at)
        return v + ga3[at] * m + gb3[at] * swap(m, real)

    def relax3(at):
        ub3[at] = relaxed3(ua3, at)

    repeat(0, 16, start3, 8)
    repeat(3, 19, relax3, 8)

    first, second = (slot == 0) & zlow, (slot == 0) & ~zlow

    def eighth(v, k):
        v = 0.125 * ((v + lroll(v, -1)) + (lroll(v, -2) + lroll(v, -3)))
        low = jnp.where(first, v, 0.0)
        return (lroll(low, k) if k else low) + lroll(jnp.where(second, v, 0.0), k - 8)

    def halve3(r):
        f, w = zero16, zero16
        for k in range(4):
            at = 4 * k + r + 3
            f = f + eighth(miss3(ub3, at)[1], k)
            w = w + eighth(w3[at], k)
        f4[r], w4[r] = f, w

    repeat(0, 4, halve3, 1)
    fs = [f4[r] for r in range(4)]
    ws = [w4[r] for r in range(4)]
    gs = [packed_gain(w, 1.0 / 256) for w in ws]

    swapped = [swap(f, real) for f in fs]

    def near4(us):
        low = jnp.where(slot >= 1, lroll(us[3], 1), 0.0)
        high = jnp.where(slot < 3, lroll(us[0], -1), 0.0)
        wide = [low, *us, high]
        nbs = []
        for r in range(4):
            down, up = y_pair(us[r])
            nbs.append(wide[r] + wide[r + 2] + down + up + z_sum(us[r], lane, 16))
        return nbs

    def miss4(f, w, v, other, nb, turn):
        return f - (6.0 * v - nb) * (1.0 / 256) + w * (v + turn * other)

    def relax4(_, both):
        us, vs = both
        nus, nvs = near4(us), near4(vs)
        new = []
        for r in range(4):
            m = miss4(fs[r], ws[r], us[r], vs[r], nus[r], sign)
            n = miss4(swapped[r], ws[r], vs[r], us[r], nvs[r], -sign)
            ga, gb = gs[r]
            new.append((us[r] + ga * m + gb * n, vs[r] + ga * n - gb * m))
        return tuple(x for x, _ in new), tuple(x for _, x in new)

    us = tuple(g[0] * f + g[1] * h for g, f, h in zip(gs, fs, swapped))
    vs = tuple(g[0] * h - g[1] * f for g, f, h in zip(gs, fs, swapped))
    us, vs = lax.fori_loop(0, 5, relax4, (us, vs))
    nus = near4(us)
    ms = [miss4(fs[r], ws[r], us[r], vs[r], nus[r], sign) for r in range(4)]
    total_m = ms[0] + ms[1] + ms[2] + ms[3]
    total_w = ws[0] + ws[1] + ws[2] + ws[3]
    sum_r = jnp.sum(jnp.where(zlow & real, total_m, 0.0))
    sum_i = jnp.sum(jnp.where(zlow & ~real, total_m, 0.0))
    sum_w = jnp.sum(jnp.where(zlow & real, total_w, 0.0))
    numer = jnp.where(real, sum_r - SHIFT * sum_i, sum_i + SHIFT * sum_r)
    const = -numer / (jnp.full((16, 128), (1.0 + SHIFT * SHIFT), F32) * sum_w)
    for r in range(4):
        s4[r] = jnp.where(zlow, us[r] + const, 0.0)

    def spread4(j):
        x = ix - 4 + j
        inside = (x >= 0) & (x < 16)
        x = jnp.clip(x, 0, 15)
        k = x // 4
        t = jnp.where((slot == k) & inside, s4[x - 4 * k], 0.0)
        t = [pltpu.roll(t, lax.rem(128 - k + d, 128), 1) for d in range(4)]
        t = (t[0] + t[1]) + (t[2] + t[3])
        above = lroll(jnp.where(lane < 112, t, 0.0), 16)
        below = lroll(jnp.where(lane >= 16, t, 0.0), -8)
        t = 0.75 * (t + lroll(t, 8)) + 0.25 * (above + below)
        down, up = y_pair(t)
        return 0.75 * t + 0.25 * jnp.where(ylow, down, up)

    wide = [spread4(j) for j in range(9)]
    for j in range(7):
        at = ix + j
        fix = 0.75 * wide[j + 1] + 0.25 * jnp.where(xlow, wide[j], wide[j + 2])
        fix = jnp.where((at >= 3) & (at < 19), fix, 0.0)
        ub3[at] = ub3[at] + fix

    def sweep3(_):
        new = [relaxed3(ub3, ix + j) for j in range(1, 6)]
        for j in range(1, 6):
            ub3[ix + j] = new[j - 1]

    repeat(0, 2, sweep3, 2)
    for j in range(1, 6):
        e3[j - 1, pl.ds(8, 16), :] = ub3[ix + j]

    lane8 = lanes(8)
    lane24 = lanes(24)
    zero24 = jnp.zeros((24, 128), F32)
    for c in range(2):
        u2[c, 0] = zero16
        u2[c, 5] = zero16
    win2 = Window(src2, gain2, 0.0625, 1, functools.partial(near2, lane))
    keep2 = [block_mask(16, lane, ix * 4 - 6 + 4 * b, iy * 4 - 6) for b in range(4)]
    for b in range(4):
        win2.start(b, keep2[b], u2)
    a_low = lane8 % 2 == 0
    h_low = lane8 // 2 % 2 == 0

    def widen3(c):
        sides = []
        for yl in range(2):
            pick = (lane8 // 4 % 2 == c) & (lane8 % 2 == yl)
            ups, downs = [], []
            for bb in range(5):
                t = jnp.where(pick, e3[bb, pl.ds(iy + 5, 8), :], 0.0)
                t = t + lroll(t, 1 - 2 * yl)
                above = lroll(jnp.where(lane8 < 120, t, 0.0), 8 - 4 * c)
                below = lroll(jnp.where(lane8 >= 8, t, 0.0), -4 - 4 * c)
                t = 0.75 * (t + lroll(t, 4 - 8 * c)) + 0.25 * (above + below)
                ups.append(lroll(t, 2))
                downs.append(lroll(t, -2))
            cells = [ups[0]]
            cells += [jnp.where(h_low, downs[b], ups[b + 1]) for b in range(4)]
            cells += [downs[4]]
            blocks = []
            for b in range(1, 5):
                low = lroll(jnp.where(a_low, cells[b - 1], cells[b]), -2)
                high = lroll(jnp.where(a_low, cells[b], cells[b + 1]), 2)
                blocks.append(0.75 * cells[b] + 0.25 * jnp.where(h_low, low, high))
            sides.append(blocks)
        for b in range(4):
            t0, t1 = sides[0][b], sides[1][b]
            wide2[c, b, pl.ds(0, 8, 4), :] = 0.75 * t0 + 0.25 * sroll(t1, 1)
            wide2[c, b, pl.ds(1, 8, 4), :] = 0.75 * t0 + 0.25 * t1
            wide2[c, b, pl.ds(2, 8, 4), :] = 0.75 * t1 + 0.25 * t0
            wide2[c, b, pl.ds(3, 8, 4), :] = 0.75 * t1 + 0.25 * sroll(t0, -1)

    for c in range(2):
        widen3(c)

    def sweep2(i):
        add = jnp.where(i == 0, F32(1), F32(0))
        new = [win2.relaxed(b, u2) for b in range(4)]
        for b in range(4):
            for c in range(2):
                fix = wide2[c, b, pl.ds(6, 16), :] * (keep2[b] * add)
                u2[c, b + 1] = new[b][c] + fix

    repeat(0, 3, sweep2, 3)


    def widen2(at, b, xl):
        for c in range(2):
            t = jnp.where(slot == xl, u2[c, b + 1], 0.0)
            t = lroll(t, -xl) if xl else t
            t = t + lroll(t, 1)
            above = lroll(jnp.where(lane < 124, t, 0.0), 4)
            below = lroll(jnp.where(lane >= 4, t, 0.0), -2)
            cell1[c, at] = 0.75 * (t + lroll(t, 2)) + 0.25 * (above + below)

    for at in range(10):
        widen2(at, (at + 3) // 4, (at + 3) % 4)
    lane_even = lane % 2 == 0

    def mix2(q):
        for c in range(2):
            side = jnp.where(lane_even, cell1[c, q - 1], cell1[c, q + 1])
            t = 0.75 * cell1[c, q] + 0.25 * side
            wide1[c, q, pl.ds(0, 16, 2), :] = 0.75 * t + 0.25 * sroll(t, 1)
            wide1[c, q, pl.ds(1, 16, 2), :] = 0.75 * t + 0.25 * sroll(t, -1)

    repeat(1, 9, mix2, 8)
    for c in range(2):
        ua1[c, 1] = zero24
        ua1[c, 10] = zero24
    inside1 = row_mask(24, iy * 8 - 8, 128)

    def correct1(q):
        keep = inside1 * scalar_mask(ix * 4 - 3 + q, 64)
        for c in range(2):
            ua1[c, q + 1] = ub1[c, q + 1] + wide1[c, q, pl.ds(4, 24), :] * keep

    repeat(1, 9, correct1, 4)
    win1 = Window(src1, gain1, 0.25, 1, functools.partial(near1, lane24))

    repeat(1, 9, lambda q: win1.relax(q, ua1, ut1), 8)
    repeat(2, 8, lambda q: win1.relax(q, ut1, ua1), 6)

    def widen1(q):
        for c in range(2):
            t = ua1[c, q + 1, pl.ds(5, 16), :]
            for p in range(2):
                v = jnp.where(lane_even, t, 0.0) if p == 0 else jnp.where(lane_even, 0.0, t)
                above = lroll(jnp.where(lane < 126, v, 0.0), 2 - p)
                below = lroll(jnp.where(lane >= 2, v, 0.0), -1 - p)
                v = 0.75 * (v + lroll(v, 1 - 2 * p)) + 0.25 * (above + below)
                wide0[c, 2 * q + p, pl.ds(0, 16, 2), :] = 0.75 * v + 0.25 * sroll(v, 1)
                wide0[c, 2 * q + p, pl.ds(1, 16, 2), :] = 0.75 * v + 0.25 * sroll(v, -1)

    repeat(2, 8, widen1, 6)
    inside0 = row_mask(24, iy * 16 - 3, 256)

    def correct0(at):
        for c in range(2):
            low = wide0[c, at - 1, pl.ds(3, 24), :]
            mid = wide0[c, at, pl.ds(3, 24), :]
            high = wide0[c, at + 1, pl.ds(3, 24), :]
            for child, side in ((0, low), (1, high)):
                x = 2 * at - 9 + child
                keep = inside0 * scalar_mask(ix * 16 - 3 + x, 256)
                ua0[c, x] = ub0[c, x] + (0.75 * mid + 0.25 * side) * keep

    repeat(5, 15, correct0, 10)
    win0 = Window(src0, gain0, 1.0, 0, functools.partial(near0, lane24))
    repeat(2, 20, lambda x: win0.relax(x, ua0, ut0), 18)

    def finish0(x):
        new = win0.relaxed(x + 3, ut0)
        for c in range(2):
            ua0[c, x + 3] = new[c]
            done[c, x] = ua0[c, x + 3, pl.ds(3, 16), :]

    copies = []
    for half in range(2):
        repeat(8 * half, 8 * half + 8, finish0, 8)
        rows = pl.ds(8 * half, 8)
        copy = pltpu.make_async_copy(done.at[:, rows], out.at[:, rows], sems.at[half])
        copy.start()
        copies.append(copy)
    for copy in copies:
        copy.wait()


def call(kernel, name, out_shape, scratch, *args, micros=2, sems=0):
    vmem = pl.BlockSpec(memory_space=pltpu.VMEM)
    return pl.pallas_call(
        kernel,
        name=name,
        out_shape=[jax.ShapeDtypeStruct(shape, F32) for shape in out_shape],
        in_specs=[pl.BlockSpec(memory_space=pltpu.SMEM)] + [vmem] * (len(args) - 1),
        out_specs=[pl.BlockSpec(memory_space=pl.ANY) if sems else vmem] * len(out_shape),
        scratch_shapes=[pltpu.VMEM(shape, F32) for shape in scratch]
        + ([pltpu.SemaphoreType.DMA((sems,))] if sems else []),
        cost_estimate=pl.CostEstimate(
            flops=0, bytes_accessed=micros * 3_500_000, transcendentals=0
        ),
        compiler_params=pltpu.CompilerParams(vmem_limit_bytes=40 * 1024 * 1024),
    )(*args)


BOTH = ("gx", "gy")


def partners(axis, first):
    counts = [lax.axis_size(name) for name in BOTH]
    along = BOTH.index(axis)
    pairs = []
    for i in range(counts[0]):
        for j in range(counts[1]):
            place = [i, j]
            other = ((place[along] + first) ^ 1) - first
            if 0 <= other < counts[along]:
                place[along] = other
            else:
                place[1 - along] ^= 1
            pairs.append((i * counts[1] + j, place[0] * counts[1] + place[1]))
    return pairs


def trade(to_low, to_high, axis, near=None):
    even = lax.axis_index(axis) % 2 == 0
    if to_low is to_high:
        one = two = to_low
    else:
        low, high = near or (to_low, to_high)
        one = jnp.where(even, high, low)
        two = jnp.where(even, to_low, to_high)
    two = lax.ppermute(two, BOTH, partners(axis, 1))
    one = lax.ppermute(one, BOTH, partners(axis, 0))
    one, two = lax.optimization_barrier((one, two))
    return jnp.where(even, two, one), jnp.where(even, one, two)


def body(residual_in, wave_sq):
    ix = lax.axis_index("gx")
    iy = lax.axis_index("gy")
    idx = jnp.stack([ix, iy]).astype(jnp.int32)

    own = jnp.concatenate([residual_in, wave_sq[None]], axis=0)
    near_f, near_w = lax.optimization_barrier((residual_in, wave_sq))
    near = jnp.concatenate([near_f, near_w[None]], axis=0)
    low, high = trade(own[:, :3], own[:, 13:], "gx", (near[:, :3], near[:, 13:]))
    strip = jnp.concatenate([low, own, high], axis=1)
    low, high = trade(
        strip[:, :, :3].transpose(0, 2, 1, 3).reshape(9, 22, 128),
        strip[:, :, 13:].transpose(0, 2, 1, 3).reshape(9, 22, 128),
        "gy",
    )
    low = low.reshape(3, 3, 22, 128).transpose(0, 2, 1, 3)
    high = high.reshape(3, 3, 22, 128).transpose(0, 2, 1, 3)
    src0 = jnp.concatenate([low, strip, high, jnp.zeros((3, 22, 2, 128), F32)], axis=2)

    n0 = (2, 22, 24, 128)
    n1 = (2, 12, 24, 128)
    own1, gain0, first0 = call(
        down0_kernel, "down0", [(3, 4, 8, 128), n0, n0], [n0, (3, 8, 24, 128)], idx, src0
    )
    low, high = trade(own1[:, :3], own1[:, 1:], "gx")
    strip = jnp.concatenate([low, own1, high], axis=1)
    low, high = trade(strip, strip, "gy")
    src1 = jnp.concatenate([low, strip, high], axis=2)

    part, own2, gain1, first1 = call(
        down1_kernel,
        "down1",
        [(64, 8, 128), (3, 2, 8, 128), (2, 10, 24, 128), n1],
        [n1, (3, 10, 24, 128), (2, 2, 8, 128), (2, 4, 8, 128), (2, 4, 8, 128)],
        idx,
        src1,
    )
    part = part.reshape(256, 2, 128)
    flat = lax.all_to_all(part, ("gx", "gy"), 0, 0).reshape(512, 128)
    low, high = trade(own2[:, 1:], own2[:, :1], "gx")
    strip = jnp.concatenate([low, own2, high], axis=1)
    low, high = trade(strip[:, :, 4:], strip[:, :, :4], "gy")
    src2 = jnp.concatenate([low, strip, high], axis=2)

    wide = (22, 16, 128)
    return call(
        up_kernel,
        "up",
        [(2, 16, 16, 128)],
        [(520, 128), wide, wide, wide, wide, wide, wide]
        + [(4, 16, 128), (4, 16, 128), (4, 16, 128), (5, 32, 128)]
        + [(2, 4, 16, 128), (2, 6, 16, 128), (2, 4, 40, 128)]
        + [(2, 10, 16, 128), n1, n1, (2, 10, 40, 128), (2, 16, 40, 128), n0, n0, (2, 16, 16, 128)],
        idx,
        src0,
        gain0,
        first0,
        src1,
        gain1,
        first1,
        src2,
        flat,
        micros=10,
        sems=2,
    )[0]


def solution(mesh):
    placed = (P(None, "gx", "gy", None), P("gx", "gy", None))
    return jax.shard_map(
        body, mesh=mesh, in_specs=placed, out_specs=P(None, "gx", "gy", None), check_vma=False
    )
```
